32 devices in a mesh: head: 4 (over z), batch: 8 (over y, x, core).
Axes of the slice: x: 2, y: 2, z: 4, core: 2. Of those that a mesh axis runs over, the one named last changes fastest.
Arguments:
- layer_input: bfloat16 [8192, 1024], P(('batch', 'head')), may hold values from -6 to 6
- cotangent: bfloat16 [8192, 1024], P(('batch', 'head')), may hold values from -6 to 6
- segments: int32 [8192], P('batch'), may hold values from 0 to 126, as said below
- mix_gain: float32 [1024], replicated, may hold values from 0.5 to 1.5
- query_weight: bfloat16 [1024, 1024], P('batch', 'head'), may hold values from -0.1875 to 0.1875
- key_weight: bfloat16 [1024, 2048], P('batch', 'head'), may hold values from -0.1875 to 0.1875
- value_weight: bfloat16 [1024, 2048], P('batch', 'head'), may hold values from -0.1875 to 0.1875
- outgate_weight: bfloat16 [1024, 1024], P('batch', 'head'), may hold values from -0.1875 to 0.1875
- rate_weight: bfloat16 [1024, 24], P('batch', 'head'), may hold values from -0.1875 to 0.1875
- conv_query: float32 [4, 1024], replicated, may hold values from -3 to 3
- conv_key: float32 [4, 2048], replicated, may hold values from -3 to 3
- conv_value: float32 [4, 2048], replicated, may hold values from -3 to 3
- decay_bias: float32 [8], replicated, may hold values from -4 to 1
- out_gain: float32 [128], replicated, may hold values from 0.5 to 1.5
- out_weight: bfloat16 [1024, 1024], P('head', 'batch'), may hold values from -0.1875 to 0.1875
- mlp_gain: float32 [1024], replicated, may hold values from 0.5 to 1.5
- gate_weight: bfloat16 [1024, 2816], P('batch', 'head'), may hold values from -0.1875 to 0.1875
- up_weight: bfloat16 [1024, 2816], P('batch', 'head'), may hold values from -0.1875 to 0.1875
- down_weight: bfloat16 [2816, 1024], P('head', 'batch'), may hold values from -0.109375 to 0.109375
Outputs:
- layer_output: bfloat16 [8192, 1024], P(('batch', 'head'))
- input_grad: float32 [8192, 1024], P(('batch', 'head'))
- mix_gain_grad: float32 [1024], replicated
- query_weight_grad: float32 [1024, 1024], P('batch', 'head')
- key_weight_grad: float32 [1024, 2048], P('batch', 'head')
- value_weight_grad: float32 [1024, 2048], P('batch', 'head')
- outgate_weight_grad: float32 [1024, 1024], P('batch', 'head')
- rate_weight_grad: float32 [1024, 24], P('batch', 'head')
- conv_query_grad: float32 [4, 1024], replicated
- conv_key_grad: float32 [4, 2048], replicated
- conv_value_grad: float32 [4, 2048], replicated
- decay_bias_grad: float32 [8], replicated
- out_gain_grad: float32 [128], replicated
- out_weight_grad: float32 [1024, 1024], P('head', 'batch')
- mlp_gain_grad: float32 [1024], replicated
- gate_weight_grad: float32 [1024, 2816], P('batch', 'head')
- up_weight_grad: float32 [1024, 2816], P('batch', 'head')
- down_weight_grad: float32 [2816, 1024], P('head', 'batch')
The draws below stay inside these ranges and needn't reach their ends.
Inputs may be any that keep to these rules, and one draw needn't show every extreme that they name: `segments`: segment ids count documents within each packed row of 1024 tokens: they are 0 at the row's first token and rise by one at each document's first token; documents begin only before position max(64, 1) or after position 1024 - max(64, 1), so in every row one document covers the positions between; in some row every one of those edge positions begins a document.
All inputs are finite; a program needn't handle non-finite values.
Results may differ from the reference program's by a relative error of at most 0.013.
The reference program's roundings to bfloat16 on the way count: a program that leaves them out, or rounds other values in their place, can miss the bound.
Values may be sent and summed in bfloat16 or wider, within the bound.
No kernel may reach another device: no remote copies, remote signals or barrier semaphores. Data moves between devices by JAX's collectives and lax.ppermute only.
A program may use at most 320 MiB of HBM per device.

```python
import math
import jax
import jax.numpy as jnp
from jax import lax

D = 1024
HEADS = 8
HEAD_DIM = 128
FF = 2816
KERNEL = 4
ROW_TOK = 1024
TOKENS = 8192


def draw_segments(key, part):
    row_count = TOKENS // ROW_TOK
    margin = max(ROW_TOK // 16, 1)
    flag_bits = jax.random.randint(key, (row_count, ROW_TOK), 0, 24) == 0
    positions = jnp.arange(ROW_TOK)
    interior = (positions >= margin) & (positions <= ROW_TOK - margin)
    full_row = jax.random.randint(jax.random.fold_in(key, 7), (), 0, row_count)
    rows = jnp.arange(row_count)
    flag_bits = jnp.where((rows == full_row)[:, None], True, flag_bits)
    flag_bits = jnp.where(interior[None, :], False, flag_bits)
    flag_bits = jnp.where(positions[None, :] == 0, True, flag_bits)
    doc_ids = jnp.cumsum(flag_bits.astype(jnp.int32), axis=1) - 1
    return doc_ids.reshape(TOKENS).astype(jnp.int32)


def steps_of(own_key, extent, cuts, low, high):
    gain, own = 1.0, jax.random.fold_in(own_key, 6)
    for dim, shards_of in cuts:
        steps = jnp.exp(jax.random.uniform(jax.random.fold_in(own, dim), (shards_of,), jnp.float32, low / len(cuts), high / len(cuts)))
        gain = gain * jnp.repeat(steps, extent[dim] // shards_of).reshape([-1 if axis == dim else 1 for axis in range(len(extent))])
    return gain


def normal_values(rng, shape, scale, most, shards=(), held_as=jnp.bfloat16):
    result = jax.random.normal(rng, shape, jnp.float32) * scale
    if len(shards) > 0:
        result = steps_of(rng, shape, shards, -0.22, 0.18) * result
    return jnp.clip(result, min=-most, max=most).astype(held_as)


def setup_inputs(seed: int = 0) -> dict:
    splits = jax.random.split(jax.random.key(seed), 20)
    return {
        "layer_input": normal_values(splits[0], (TOKENS, D), 1.0, 6.0, ((0, 32),)),
        "cotangent": normal_values(splits[1], (TOKENS, D), 1.0, 6.0, ((0, 32),)),
        "segments": draw_segments(jax.random.fold_in(splits[19], 71), 0),
        "mix_gain": jnp.clip(1.0 + 0.1 * jax.random.normal(splits[3], (D,), jnp.float32), 0.5, 1.5),
        "query_weight": normal_values(splits[4], (D, HEADS * HEAD_DIM), D ** -0.5, 0.1875, ((0, 8), (1, 4))),
        "key_weight": normal_values(splits[5], (D, HEADS * 2 * HEAD_DIM), D ** -0.5, 0.1875, ((0, 8), (1, 4))),
        "value_weight": normal_values(splits[6], (D, HEADS * 2 * HEAD_DIM), D ** -0.5, 0.1875, ((0, 8), (1, 4))),
        "outgate_weight": normal_values(splits[7], (D, HEADS * HEAD_DIM), D ** -0.5, 0.1875, ((0, 8), (1, 4))),
        "rate_weight": normal_values(splits[8], (D, HEADS * 3), D ** -0.5, 0.1875, ((0, 8), (1, 4))),
        "conv_query": normal_values(splits[9], (KERNEL, HEADS * HEAD_DIM), 0.5, 3.0, (), jnp.float32),
        "conv_key": normal_values(splits[10], (KERNEL, HEADS * 2 * HEAD_DIM), 0.5, 3.0, (), jnp.float32),
        "conv_value": normal_values(splits[11], (KERNEL, HEADS * 2 * HEAD_DIM), 0.5, 3.0, (), jnp.float32),
        "decay_bias": jnp.clip(jax.random.uniform(splits[12], (HEADS,), jnp.float32, -4.0, 1.0), -4.0, 1.0),
        "out_gain": jnp.clip(1.0 + 0.1 * jax.random.normal(splits[13], (HEAD_DIM,), jnp.float32), 0.5, 1.5),
        "out_weight": normal_values(splits[14], (HEADS * HEAD_DIM, D), (HEADS * HEAD_DIM) ** -0.5, 0.1875, ((0, 4), (1, 8))),
        "mlp_gain": jnp.clip(1.0 + 0.1 * jax.random.normal(splits[15], (D,), jnp.float32), 0.5, 1.5),
        "gate_weight": normal_values(splits[16], (D, FF), D ** -0.5, 0.1875, ((0, 8), (1, 4))),
        "up_weight": normal_values(splits[17], (D, FF), D ** -0.5, 0.1875, ((0, 8), (1, 4))),
        "down_weight": normal_values(splits[18], (FF, D), FF ** -0.5, 0.109375, ((0, 4), (1, 8))),
    }


EPS = 1e-06
EXACT_PRECISION = lax.Precision.HIGHEST

@jax.custom_vjp
def low(v):
    return lax.optimization_barrier(v.astype(jnp.bfloat16)).astype(jnp.float32)

@jax.custom_vjp
def low_back(v):
    return v

def low_keep(v):
    return (low(v), None)

def low_pass(kept, grad):
    return (grad,)

def back_keep(v):
    return (v, None)

def back_low(kept, grad):
    return (low(grad),)
low.defvjp(low_keep, low_pass)
low_back.defvjp(back_keep, back_low)

def matmul(left, right):
    return jnp.dot(left, right, precision=EXACT_PRECISION)

def row_scale(values):
    return lax.rsqrt(lax.optimization_barrier(jnp.mean(values * values, axis=-1, keepdims=True)) + EPS)

def unit_norm(values):
    return values * lax.rsqrt(lax.optimization_barrier(jnp.sum(values * values, axis=-1, keepdims=True)) + EPS)

def short_conv(raw_cols, taps, segments):
    length = raw_cols.shape[0]
    total = raw_cols * taps[0]
    for offset in range(1, taps.shape[0]):
        shifted = jnp.pad(raw_cols, ((offset, 0), (0, 0)))[:length]
        earlier = jnp.pad(segments, (offset, 0), constant_values=-1)[:length]
        total = total + jnp.where((earlier == segments)[:, None], shifted, 0.0) * taps[offset]
    return total

def token_update(memory_state, item):
    query_rows, key_pair, value_pair, beta_pair, keep_rate = item
    memory_state = memory_state * keep_rate[:, None, None]
    for house in range(2):
        current_key = key_pair[:, house]
        value_now = value_pair[:, house]
        recalled_values = jnp.einsum('aq,aqc->ac', current_key, memory_state, precision=EXACT_PRECISION)
        memory_state = memory_state + beta_pair[:, house, None, None] * current_key[:, :, None] * (value_now - recalled_values)[:, None, :]
    return (memory_state, jnp.einsum('aq,aqc->ac', query_rows, memory_state, precision=EXACT_PRECISION))

def block_update(memory_state, items):
    return lax.scan(token_update, memory_state, items)

def recurrence(query_rows, keys, values, betas, keep):
    length = query_rows.shape[0]
    block_len = math.gcd(length, 64)
    items = tuple((array.reshape((length // block_len, block_len) + array.shape[1:]) for array in (query_rows, keys, values, betas, keep)))
    memory_state = jnp.zeros((HEADS, HEAD_DIM, HEAD_DIM), jnp.float32)
    final_memory, recalls = lax.scan(jax.checkpoint(block_update), memory_state, items)
    return recalls.reshape(length, HEADS, HEAD_DIM)

def row_forward(row_input, row_segments, params):
    mix_gain, query_weight, key_weight, value_weight, outgate_weight, rate_weight, conv_query, conv_key, conv_value, decay_bias, out_gain, out_weight, mlp_gain, gate_weight, up_weight, down_weight = params
    length = row_input.shape[0]
    normed_in = low(row_input * row_scale(row_input) * mix_gain)
    query_raw = low_back(matmul(normed_in, query_weight))
    key_raw = low_back(matmul(normed_in, key_weight))
    value_raw = low_back(matmul(normed_in, value_weight))
    outgate_raw = low_back(matmul(normed_in, outgate_weight))
    rate_raw = low_back(matmul(normed_in, rate_weight))
    query_rows = unit_norm(jax.nn.silu(short_conv(query_raw, conv_query, row_segments)).reshape(length, HEADS, HEAD_DIM))
    keys = unit_norm(jax.nn.silu(short_conv(key_raw, conv_key, row_segments)).reshape(length, HEADS, 2, HEAD_DIM))
    values = jax.nn.silu(short_conv(value_raw, conv_value, row_segments)).reshape(length, HEADS, 2, HEAD_DIM)
    rates = rate_raw.reshape(length, HEADS, 3)
    betas = jax.nn.sigmoid(rates[:, :, 0:2])
    earlier = jnp.concatenate([jnp.full((1,), -1, jnp.int32), row_segments[:-1].astype(jnp.int32)])
    carry_on = (earlier == row_segments.astype(jnp.int32)).astype(jnp.float32)
    keep = jnp.exp(-jax.nn.softplus(rates[:, :, 2] + decay_bias)) * carry_on[:, None]
    recalls = recurrence(query_rows, keys, values, betas, keep)
    gated = recalls * row_scale(recalls) * out_gain * jax.nn.silu(outgate_raw.reshape(length, HEADS, HEAD_DIM))
    mixed = low(gated.reshape(length, HEADS * HEAD_DIM))
    resid_mid = row_input + low_back(matmul(mixed, out_weight))
    normed_mid = low(resid_mid * row_scale(resid_mid) * mlp_gain)
    gate_pre = low_back(matmul(normed_mid, gate_weight))
    up_pre = low_back(matmul(normed_mid, up_weight))
    hidden = low(jax.nn.silu(gate_pre) * up_pre)
    return resid_mid + matmul(hidden, down_weight)

def reference(layer_input, cotangent, segments, mix_gain, query_weight, key_weight, value_weight, outgate_weight, rate_weight, conv_query, conv_key, conv_value, decay_bias, out_gain, out_weight, mlp_gain, gate_weight, up_weight, down_weight):
    row_count = TOKENS // ROW_TOK
    params = tuple((array.astype(jnp.float32) for array in (mix_gain, query_weight, key_weight, value_weight, outgate_weight, rate_weight, conv_query, conv_key, conv_value, decay_bias, out_gain, out_weight, mlp_gain, gate_weight, up_weight, down_weight)))
    row_segments_all = segments.astype(jnp.int32).reshape(row_count, ROW_TOK)

    def forward(inputs, *weights):

        def one_row(item):
            return row_forward(item[0], item[1], weights)
        outputs = lax.map(jax.checkpoint(one_row), (inputs.reshape(row_count, ROW_TOK, D), row_segments_all))
        return outputs.reshape(TOKENS, D)
    output, pullback = jax.vjp(forward, layer_input.astype(jnp.float32), *params)
    grads = pullback(cotangent.astype(jnp.float32))
    return (output.astype(jnp.bfloat16), grads[0], grads[1], grads[2], grads[3], grads[4], grads[5], grads[6], grads[7], grads[8], grads[9], grads[10], grads[11], grads[12], grads[13], grads[14], grads[15], grads[16])
```

```python
from functools import partial

import jax
import jax.numpy as jnp
from jax import lax
from jax.experimental import pallas as pl
from jax.experimental.pallas import tpu as pltpu
from jax.sharding import PartitionSpec as P

HEAD_DIM = 128
EPS = 1e-06
EXACT = lax.Precision.HIGHEST
HIGH = lax.Precision.HIGH
FAST = lax.Precision.DEFAULT
NN = ((1,), (0,))
NT = ((1,), (1,))
TN = ((0,), (0,))
CHUNK = 64
ROWS = 2 * CHUNK


def mm(left, right, dims=NN, precision=HIGH):
    return lax.dot_general(
        left, right, (dims, ((), ())), precision=precision, preferred_element_type=jnp.float32
    )


def softplus(x):
    return jnp.maximum(x, 0.0) + jnp.log1p(jnp.exp(-jnp.abs(x)))


def chunk_masks():
    row = lax.broadcasted_iota(jnp.int32, (ROWS, ROWS), 0)
    col = lax.broadcasted_iota(jnp.int32, (ROWS, ROWS), 1)
    row_tok, col_tok = row & (CHUNK - 1), col & (CHUNK - 1)
    later = row_tok > col_tok
    same_tok = row_tok == col_tok
    pair = same_tok & (row > col)
    levels = []
    size = 1
    while size < CHUNK:
        upper = (row_tok & size) > (col_tok & size)
        together = (row_tok & (-2 * size)) == (col_tok & (-2 * size))
        levels.append(upper & together)
        size *= 2
    return row, col, later | same_tok, later | pair, pair, levels


def invert(lower, ident, pair, levels, precision):
    inverse = ident - jnp.where(pair, lower, 0.0)
    for level in levels:
        step = mm(jnp.where(level, lower, 0.0), inverse, NN, precision)
        inverse = inverse - mm(inverse, step, NN, precision)
    return inverse


def col_sum(x):
    return jnp.sum(x, axis=-1, keepdims=True)


def fwd_kernel(
    heads, per_step, raw_ref, aux_ref, segrow_ref, taps_ref, bias_ref, gain_ref,
    mixed_ref, pre_ref, recall_ref, inv_ref, prox_ref, state_ref, mem_ref, tail_ref, act_ref,
):
    width = HEAD_DIM
    block = per_step * CHUNK
    conv_cols = 5 * heads * width

    @pl.when(pl.program_id(0) == 0)
    def _():
        mem_ref[...] = jnp.zeros_like(mem_ref)
        tail_ref[...] = jnp.zeros_like(tail_ref)

    masks = [aux_ref[:, 2 + s : 3 + s] for s in range(3)]
    for tile in range(5 * heads):
        cols = slice(tile * width, (tile + 1) * width)
        raw = raw_ref[:, cols]
        joined = jnp.concatenate([tail_ref[:, cols], raw], axis=0)
        pre = raw * taps_ref[0:1, cols]
        for s in range(1, 4):
            shifted = pltpu.roll(joined, s, 0)[8:]
            pre = pre + shifted * masks[s - 1] * taps_ref[s : s + 1, cols]
        pre_ref[:, cols] = pre
        tail_ref[:, cols] = raw[block - 8 :]
        act = pre * jax.nn.sigmoid(pre)
        if tile < 3 * heads:
            act = act * lax.rsqrt(col_sum(act * act) + EPS)
        act_ref[:, cols] = act

    row, col, lower_eq, strict, pair, levels = chunk_masks()
    ident = (row == col).astype(jnp.float32)
    tri = (
        lax.broadcasted_iota(jnp.int32, (CHUNK, CHUNK), 0)
        >= lax.broadcasted_iota(jnp.int32, (CHUNK, CHUNK), 1)
    ).astype(jnp.float32)
    rates = raw_ref[:, 6 * heads * width :]
    beta_tile = jax.nn.sigmoid(rates)
    log_tile = -softplus(rates + bias_ref[...])
    units = []
    for part in range(per_step):
        rows = slice(part * CHUNK, (part + 1) * CHUNK)
        cumul = mm(tri, log_tile[rows], NN, EXACT)
        cumul_t = jnp.concatenate([cumul, cumul], axis=0).T
        aux = aux_ref[rows]
        aux2 = jnp.concatenate([aux, aux], axis=0)
        same = (aux2[:, 8:9] == segrow_ref[part]) & lower_eq
        end = cumul[CHUNK - 1 :]
        for head in range(heads):
            key1 = act_ref[rows, (heads + 2 * head) * width : (heads + 2 * head + 1) * width]
            key2 = act_ref[rows, (heads + 2 * head + 1) * width : (heads + 2 * head + 2) * width]
            val1 = act_ref[rows, (3 * heads + 2 * head) * width : (3 * heads + 2 * head + 1) * width]
            val2 = act_ref[rows, (3 * heads + 2 * head + 1) * width : (3 * heads + 2 * head + 2) * width]
            query = act_ref[rows, head * width : (head + 1) * width]
            keys = jnp.concatenate([key1, key2], axis=0)
            lane = 3 * head
            c_tok = cumul[:, lane + 2 : lane + 3]
            c_end = end[:, lane + 2 : lane + 3]
            c_col = jnp.concatenate([c_tok, c_tok], axis=0)
            c_row = cumul_t[lane + 2 : lane + 3, :]
            decay = jnp.where(same, jnp.exp(jnp.minimum(c_col - c_row, 0.0)), 0.0)
            beta1 = beta_tile[rows, lane : lane + 1]
            beta2 = beta_tile[rows, lane + 1 : lane + 2]
            beta = jnp.concatenate([beta1, beta2], axis=0)
            start = aux[:, 0:1] * jnp.exp(c_tok)
            start2 = jnp.concatenate([start, start], axis=0)
            final = aux[:, 1:2] * jnp.exp(c_end - c_tok)
            final2 = jnp.concatenate([final, final], axis=0)
            total = aux[CHUNK - 1 :, 0:1] * jnp.exp(c_end)
            dots = mm(jnp.concatenate([keys, query], axis=0), keys, NT)
            lower = jnp.where(strict, beta * decay * dots[:ROWS], 0.0)
            scores = decay[CHUNK:] * dots[ROWS:]
            inverse = invert(lower, ident, pair, levels, HIGH)
            inv_ref[part * heads + head] = inverse
            values = jnp.concatenate([val1, val2], axis=0)
            solved = mm(
                inverse, jnp.concatenate([beta * values, beta * start2 * keys], axis=1)
            )
            probe = jnp.concatenate([solved[:, width:], start * query], axis=0)
            units.append(
                (part, head, rows, probe, solved[:, :width], scores, total, final2 * keys)
            )
    for part, head, rows, probe, base, scores, total, final_keys in units:
        memory = mem_ref[head]
        state_ref[part * heads + head] = memory
        seen = mm(probe, memory)
        proxy = base - seen[:ROWS]
        prox_ref[part * heads + head] = proxy
        mem_ref[head] = total * memory + mm(final_keys, proxy, TN)
        recall = seen[ROWS:] + mm(scores, proxy)
        cols = slice(head * width, (head + 1) * width)
        recall_ref[rows, cols] = recall
        scale = lax.rsqrt(jnp.mean(recall * recall, axis=-1, keepdims=True) + EPS)
        gate = raw_ref[rows, (5 * heads + head) * width : (5 * heads + head + 1) * width]
        mixed = recall * scale * gain_ref[...] * (gate * jax.nn.sigmoid(gate))
        mixed_ref[rows, cols] = mixed.astype(jnp.bfloat16)


def bwd_kernel(
    heads, per_step, grad_ref, raw_ref, aux_ref, segrow_ref, pre_ref, recall_ref, inv_ref,
    prox_ref, state_ref, taps_ref, bias_ref, gain_ref,
    low_ref, taps_grad_ref, bias_grad_ref, gain_grad_ref, adj_ref, head_ref, act_ref, norm_ref, dact_ref,
):
    width = HEAD_DIM
    block = per_step * CHUNK

    @pl.when(pl.program_id(0) == 0)
    def _():
        adj_ref[...] = jnp.zeros_like(adj_ref)
        head_ref[...] = jnp.zeros_like(head_ref)
        taps_grad_ref[...] = jnp.zeros_like(taps_grad_ref)
        bias_grad_ref[...] = jnp.zeros_like(bias_grad_ref)
        gain_grad_ref[...] = jnp.zeros_like(gain_grad_ref)

    for tile in range(5 * heads):
        cols = slice(tile * width, (tile + 1) * width)
        pre = pre_ref[:, cols]
        act = pre * jax.nn.sigmoid(pre)
        if tile < 3 * heads:
            scale = lax.rsqrt(col_sum(act * act) + EPS)
            norm_ref[:, cols] = jnp.broadcast_to(scale, act.shape)
            act = act * scale
        act_ref[:, cols] = act

    row, col, lower_eq, strict, pair, levels = chunk_masks()
    tri_t = (
        lax.broadcasted_iota(jnp.int32, (CHUNK, CHUNK), 0)
        <= lax.broadcasted_iota(jnp.int32, (CHUNK, CHUNK), 1)
    ).astype(jnp.float32)
    tri = (
        lax.broadcasted_iota(jnp.int32, (CHUNK, CHUNK), 0)
        >= lax.broadcasted_iota(jnp.int32, (CHUNK, CHUNK), 1)
    ).astype(jnp.float32)
    lanes = lax.broadcasted_iota(jnp.int32, (CHUNK, width), 1)
    rates = raw_ref[:, 6 * heads * width :]
    beta_tile = jax.nn.sigmoid(rates)
    keep_in = rates + bias_ref[...]
    log_tile = -softplus(keep_in)
    gain_total = jnp.zeros((1, width), jnp.float32)
    bias_total = jnp.zeros((1, width), jnp.float32)
    for part in reversed(range(per_step)):
        rows = slice(part * CHUNK, (part + 1) * CHUNK)
        cumul = mm(tri, log_tile[rows], NN, EXACT)
        cumul_t = jnp.concatenate([cumul, cumul], axis=0).T
        aux = aux_ref[rows]
        aux2 = jnp.concatenate([aux, aux], axis=0)
        same = (aux2[:, 8:9] == segrow_ref[part]) & lower_eq
        end = cumul[CHUNK - 1 :]
        beta_grad = jnp.zeros((CHUNK, width), jnp.float32)
        cumul_grad = jnp.zeros((CHUNK, width), jnp.float32)
        end_grad = jnp.zeros((CHUNK, width), jnp.float32)
        for head in range(heads):
            spot = part * heads + head
            k1 = slice((heads + 2 * head) * width, (heads + 2 * head + 1) * width)
            k2 = slice((heads + 2 * head + 1) * width, (heads + 2 * head + 2) * width)
            v1 = slice((3 * heads + 2 * head) * width, (3 * heads + 2 * head + 1) * width)
            v2 = slice((3 * heads + 2 * head + 1) * width, (3 * heads + 2 * head + 2) * width)
            q0 = slice(head * width, (head + 1) * width)
            g0 = slice((5 * heads + head) * width, (5 * heads + head + 1) * width)
            keys = jnp.concatenate([act_ref[rows, k1], act_ref[rows, k2]], axis=0)
            values = jnp.concatenate([act_ref[rows, v1], act_ref[rows, v2]], axis=0)
            query = act_ref[rows, q0]
            recall = recall_ref[rows, q0]
            grad = grad_ref[rows, q0]
            gate = raw_ref[rows, g0]
            gate_sig = jax.nn.sigmoid(gate)
            silu_gate = gate * gate_sig
            scale = lax.rsqrt(jnp.mean(recall * recall, axis=-1, keepdims=True) + EPS)
            normed = recall * scale
            gain_total = gain_total + jnp.sum(grad * normed * silu_gate, axis=0, keepdims=True)
            weighted = grad * gain_ref[...]
            low_ref[rows, g0] = (
                weighted * normed * gate_sig * (1.0 + gate * (1.0 - gate_sig))
            ).astype(jnp.bfloat16)
            normed_grad = weighted * silu_gate
            out_grad = scale * (
                normed_grad - normed * jnp.mean(normed_grad * normed, axis=-1, keepdims=True)
            )
            lane = 3 * head
            c_tok = cumul[:, lane + 2 : lane + 3]
            c_end = end[:, lane + 2 : lane + 3]
            c_col = jnp.concatenate([c_tok, c_tok], axis=0)
            c_row = cumul_t[lane + 2 : lane + 3, :]
            decay = jnp.where(same, jnp.exp(jnp.minimum(c_col - c_row, 0.0)), 0.0)
            beta = jnp.concatenate(
                [beta_tile[rows, lane : lane + 1], beta_tile[rows, lane + 1 : lane + 2]], axis=0
            )
            start = aux[:, 0:1] * jnp.exp(c_tok)
            start2 = jnp.concatenate([start, start], axis=0)
            final = aux[:, 1:2] * jnp.exp(c_end - c_tok)
            final2 = jnp.concatenate([final, final], axis=0)
            total = aux[CHUNK - 1 :, 0:1] * jnp.exp(c_end)
            dots = mm(jnp.concatenate([keys, query], axis=0), keys, NT)
            key_decay = jnp.where(strict, decay * dots[:ROWS], 0.0)
            scores = decay[CHUNK:] * dots[ROWS:]
            adjoint = adj_ref[head]
            memory = state_ref[spot]
            proxy = prox_ref[spot]
            proxy_grad = mm(scores, out_grad, TN) + mm(final2 * keys, adjoint)
            right_grad = mm(inv_ref[spot], proxy_grad, TN)
            both_grad = jnp.concatenate([right_grad, out_grad], axis=0)
            beta_start = beta * start2
            adj_ref[head] = total * adjoint + mm(
                jnp.concatenate([-beta_start * keys, start * query], axis=0), both_grad, TN
            )
            outer = mm(both_grad, proxy, NT)
            through = mm(both_grad, memory, NT)
            final_part = final2 * mm(proxy, adjoint, NT)
            lower_grad = -outer[:ROWS]
            beta_part = lower_grad * key_decay
            dots_grad = jnp.where(strict, lower_grad * beta * decay, 0.0)
            score_grad = outer[ROWS:] * decay[CHUNK:]
            log_part = beta_part * beta
            log_part = jnp.concatenate(
                [log_part[:CHUNK], log_part[CHUNK:] + outer[ROWS:] * scores], axis=0
            )
            inner = mm(
                jnp.concatenate([dots_grad + dots_grad.T, score_grad], axis=0), keys
            )
            key_through = col_sum(keys * through[:ROWS])
            query_through = start * col_sum(query * through[ROWS:])
            final_sum = col_sum(keys * final_part)
            key_grad = (
                inner[:ROWS]
                + mm(score_grad, query, TN)
                - beta_start * through[:ROWS]
                + final_part
            )
            query_grad = inner[ROWS:] + start * through[ROWS:]
            value_grad = beta * right_grad
            beta_col = (
                col_sum(right_grad * values) - start2 * key_through + col_sum(beta_part)
            )
            c_grad = col_sum(log_part - log_part.T) - beta_start * key_through - final_sum
            c_grad = c_grad[:CHUNK] + c_grad[CHUNK:] + query_through
            end_part = jnp.sum(final_sum, axis=0, keepdims=True) + total * jnp.sum(
                col_sum(memory * adjoint), axis=0, keepdims=True
            )
            beta_grad = jnp.where(lanes == lane, beta_col[:CHUNK], beta_grad)
            beta_grad = jnp.where(lanes == lane + 1, beta_col[CHUNK:], beta_grad)
            cumul_grad = jnp.where(lanes == lane + 2, c_grad, cumul_grad)
            end_grad = jnp.where(lanes == lane + 2, end_part, end_grad)
            dact_ref[rows, k1] = key_grad[:CHUNK]
            dact_ref[rows, k2] = key_grad[CHUNK:]
            dact_ref[rows, v1] = value_grad[:CHUNK]
            dact_ref[rows, v2] = value_grad[CHUNK:]
            dact_ref[rows, q0] = query_grad
        log_grad = mm(tri_t, cumul_grad, NN, EXACT) + end_grad
        keep_sig = jax.nn.sigmoid(keep_in[rows])
        beta_rows = beta_tile[rows]
        keep_grad = -log_grad * keep_sig * aux[:, 2:3]
        rate_grad = beta_grad * beta_rows * (1.0 - beta_rows) + keep_grad
        bias_total = bias_total + jnp.sum(keep_grad, axis=0, keepdims=True)
        low_ref[rows, 6 * heads * width :] = rate_grad.astype(jnp.bfloat16)
    gain_grad_ref[...] += gain_total
    bias_grad_ref[...] += bias_total

    masks = [aux_ref[:, 5 + s : 6 + s] for s in range(3)]
    for tile in range(5 * heads):
        cols = slice(tile * width, (tile + 1) * width)
        pre = pre_ref[:, cols]
        sig = jax.nn.sigmoid(pre)
        grad = dact_ref[:, cols]
        if tile < 3 * heads:
            act = act_ref[:, cols]
            grad = norm_ref[:, cols] * (grad - act * col_sum(grad * act))
        grad = grad * sig * (1.0 + pre * (1.0 - sig))
        raw = raw_ref[:, cols]
        joined = jnp.concatenate([grad, head_ref[:, cols]], axis=0)
        head_ref[:, cols] = grad[:8]
        raw_grad = grad * taps_ref[0:1, cols]
        taps_grad_ref[0:1, cols] += jnp.sum(raw * grad, axis=0, keepdims=True)
        for s in range(1, 4):
            shifted = pltpu.roll(joined, block + 8 - s, 0)[:block] * masks[s - 1]
            raw_grad = raw_grad + shifted * taps_ref[s : s + 1, cols]
            taps_grad_ref[s : s + 1, cols] += jnp.sum(raw * shifted, axis=0, keepdims=True)
        low_ref[:, cols] = raw_grad.astype(jnp.bfloat16)


def token_aux(segments):
    length = segments.shape[0]
    seg = segments.astype(jnp.int32)
    chunks = seg.reshape(length // CHUNK, CHUNK)
    last = chunks[:, -1]
    before = jnp.concatenate([jnp.full((1,), -1, jnp.int32), last[:-1]])
    columns = [
        (chunks == before[:, None]).reshape(length),
        (chunks == last[:, None]).reshape(length),
    ]
    for s in range(1, 4):
        columns.append(jnp.pad(seg, (s, 0), constant_values=-1)[:length] == seg)
    for s in range(1, 4):
        columns.append(jnp.pad(seg, (0, s), constant_values=-1)[s:] == seg)
    columns.append(seg)
    columns += [jnp.zeros_like(seg)] * 7
    aux = jnp.stack([c.astype(jnp.float32) for c in columns], axis=1)
    row = chunks.astype(jnp.float32)
    return aux, jnp.concatenate([row, row], axis=1)[:, None, :]


def mixer_forward(raw, aux, segrow, taps, bias, gain, heads, per_step):
    length = raw.shape[0]
    width = HEAD_DIM
    block = per_step * CHUNK
    steps = length // block
    units = per_step * heads
    total_units = steps * units
    cols = raw.shape[1]
    f32 = jnp.float32
    tiles = lambda i: (i, 0)
    cubes = lambda i: (i, 0, 0)
    fixed = lambda i: (0, 0)
    unit_spec = pl.BlockSpec((units, ROWS, width), cubes)
    unit_shape = jax.ShapeDtypeStruct((total_units, ROWS, width), f32)
    return pl.pallas_call(
        partial(fwd_kernel, heads, per_step),
        grid=(steps,),
        in_specs=[
            pl.BlockSpec((block, cols), tiles),
            pl.BlockSpec((block, 16), tiles),
            pl.BlockSpec((per_step, 1, ROWS), cubes),
            pl.BlockSpec(taps.shape, fixed),
            pl.BlockSpec((1, width), fixed),
            pl.BlockSpec((1, width), fixed),
        ],
        out_specs=[
            pl.BlockSpec((block, heads * width), tiles),
            pl.BlockSpec((block, 5 * heads * width), tiles),
            pl.BlockSpec((block, heads * width), tiles),
            unit_spec,
            unit_spec,
            unit_spec,
        ],
        out_shape=[
            jax.ShapeDtypeStruct((length, heads * width), jnp.bfloat16),
            jax.ShapeDtypeStruct((length, 5 * heads * width), f32),
            jax.ShapeDtypeStruct((length, heads * width), f32),
            unit_shape,
            unit_shape,
            unit_shape,
        ],
        scratch_shapes=[
            pltpu.VMEM((heads, width, width), f32),
            pltpu.VMEM((8, 5 * heads * width), f32),
            pltpu.VMEM((block, 5 * heads * width), f32),
        ],
        compiler_params=pltpu.CompilerParams(
            dimension_semantics=("arbitrary",), vmem_limit_bytes=48 * 1024 * 1024
        ),
        name="mixer_forward",
    )(raw, aux, segrow, taps, bias, gain)


def mixer_backward(grad, raw, aux, segrow, saved, taps, bias, gain, heads, per_step):
    pre, recall, inverse, proxy, state = saved
    length = raw.shape[0]
    width = HEAD_DIM
    block = per_step * CHUNK
    steps = length // block
    units = per_step * heads
    cols = raw.shape[1]
    f32 = jnp.float32
    tiles = lambda i: (steps - 1 - i, 0)
    cubes = lambda i: (steps - 1 - i, 0, 0)
    fixed = lambda i: (0, 0)
    unit_spec = pl.BlockSpec((units, ROWS, width), cubes)
    return pl.pallas_call(
        partial(bwd_kernel, heads, per_step),
        grid=(steps,),
        in_specs=[
            pl.BlockSpec((block, heads * width), tiles),
            pl.BlockSpec((block, cols), tiles),
            pl.BlockSpec((block, 16), tiles),
            pl.BlockSpec((per_step, 1, ROWS), cubes),
            pl.BlockSpec((block, 5 * heads * width), tiles),
            pl.BlockSpec((block, heads * width), tiles),
            unit_spec,
            unit_spec,
            unit_spec,
            pl.BlockSpec(taps.shape, fixed),
            pl.BlockSpec((1, width), fixed),
            pl.BlockSpec((1, width), fixed),
        ],
        out_specs=[
            pl.BlockSpec((block, cols), tiles),
            pl.BlockSpec(taps.shape, fixed),
            pl.BlockSpec((1, width), fixed),
            pl.BlockSpec((1, width), fixed),
        ],
        out_shape=[
            jax.ShapeDtypeStruct((length, cols), jnp.bfloat16),
            jax.ShapeDtypeStruct(taps.shape, f32),
            jax.ShapeDtypeStruct((1, width), f32),
            jax.ShapeDtypeStruct((1, width), f32),
        ],
        scratch_shapes=[
            pltpu.VMEM((heads, width, width), f32),
            pltpu.VMEM((8, 5 * heads * width), f32),
            pltpu.VMEM((block, 5 * heads * width), f32),
            pltpu.VMEM((block, 3 * heads * width), f32),
            pltpu.VMEM((block, 5 * heads * width), f32),
        ],
        compiler_params=pltpu.CompilerParams(
            dimension_semantics=("arbitrary",), vmem_limit_bytes=48 * 1024 * 1024
        ),
        name="mixer_backward",
    )(grad, raw, aux, segrow, pre, recall, inverse, proxy, state, taps, bias, gain)


def dot_rows(left, right):
    return lax.dot_general(
        left, right, (((0,), (0,)), ((), ())), preferred_element_type=jnp.float32
    )


def dot_cols(left, right):
    return lax.dot_general(
        left, right, (((1,), (1,)), ((), ())), preferred_element_type=jnp.float32
    )


def row_norm(values, gain):
    scale = lax.rsqrt(jnp.mean(values * values, axis=-1, keepdims=True) + EPS)
    return (values * scale * gain, scale)


def norm_back(grad, values, scale, gain):
    normed = values * scale
    gain_grad = jnp.sum(grad * normed, axis=0)
    weighted = grad * gain
    value_grad = scale * (weighted - normed * jnp.mean(weighted * normed, axis=-1, keepdims=True))
    return (value_grad, gain_grad)


def swiglu_back(hidden_grad, gate_pre, up_pre):
    gate_sigmoid = jax.nn.sigmoid(gate_pre)
    gate_grad = hidden_grad * up_pre * gate_sigmoid * (1.0 + gate_pre * (1.0 - gate_sigmoid))
    up_grad = hidden_grad * gate_pre * gate_sigmoid
    return (gate_grad.astype(jnp.bfloat16), up_grad.astype(jnp.bfloat16))


def body(
    layer_input,
    cotangent,
    segments,
    mix_gain,
    query_weight,
    key_weight,
    value_weight,
    outgate_weight,
    rate_weight,
    conv_query,
    conv_key,
    conv_value,
    decay_bias,
    out_gain,
    out_weight,
    mlp_gain,
    gate_weight,
    up_weight,
    down_weight,
):
    head_index = lax.axis_index("head")
    local_rows = layer_input.shape[0]
    local_heads = query_weight.shape[1] // HEAD_DIM
    own_weight = jnp.concatenate(
        [
            query_weight,
            key_weight,
            value_weight,
            outgate_weight,
            jnp.pad(rate_weight, ((0, 0), (0, HEAD_DIM - rate_weight.shape[1]))),
        ],
        axis=1,
    )
    proj_w, out_w, gate_w, up_w, down_w = (
        lax.all_gather(own_weight, "batch", axis=0, tiled=True),
        lax.all_gather(out_weight, "batch", axis=1, tiled=True),
        lax.all_gather(gate_weight, "batch", axis=0, tiled=True),
        lax.all_gather(up_weight, "batch", axis=0, tiled=True),
        lax.all_gather(down_weight, "batch", axis=1, tiled=True),
    )
    def head_cols(table, per_head):
        return lax.dynamic_slice_in_dim(
            table, head_index * local_heads * per_head, local_heads * per_head, axis=table.ndim - 1
        )

    resid_in = layer_input.astype(jnp.float32)
    normed_in, scale_in = row_norm(resid_in, mix_gain)
    rows_in = lax.all_gather(normed_in.astype(jnp.bfloat16), "head", axis=0, tiled=True)
    raw = jnp.dot(rows_in, proj_w, preferred_element_type=jnp.float32)
    taps = jnp.concatenate(
        [
            head_cols(conv_query, HEAD_DIM),
            head_cols(conv_key, 2 * HEAD_DIM),
            head_cols(conv_value, 2 * HEAD_DIM),
        ],
        axis=1,
    )
    own_bias = head_cols(decay_bias, 1)
    bias = jnp.stack([jnp.zeros_like(own_bias), jnp.zeros_like(own_bias), own_bias], axis=1)
    bias = jnp.pad(bias.reshape(-1), (0, HEAD_DIM - 3 * local_heads))[None]
    aux, segrow = token_aux(segments)
    gain = out_gain[None]
    per_step = 2
    mixed_low, *saved = mixer_forward(raw, aux, segrow, taps, bias, gain, local_heads, per_step)
    resid_mid = resid_in + lax.psum_scatter(
        jnp.dot(mixed_low, out_w, preferred_element_type=jnp.float32),
        "head",
        scatter_dimension=0,
        tiled=True,
    )
    normed_mid, scale_mid = row_norm(resid_mid, mlp_gain)
    normed_mid_low = normed_mid.astype(jnp.bfloat16)
    grad_out = cotangent.astype(jnp.float32)
    rows_mid = lax.all_gather(normed_mid_low, "head", axis=0, tiled=True)
    gate_pre = jnp.dot(rows_mid, gate_w, preferred_element_type=jnp.float32)
    up_pre = jnp.dot(rows_mid, up_w, preferred_element_type=jnp.float32)
    hidden = (jax.nn.silu(gate_pre) * up_pre).astype(jnp.bfloat16)
    layer_output = (
        resid_mid
        + lax.psum_scatter(
            jnp.dot(hidden, down_w, preferred_element_type=jnp.float32).astype(jnp.bfloat16),
            "head",
            scatter_dimension=0,
            tiled=True,
        ).astype(jnp.float32)
    ).astype(jnp.bfloat16)
    rows_grad = lax.all_gather(cotangent, "head", axis=0, tiled=True)
    hidden_grad = dot_cols(rows_grad, down_w)
    gate_grad, up_grad = swiglu_back(hidden_grad, gate_pre, up_pre)
    mid_grad = lax.psum_scatter(
        dot_cols(gate_grad, gate_w) + dot_cols(up_grad, up_w),
        "head",
        scatter_dimension=0,
        tiled=True,
    )
    gate_total, up_total, down_total = (
        lax.psum_scatter(
            dot_rows(rows_mid, gate_grad).astype(jnp.bfloat16),
            "batch",
            scatter_dimension=0,
            tiled=True,
        ).astype(jnp.float32),
        lax.psum_scatter(
            dot_rows(rows_mid, up_grad).astype(jnp.bfloat16),
            "batch",
            scatter_dimension=0,
            tiled=True,
        ).astype(jnp.float32),
        lax.psum_scatter(
            dot_rows(hidden, rows_grad).astype(jnp.bfloat16),
            "batch",
            scatter_dimension=1,
            tiled=True,
        ).astype(jnp.float32),
    )
    mid_back, mlp_gain_part = norm_back(mid_grad, resid_mid, scale_mid, mlp_gain)
    resid_grad = grad_out + mid_back
    rows_resid_grad = lax.all_gather(resid_grad.astype(jnp.bfloat16), "head", axis=0, tiled=True)
    mixed_grad = dot_cols(rows_resid_grad, out_w)
    out_sum = dot_rows(mixed_low, rows_resid_grad)
    raw_low, taps_grad, bias_grad, gain_grad = mixer_backward(
        mixed_grad, raw, aux, segrow, saved, taps, bias, gain, local_heads, per_step
    )
    proj_sum = dot_rows(rows_in, raw_low)
    total = dot_cols(raw_low, proj_w)
    in_grad = lax.psum_scatter(
        total.astype(jnp.bfloat16), "head", scatter_dimension=0, tiled=True
    ).astype(jnp.float32)
    in_back, mix_gain_part = norm_back(in_grad, resid_in, scale_in, mix_gain)
    input_grad = resid_grad + in_back
    proj_total, out_total = (
        lax.psum_scatter(
            proj_sum.astype(jnp.bfloat16), "batch", scatter_dimension=0, tiled=True
        ).astype(jnp.float32),
        lax.psum_scatter(
            out_sum.astype(jnp.bfloat16), "batch", scatter_dimension=1, tiled=True
        ).astype(jnp.float32),
    )
    unit = local_heads * HEAD_DIM
    query_sum = proj_total[:, :unit]
    key_sum = proj_total[:, unit : 3 * unit]
    value_sum = proj_total[:, 3 * unit : 5 * unit]
    outgate_sum = proj_total[:, 5 * unit : 6 * unit]
    rate_sum = proj_total[:, 6 * unit : 6 * unit + 3 * local_heads]
    own_bias_grad = bias_grad[0, : 3 * local_heads].reshape(local_heads, 3)[:, 2]

    def place_cols(table_shape, local_part, per_head):
        return lax.dynamic_update_slice_in_dim(
            jnp.zeros(table_shape, jnp.float32),
            local_part,
            head_index * local_heads * per_head,
            axis=len(table_shape) - 1,
        )

    (
        mix_gain_grad,
        mlp_gain_grad,
        out_gain_grad,
        conv_query_grad,
        conv_key_grad,
        conv_value_grad,
        decay_bias_grad,
    ) = lax.psum(
        (
            mix_gain_part,
            mlp_gain_part,
            gain_grad[0],
            place_cols(conv_query.shape, taps_grad[:, :unit], HEAD_DIM),
            place_cols(conv_key.shape, taps_grad[:, unit : 3 * unit], 2 * HEAD_DIM),
            place_cols(conv_value.shape, taps_grad[:, 3 * unit :], 2 * HEAD_DIM),
            place_cols(decay_bias.shape, own_bias_grad, 1),
        ),
        ("head", "batch"),
    )
    return (
        layer_output,
        input_grad,
        mix_gain_grad,
        query_sum,
        key_sum,
        value_sum,
        outgate_sum,
        rate_sum,
        conv_query_grad,
        conv_key_grad,
        conv_value_grad,
        decay_bias_grad,
        out_gain_grad,
        out_total,
        mlp_gain_grad,
        gate_total,
        up_total,
        down_total,
    )


def solution(mesh):
    placed = (
        P(("batch", "head"), None),
        P(("batch", "head"), None),
        P("batch"),
        P(),
        P("batch", "head"),
        P("batch", "head"),
        P("batch", "head"),
        P("batch", "head"),
        P("batch", "head"),
        P(),
        P(),
        P(),
        P(),
        P(),
        P("head", "batch"),
        P(),
        P("batch", "head"),
        P("batch", "head"),
        P("head", "batch"),
    )
    return jax.shard_map(
        body,
        mesh=mesh,
        in_specs=placed,
        out_specs=(
            P(("batch", "head"), None),
            P(("batch", "head"), None),
            P(),
            P("batch", "head"),
            P("batch", "head"),
            P("batch", "head"),
            P("batch", "head"),
            P("batch", "head"),
            P(),
            P(),
            P(),
            P(),
            P(),
            P("head", "batch"),
            P(),
            P("batch", "head"),
            P("batch", "head"),
            P("head", "batch"),
        ),
        check_vma=False,
    )
```

```python
from functools import partial

import jax
import jax.numpy as jnp
from jax import lax
from jax.experimental import pallas as pl
from jax.experimental.pallas import tpu as pltpu
from jax.sharding import PartitionSpec as P

HEAD_DIM = 128
EPS = 1e-06
EXACT = lax.Precision.HIGHEST
HIGH = lax.Precision.HIGH
FAST = lax.Precision.DEFAULT
NN = ((1,), (0,))
NT = ((1,), (1,))
TN = ((0,), (0,))
LANE = 128
CHUNK = 64
ROWS = 2 * CHUNK
FWD_CHUNKS = 4
BWD_CHUNKS = 2


def mm(left, right, dims=NN, precision=HIGH):
    return lax.dot_general(
        left, right, (dims, ((), ())), precision=precision, preferred_element_type=jnp.float32
    )


def softplus(x):
    return jnp.maximum(x, 0.0) + jnp.log1p(jnp.exp(-jnp.abs(x)))


def chunk_masks():
    row = lax.broadcasted_iota(jnp.int32, (ROWS, ROWS), 0)
    col = lax.broadcasted_iota(jnp.int32, (ROWS, ROWS), 1)
    row_tok, col_tok = row & (CHUNK - 1), col & (CHUNK - 1)
    later = row_tok > col_tok
    same_tok = row_tok == col_tok
    pair = same_tok & (row > col)
    levels = []
    size = 1
    while size < CHUNK:
        upper = (row_tok & size) > (col_tok & size)
        together = (row_tok & (-2 * size)) == (col_tok & (-2 * size))
        levels.append(upper & together)
        size *= 2
    return row, col, later | same_tok, later | pair, pair, levels


def invert(lowers, ident, pair, levels, precision):
    inverses = [ident - jnp.where(pair, lower, 0.0) for lower in lowers]
    for level in levels:
        steps = [
            mm(jnp.where(level, lower, 0.0), inverse, NN, precision)
            for lower, inverse in zip(lowers, inverses)
        ]
        inverses = [
            inverse - mm(inverse, step, NN, precision) for inverse, step in zip(inverses, steps)
        ]
    return inverses


def col_sum(x):
    return jnp.sum(x, axis=-1, keepdims=True)


def twice(x):
    return jnp.concatenate([x, x], axis=0)


def unit_slices(heads, head):
    names = [heads + 2 * head, heads + 2 * head + 1, 3 * heads + 2 * head, 3 * heads + 2 * head + 1]
    names += [head, 5 * heads + head]
    return [slice(n * HEAD_DIM, (n + 1) * HEAD_DIM) for n in names]


def decays_of(cumul, cumul_t, beta_rows, aux, same, lane):
    c_tok = cumul[:, lane + 2 : lane + 3]
    c_end = cumul[CHUNK - 1 :, lane + 2 : lane + 3]
    decay = jnp.where(
        same, jnp.exp(jnp.minimum(twice(c_tok) - cumul_t[lane + 2 : lane + 3, :], 0.0)), 0.0
    )
    beta = jnp.concatenate(
        [beta_rows[:, lane : lane + 1], beta_rows[:, lane + 1 : lane + 2]], axis=0
    )
    start = aux[:, 0:1] * jnp.exp(c_tok)
    final = twice(aux[:, 1:2] * jnp.exp(c_end - c_tok))
    total = aux[CHUNK - 1 :, 0:1] * jnp.exp(c_end)
    return decay, beta, start, final, total


def fwd_kernel(
    heads, per_step, raw_ref, aux_ref, segrow_ref, taps_ref, bias_ref, gain_ref,
    mixed_ref, pre_ref, recall_ref, inv_ref, prox_ref, state_ref, move_ref, probe_ref,
    mem_ref, tail_ref, act_ref,
):
    width = HEAD_DIM
    block = per_step * CHUNK

    @pl.when(pl.program_id(0) == 0)
    def _():
        mem_ref[...] = jnp.zeros_like(mem_ref)
        tail_ref[...] = jnp.zeros_like(tail_ref)

    masks = [aux_ref[:, 2 + s : 3 + s] for s in range(3)]
    for tile in range(5 * heads):
        cols = slice(tile * width, (tile + 1) * width)
        raw = raw_ref[:, cols]
        joined = jnp.concatenate([tail_ref[:, cols], raw], axis=0)
        pre = raw * taps_ref[0:1, cols]
        for s in range(1, 4):
            shifted = pltpu.roll(joined, s, 0)[8:]
            pre = pre + shifted * masks[s - 1] * taps_ref[s : s + 1, cols]
        pre_ref[:, cols] = pre
        tail_ref[:, cols] = raw[block - 8 :]
        act = pre * jax.nn.sigmoid(pre)
        if tile < 3 * heads:
            act = act * lax.rsqrt(col_sum(act * act) + EPS)
        act_ref[:, cols] = act

    row, col, lower_eq, strict, pair, levels = chunk_masks()
    ident = (row == col).astype(jnp.float32)
    tri = (row[:CHUNK, :CHUNK] >= col[:CHUNK, :CHUNK]).astype(jnp.float32)
    rates = raw_ref[:, 6 * heads * width :]
    beta_tile = jax.nn.sigmoid(rates)
    log_tile = -softplus(rates + bias_ref[...])
    units = [(part, head) for part in range(per_step) for head in range(heads)]
    spans = [slice(part * CHUNK, (part + 1) * CHUNK) for part in range(per_step)]
    cumuls = [mm(tri, log_tile[rows], NN, EXACT) for rows in spans]
    cumul_ts = [twice(cumul).T for cumul in cumuls]
    sames = [
        (twice(aux_ref[rows, 8:9]) == segrow_ref[part]) & lower_eq
        for part, rows in enumerate(spans)
    ]
    keys, queries, decays, lowers, scores = [], [], [], [], []
    for part, head in units:
        k1, k2, v1, v2, q0, g0 = unit_slices(heads, head)
        rows = spans[part]
        key = jnp.concatenate([act_ref[rows, k1], act_ref[rows, k2]], axis=0)
        query = act_ref[rows, q0]
        decay = decays_of(
            cumuls[part], cumul_ts[part], beta_tile[rows], aux_ref[rows], sames[part], 3 * head
        )
        dots = mm(jnp.concatenate([key, query], axis=0), key, NT)
        keys.append(key)
        queries.append(query)
        decays.append(decay)
        lowers.append(jnp.where(strict, decay[1] * decay[0] * dots[:ROWS], 0.0))
        scores.append(decay[0][CHUNK:] * dots[ROWS:])
    inverses = invert(lowers, ident, pair, levels, HIGH)
    solved = []
    for u, (part, head) in enumerate(units):
        k1, k2, v1, v2, q0, g0 = unit_slices(heads, head)
        rows = spans[part]
        decay, beta, start, final, total = decays[u]
        inv_ref[u] = inverses[u]
        value = jnp.concatenate([act_ref[rows, v1], act_ref[rows, v2]], axis=0)
        solved.append(
            mm(
                inverses[u],
                jnp.concatenate([beta * value, beta * twice(start) * keys[u]], axis=1),
            )
        )
    moves = [mm(decays[u][3] * keys[u], solved[u], TN) for u in range(len(units))]
    reads = [mm(scores[u], solved[u]) for u in range(len(units))]
    for u, (part, head) in enumerate(units):
        memory = mem_ref[head]
        state_ref[u] = memory
        move_ref[u] = moves[u][:, width:]
        mem_ref[head] = (
            decays[u][4] * memory + moves[u][:, :width] - mm(moves[u][:, width:], memory)
        )
    for u, (part, head) in enumerate(units):
        probe = decays[u][2] * queries[u] - reads[u][:, width:]
        probe_ref[u] = probe
        seen = mm(jnp.concatenate([solved[u][:, width:], probe], axis=0), state_ref[u])
        prox_ref[u] = solved[u][:, :width] - seen[:ROWS]
        recall = reads[u][:, :width] + seen[ROWS:]
        rows = spans[part]
        cols = slice(head * width, (head + 1) * width)
        recall_ref[rows, cols] = recall
        scale = lax.rsqrt(jnp.mean(recall * recall, axis=-1, keepdims=True) + EPS)
        gate = raw_ref[rows, unit_slices(heads, head)[5]]
        mixed = recall * scale * gain_ref[...] * (gate * jax.nn.sigmoid(gate))
        mixed_ref[rows, cols] = mixed.astype(jnp.bfloat16)


def bwd_kernel(
    heads, per_step, grad_ref, raw_ref, aux_ref, segrow_ref, pre_ref, recall_ref, inv_ref,
    prox_ref, state_ref, move_ref, probe_ref, taps_ref, bias_ref, gain_ref,
    low_ref, taps_grad_ref, bias_grad_ref, gain_grad_ref,
    adj_ref, head_ref, act_ref, norm_ref, dact_ref, keep_ref,
):
    width = HEAD_DIM
    block = per_step * CHUNK

    @pl.when(pl.program_id(0) == 0)
    def _():
        adj_ref[...] = jnp.zeros_like(adj_ref)
        head_ref[...] = jnp.zeros_like(head_ref)
        taps_grad_ref[...] = jnp.zeros_like(taps_grad_ref)
        bias_grad_ref[...] = jnp.zeros_like(bias_grad_ref)
        gain_grad_ref[...] = jnp.zeros_like(gain_grad_ref)

    row, col, lower_eq, strict, pair, levels = chunk_masks()
    tri = (row[:CHUNK, :CHUNK] >= col[:CHUNK, :CHUNK]).astype(jnp.float32)
    tri_t = (row[:CHUNK, :CHUNK] <= col[:CHUNK, :CHUNK]).astype(jnp.float32)
    lanes = col[:CHUNK, :]
    rates = raw_ref[:, 6 * heads * width :]
    beta_tile = jax.nn.sigmoid(rates)
    keep_in = rates + bias_ref[...]
    log_tile = -softplus(keep_in)
    units = [(part, head) for part in reversed(range(per_step)) for head in range(heads)]
    spans = [slice(part * CHUNK, (part + 1) * CHUNK) for part in range(per_step)]
    cumuls = [mm(tri, log_tile[rows], NN, EXACT) for rows in spans]
    cumul_ts = [twice(cumul).T for cumul in cumuls]
    sames = [
        (twice(aux_ref[rows, 8:9]) == segrow_ref[part]) & lower_eq
        for part, rows in enumerate(spans)
    ]
    gain_total = jnp.zeros((1, width), jnp.float32)
    out_grads = []
    for part, head in units:
        rows = spans[part]
        q0, g0 = unit_slices(heads, head)[4:]
        recall = recall_ref[rows, q0]
        grad = grad_ref[rows, q0].astype(jnp.float32)
        gate = raw_ref[rows, g0]
        gate_sig = jax.nn.sigmoid(gate)
        silu_gate = gate * gate_sig
        scale = lax.rsqrt(jnp.mean(recall * recall, axis=-1, keepdims=True) + EPS)
        normed = recall * scale
        gain_total = gain_total + jnp.sum(grad * normed * silu_gate, axis=0, keepdims=True)
        weighted = grad * gain_ref[...]
        low_ref[rows, g0] = (
            weighted * normed * gate_sig * (1.0 + gate * (1.0 - gate_sig))
        ).astype(jnp.bfloat16)
        normed_grad = weighted * silu_gate
        out_grads.append(
            scale * (normed_grad - normed * jnp.mean(normed_grad * normed, axis=-1, keepdims=True))
        )
    gain_grad_ref[...] += gain_total
    reads = [
        mm(probe_ref[part * heads + head], out_grads[u], TN) for u, (part, head) in enumerate(units)
    ]
    for u, (part, head) in enumerate(units):
        spot = part * heads + head
        c_end = cumuls[part][CHUNK - 1 :, 3 * head + 2 : 3 * head + 3]
        total = aux_ref[(part + 1) * CHUNK - 1 : (part + 1) * CHUNK, 0:1] * jnp.exp(c_end)
        adjoint = adj_ref[head]
        keep_ref[spot] = adjoint
        adj_ref[head] = total * adjoint + reads[u] - mm(move_ref[spot], adjoint, TN)
    for tile in range(5 * heads):
        cols = slice(tile * width, (tile + 1) * width)
        pre = pre_ref[:, cols]
        act = pre * jax.nn.sigmoid(pre)
        if tile < 3 * heads:
            scale = lax.rsqrt(col_sum(act * act) + EPS)
            norm_ref[:, cols] = jnp.broadcast_to(scale, act.shape)
            act = act * scale
        act_ref[:, cols] = act
    keys, decays, dots = [], [], []
    for u, (part, head) in enumerate(units):
        k1, k2, v1, v2, q0, g0 = unit_slices(heads, head)
        rows = spans[part]
        key = jnp.concatenate([act_ref[rows, k1], act_ref[rows, k2]], axis=0)
        keys.append(key)
        decays.append(
            decays_of(
                cumuls[part], cumul_ts[part], beta_tile[rows], aux_ref[rows], sames[part], 3 * head
            )
        )
        dots.append(mm(jnp.concatenate([key, act_ref[rows, q0]], axis=0), key, NT))
    scores = [decays[u][0][CHUNK:] * dots[u][ROWS:] for u in range(len(units))]
    proxy_grads = [
        mm(scores[u], out_grads[u], TN)
        + mm(decays[u][3] * keys[u], keep_ref[part * heads + head])
        for u, (part, head) in enumerate(units)
    ]
    both_grads = [
        jnp.concatenate(
            [mm(inv_ref[part * heads + head], proxy_grads[u], TN), out_grads[u]], axis=0
        )
        for u, (part, head) in enumerate(units)
    ]
    outers = [
        mm(both_grads[u], prox_ref[part * heads + head], NT)
        for u, (part, head) in enumerate(units)
    ]
    throughs = [
        mm(both_grads[u], state_ref[part * heads + head], NT)
        for u, (part, head) in enumerate(units)
    ]
    finals = [
        decays[u][3] * mm(prox_ref[part * heads + head], keep_ref[part * heads + head], NT)
        for u, (part, head) in enumerate(units)
    ]
    score_grads, inners, beta_parts, log_cols = [], [], [], []
    for u, (part, head) in enumerate(units):
        decay, beta, start, final, total = decays[u]
        key_decay = jnp.where(strict, decay * dots[u][:ROWS], 0.0)
        lower_grad = -outers[u][:ROWS]
        beta_part = lower_grad * key_decay
        dots_grad = jnp.where(strict, lower_grad * beta * decay, 0.0)
        score_grad = outers[u][ROWS:] * decay[CHUNK:]
        log_part = beta_part * beta
        log_part = jnp.concatenate(
            [log_part[:CHUNK], log_part[CHUNK:] + outers[u][ROWS:] * scores[u]], axis=0
        )
        log_cols.append(col_sum(log_part - log_part.T))
        beta_parts.append(col_sum(beta_part))
        score_grads.append(score_grad)
        inners.append(
            mm(jnp.concatenate([dots_grad + dots_grad.T, score_grad], axis=0), keys[u])
        )
    zero = jnp.zeros((CHUNK, width), jnp.float32)
    beta_grads, cumul_grads, end_grads = [zero] * per_step, [zero] * per_step, [zero] * per_step
    for u, (part, head) in enumerate(units):
        k1, k2, v1, v2, q0, g0 = unit_slices(heads, head)
        rows = spans[part]
        spot = part * heads + head
        lane = 3 * head
        decay, beta, start, final, total = decays[u]
        through, final_part, right_grad = throughs[u], finals[u], both_grads[u][:ROWS]
        query = act_ref[rows, q0]
        value = jnp.concatenate([act_ref[rows, v1], act_ref[rows, v2]], axis=0)
        beta_start = beta * twice(start)
        key_through = col_sum(keys[u] * through[:ROWS])
        query_through = start * col_sum(query * through[ROWS:])
        final_sum = col_sum(keys[u] * final_part)
        key_grad = (
            inners[u][:ROWS]
            + mm(score_grads[u], query, TN)
            - beta_start * through[:ROWS]
            + final_part
        )
        dact_ref[rows, k1] = key_grad[:CHUNK]
        dact_ref[rows, k2] = key_grad[CHUNK:]
        value_grad = beta * right_grad
        dact_ref[rows, v1] = value_grad[:CHUNK]
        dact_ref[rows, v2] = value_grad[CHUNK:]
        dact_ref[rows, q0] = inners[u][ROWS:] + start * through[ROWS:]
        beta_col = col_sum(right_grad * value) - twice(start) * key_through + beta_parts[u]
        c_grad = log_cols[u] - beta_start * key_through - final_sum
        c_grad = c_grad[:CHUNK] + c_grad[CHUNK:] + query_through
        end_part = jnp.sum(final_sum, axis=0, keepdims=True) + total * jnp.sum(
            col_sum(state_ref[spot] * keep_ref[spot]), axis=0, keepdims=True
        )
        beta_grads[part] = jnp.where(
            lanes == lane,
            beta_col[:CHUNK],
            jnp.where(lanes == lane + 1, beta_col[CHUNK:], beta_grads[part]),
        )
        cumul_grads[part] = jnp.where(lanes == lane + 2, c_grad, cumul_grads[part])
        end_grads[part] = jnp.where(lanes == lane + 2, end_part, end_grads[part])
    bias_total = jnp.zeros((1, width), jnp.float32)
    for part, rows in enumerate(spans):
        log_grad = mm(tri_t, cumul_grads[part], NN, EXACT) + end_grads[part]
        beta_rows = beta_tile[rows]
        keep_grad = -log_grad * jax.nn.sigmoid(keep_in[rows]) * aux_ref[rows, 2:3]
        rate_grad = beta_grads[part] * beta_rows * (1.0 - beta_rows) + keep_grad
        bias_total = bias_total + jnp.sum(keep_grad, axis=0, keepdims=True)
        low_ref[rows, 6 * heads * width :] = rate_grad.astype(jnp.bfloat16)
    bias_grad_ref[...] += bias_total

    masks = [aux_ref[:, 5 + s : 6 + s] for s in range(3)]
    for tile in range(5 * heads):
        cols = slice(tile * width, (tile + 1) * width)
        pre = pre_ref[:, cols]
        sig = jax.nn.sigmoid(pre)
        grad = dact_ref[:, cols]
        if tile < 3 * heads:
            act = act_ref[:, cols]
            grad = norm_ref[:, cols] * (grad - act * col_sum(grad * act))
        grad = grad * sig * (1.0 + pre * (1.0 - sig))
        raw = raw_ref[:, cols]
        joined = jnp.concatenate([grad, head_ref[:, cols]], axis=0)
        head_ref[:, cols] = grad[:8]
        raw_grad = grad * taps_ref[0:1, cols]
        taps_grad_ref[0:1, cols] += jnp.sum(raw * grad, axis=0, keepdims=True)
        for s in range(1, 4):
            shifted = pltpu.roll(joined, block + 8 - s, 0)[:block] * masks[s - 1]
            raw_grad = raw_grad + shifted * taps_ref[s : s + 1, cols]
            taps_grad_ref[s : s + 1, cols] += jnp.sum(raw * shifted, axis=0, keepdims=True)
        low_ref[:, cols] = raw_grad.astype(jnp.bfloat16)


def token_aux(segments):
    length = segments.shape[0]
    seg = segments.astype(jnp.int32)
    chunks = seg.reshape(length // CHUNK, CHUNK)
    last = chunks[:, -1]
    before = jnp.concatenate([jnp.full((1,), -1, jnp.int32), last[:-1]])
    columns = [
        (chunks == before[:, None]).reshape(length),
        (chunks == last[:, None]).reshape(length),
    ]
    for s in range(1, 4):
        columns.append(jnp.pad(seg, (s, 0), constant_values=-1)[:length] == seg)
    for s in range(1, 4):
        columns.append(jnp.pad(seg, (0, s), constant_values=-1)[s:] == seg)
    columns.append(seg)
    columns += [jnp.zeros_like(seg)] * 7
    aux = jnp.stack([c.astype(jnp.float32) for c in columns], axis=1)
    row = chunks.astype(jnp.float32)
    return aux, jnp.concatenate([row, row], axis=1)[:, None, :]


def mixer_forward(raw, aux, segrow, taps, bias, gain, heads, per_step):
    length = raw.shape[0]
    width = HEAD_DIM
    block = per_step * CHUNK
    steps = length // block
    units = per_step * heads
    total_units = steps * units
    cols = raw.shape[1]
    f32 = jnp.float32
    tiles = lambda i: (i, 0)
    cubes = lambda i: (i, 0, 0)
    fixed = lambda i: (0, 0)
    unit_spec = pl.BlockSpec((units, ROWS, width), cubes)
    unit_shape = jax.ShapeDtypeStruct((total_units, ROWS, width), f32)
    return pl.pallas_call(
        partial(fwd_kernel, heads, per_step),
        grid=(steps,),
        in_specs=[
            pl.BlockSpec((block, cols), tiles),
            pl.BlockSpec((block, 16), tiles),
            pl.BlockSpec((per_step, 1, ROWS), cubes),
            pl.BlockSpec(taps.shape, fixed),
            pl.BlockSpec((1, width), fixed),
            pl.BlockSpec((1, width), fixed),
        ],
        out_specs=[
            pl.BlockSpec((block, heads * width), tiles),
            pl.BlockSpec((block, 5 * heads * width), tiles),
            pl.BlockSpec((block, heads * width), tiles),
            unit_spec,
            unit_spec,
            unit_spec,
            unit_spec,
            pl.BlockSpec((units, CHUNK, width), cubes),
        ],
        out_shape=[
            jax.ShapeDtypeStruct((length, heads * width), jnp.bfloat16),
            jax.ShapeDtypeStruct((length, 5 * heads * width), f32),
            jax.ShapeDtypeStruct((length, heads * width), f32),
            unit_shape,
            unit_shape,
            unit_shape,
            unit_shape,
            jax.ShapeDtypeStruct((total_units, CHUNK, width), f32),
        ],
        scratch_shapes=[
            pltpu.VMEM((heads, width, width), f32),
            pltpu.VMEM((8, 5 * heads * width), f32),
            pltpu.VMEM((block, 5 * heads * width), f32),
        ],
        compiler_params=pltpu.CompilerParams(
            dimension_semantics=("arbitrary",), vmem_limit_bytes=48 * 1024 * 1024
        ),
        name="mixer_forward",
    )(raw, aux, segrow, taps, bias, gain)


def mixer_backward(grad, raw, aux, segrow, saved, taps, bias, gain, heads, per_step):
    pre, recall, inverse, proxy, state, move, probe = saved
    length = raw.shape[0]
    width = HEAD_DIM
    block = per_step * CHUNK
    steps = length // block
    units = per_step * heads
    cols = raw.shape[1]
    f32 = jnp.float32
    tiles = lambda i: (steps - 1 - i, 0)
    cubes = lambda i: (steps - 1 - i, 0, 0)
    fixed = lambda i: (0, 0)
    unit_spec = pl.BlockSpec((units, ROWS, width), cubes)
    return pl.pallas_call(
        partial(bwd_kernel, heads, per_step),
        grid=(steps,),
        in_specs=[
            pl.BlockSpec((block, heads * width), tiles),
            pl.BlockSpec((block, cols), tiles),
            pl.BlockSpec((block, 16), tiles),
            pl.BlockSpec((per_step, 1, ROWS), cubes),
            pl.BlockSpec((block, 5 * heads * width), tiles),
            pl.BlockSpec((block, heads * width), tiles),
            unit_spec,
            unit_spec,
            unit_spec,
            unit_spec,
            pl.BlockSpec((units, CHUNK, width), cubes),
            pl.BlockSpec(taps.shape, fixed),
            pl.BlockSpec((1, width), fixed),
            pl.BlockSpec((1, width), fixed),
        ],
        out_specs=[
            pl.BlockSpec((block, cols), tiles),
            pl.BlockSpec(taps.shape, fixed),
            pl.BlockSpec((1, width), fixed),
            pl.BlockSpec((1, width), fixed),
        ],
        out_shape=[
            jax.ShapeDtypeStruct((length, cols), jnp.bfloat16),
            jax.ShapeDtypeStruct(taps.shape, f32),
            jax.ShapeDtypeStruct((1, width), f32),
            jax.ShapeDtypeStruct((1, width), f32),
        ],
        scratch_shapes=[
            pltpu.VMEM((heads, width, width), f32),
            pltpu.VMEM((8, 5 * heads * width), f32),
            pltpu.VMEM((block, 5 * heads * width), f32),
            pltpu.VMEM((block, 3 * heads * width), f32),
            pltpu.VMEM((block, 5 * heads * width), f32),
            pltpu.VMEM((units, width, width), f32),
        ],
        compiler_params=pltpu.CompilerParams(
            dimension_semantics=("arbitrary",), vmem_limit_bytes=48 * 1024 * 1024
        ),
        name="mixer_backward",
    )(grad, raw, aux, segrow, pre, recall, inverse, proxy, state, move, probe, taps, bias, gain)


def up_to(x, multiple):
    return -(-x // multiple) * multiple


def row_scale(values):
    return lax.rsqrt(jnp.mean(values * values, axis=-1, keepdims=True) + EPS)


def norm_back(grad, values, scale, gain):
    normed = values * scale
    gain_grad = jnp.sum(grad * normed, axis=0)
    weighted = grad * gain
    value_grad = scale * (weighted - normed * jnp.mean(weighted * normed, axis=-1, keepdims=True))
    return (value_grad, gain_grad)


def dot(left, right, dims=NN):
    return lax.dot_general(left, right, (dims, ((), ())), preferred_element_type=jnp.float32)


def swap(x, axis, bit):
    size = lax.axis_size(axis)
    return lax.ppermute(x, axis, [(i, i ^ bit) for i in range(size)])


def line_gather(x, axis):
    size = lax.axis_size(axis)
    index = lax.axis_index(axis)
    up = [(i, i + 1) for i in range(size - 1)]
    down = [(i + 1, i) for i in range(size - 1)]
    below, above = [], []
    from_below = from_above = x
    for _ in range(size - 1):
        from_below = lax.ppermute(from_below, axis, up)
        from_above = lax.ppermute(from_above, axis, down)
        below.insert(0, from_below)
        above.append(from_above)
    stacked = jnp.stack(below + [x] + above)
    return lax.dynamic_slice_in_dim(stacked, size - 1 - index, size, axis=0)


def direct_gather(x, axis):
    size = lax.axis_size(axis)
    index = lax.axis_index(axis)
    pieces = []
    for step in range(1 - size, size):
        if step == 0:
            pieces.append(x)
        else:
            pairs = [(i + step, i) for i in range(size) if 0 <= i + step < size]
            pieces.append(lax.ppermute(x, axis, pairs))
    return lax.dynamic_slice_in_dim(jnp.stack(pieces), size - 1 - index, size, axis=0)


def line_scatter(blocks, axis):
    size = lax.axis_size(axis)
    index = lax.axis_index(axis)

    def block(j):
        return lax.dynamic_index_in_dim(blocks, jnp.clip(j, 0, size - 1), 0, keepdims=False)

    up = down = None
    for step in range(1, size):
        up_next, down_next = block(index + size - step), block(index - size + step)
        if step > 1:
            up_next = (up_next.astype(jnp.float32) + up.astype(jnp.float32)).astype(blocks.dtype)
            down_next = (down_next.astype(jnp.float32) + down.astype(jnp.float32)).astype(
                blocks.dtype
            )
        up = lax.ppermute(up_next, axis, [(i, i + 1) for i in range(step)])
        down = lax.ppermute(
            down_next, axis, [(i, i - 1) for i in range(size - step, size)]
        )
    own = block(index).astype(jnp.float32)
    return own + up.astype(jnp.float32) + down.astype(jnp.float32)


def bits_of(size):
    return [1 << b for b in range(size.bit_length() - 1)]


def tree_gather(x, axis):
    size = lax.axis_size(axis)
    index = lax.axis_index(axis)
    bits = bits_of(size)
    half = x.shape[1] // 2 // LANE * LANE
    halves = []
    for part, order in ((x[:, :half], bits[:0:-1] + bits[:1]), (x[:, half:], bits[1:] + bits[:1])):
        joined = part[None]
        places = [0]
        for bit in order:
            got = swap(joined, axis, bit)
            joined = jnp.concatenate([joined, got], axis=0)
            places = places + [p ^ bit for p in places]
        halves.append((joined, places))
    out = []
    for j in range(size):
        out.append([])
        for joined, places in halves:
            where = jnp.asarray([places.index(r) for r in range(size)], jnp.int32)
            spot = lax.dynamic_index_in_dim(where, index ^ j, 0, keepdims=False)
            out[j].append(lax.dynamic_index_in_dim(joined, spot, 0, keepdims=False))
    return jnp.concatenate([jnp.concatenate(pair, axis=1) for pair in out], axis=0)


def tree_scatter(blocks, axis):
    size = lax.axis_size(axis)
    index = lax.axis_index(axis)
    bits = bits_of(size)
    cols = blocks.shape[2]
    half = cols // 2 // LANE * LANE
    out = []
    for part, order in (
        (blocks[:, :, :half], bits[:1] + bits[1:]),
        (blocks[:, :, half:], bits[:1] + bits[:0:-1]),
    ):
        rows = part.shape[1]
        held = part.reshape((2,) * len(bits) + (rows, part.shape[2]))
        left = list(reversed(bits))
        for bit in order:
            at = left.index(bit)
            mine = (index // bit) % 2
            sent = lax.dynamic_index_in_dim(held, 1 - mine, at, keepdims=False)
            kept = lax.dynamic_index_in_dim(held, mine, at, keepdims=False)
            got = swap(sent.astype(jnp.bfloat16), axis, bit)
            held = kept.astype(jnp.float32) + got.astype(jnp.float32)
            left.pop(at)
        out.append(held)
    return jnp.concatenate(out, axis=1)


def body(
    layer_input,
    cotangent,
    segments,
    mix_gain,
    query_weight,
    key_weight,
    value_weight,
    outgate_weight,
    rate_weight,
    conv_query,
    conv_key,
    conv_value,
    decay_bias,
    out_gain,
    out_weight,
    mlp_gain,
    gate_weight,
    up_weight,
    down_weight,
):
    f32, bf16 = jnp.float32, jnp.bfloat16
    head_index = lax.axis_index("head")
    n_head, n_batch = lax.axis_size("head"), lax.axis_size("batch")
    rows, width = layer_input.shape
    length = rows * n_head
    local_heads = query_weight.shape[1] // HEAD_DIM
    unit = local_heads * HEAD_DIM
    mix_cols = 6 * unit + HEAD_DIM
    ff = gate_weight.shape[1]
    ff_pad = up_to(ff, LANE)

    own_mix = jnp.concatenate(
        [
            query_weight,
            key_weight,
            value_weight,
            outgate_weight,
            jnp.pad(rate_weight, ((0, 0), (0, HEAD_DIM - rate_weight.shape[1]))),
            out_weight.T,
        ],
        axis=1,
    )
    tokens = line_gather(layer_input, "head")
    mix_w = tree_gather(own_mix, "batch")
    proj_w, own_out_t = mix_w[:, :mix_cols], mix_w[:, mix_cols:]

    pad = ((0, 0), (0, ff_pad - ff))
    own_ff = jnp.concatenate(
        [jnp.pad(gate_weight, pad), jnp.pad(up_weight, pad), jnp.pad(down_weight.T, pad)], axis=1
    )
    own_ff, tokens, mix_w_done = lax.optimization_barrier((own_ff, tokens, own_out_t))
    shards = [own_ff]
    for bit in bits_of(n_head)[1:]:
        shards = shards + [swap(shard, "head", bit) for shard in shards]
    ff_sets = [lax.all_gather(shard, "batch", axis=0, tiled=True) for shard in shards]

    all_in = tokens.reshape(length, width).astype(f32)
    scale_all = row_scale(all_in)
    rows_in = (all_in * scale_all * mix_gain).astype(bf16)
    raw = dot(rows_in, proj_w)

    def head_cols(table, per_head):
        return lax.dynamic_slice_in_dim(
            table, head_index * local_heads * per_head, local_heads * per_head, axis=table.ndim - 1
        )

    taps = jnp.concatenate(
        [
            head_cols(conv_query, HEAD_DIM),
            head_cols(conv_key, 2 * HEAD_DIM),
            head_cols(conv_value, 2 * HEAD_DIM),
        ],
        axis=1,
    )
    own_bias = head_cols(decay_bias, 1)
    bias = jnp.stack([jnp.zeros_like(own_bias), jnp.zeros_like(own_bias), own_bias], axis=1)
    bias = jnp.pad(bias.reshape(-1), (0, HEAD_DIM - 3 * local_heads))[None]
    aux, segrow = token_aux(segments)
    gain = out_gain[None]
    out_t = direct_gather(mix_w_done, "head")
    pair_grad = swap(cotangent, "head", 1)
    mixed_low, *saved = mixer_forward(raw, aux, segrow, taps, bias, gain, local_heads, FWD_CHUNKS)

    mixed_all = lax.all_to_all(
        mixed_low.reshape(n_head, rows, unit), "head", split_axis=0, concat_axis=0, tiled=True
    )
    resid_in = layer_input.astype(f32)
    resid_mid = resid_in + sum(dot(mixed_all[j], out_t[j], NT) for j in range(n_head))
    scale_mid = row_scale(resid_mid)
    normed_mid = (resid_mid * scale_mid * mlp_gain).astype(bf16)
    pair_mid = jnp.concatenate([normed_mid, swap(normed_mid, "head", 1)], axis=0)
    pair_cot = jnp.concatenate([cotangent, pair_grad], axis=0)
    out_part = mid_part = None
    ff_grads = []
    for ff_set in ff_sets:
        gate_up = dot(pair_mid, ff_set[:, : 2 * ff_pad])
        gate_pre, up_pre = gate_up[:, :ff_pad], gate_up[:, ff_pad:]
        gate_sig = jax.nn.sigmoid(gate_pre)
        silu_gate = gate_pre * gate_sig
        hidden = (silu_gate * up_pre).astype(bf16)
        hidden_grad = dot(pair_cot, ff_set[:, 2 * ff_pad :])
        gate_grad = (
            hidden_grad * up_pre * gate_sig * (1.0 + gate_pre * (1.0 - gate_sig))
        ).astype(bf16)
        up_grad = (hidden_grad * silu_gate).astype(bf16)
        both_grad = jnp.concatenate([gate_grad, up_grad], axis=1)
        out_here = dot(hidden, ff_set[:, 2 * ff_pad :], NT)
        mid_here = dot(both_grad, ff_set[:, : 2 * ff_pad], NT)
        out_part = out_here if out_part is None else out_part + out_here
        mid_part = mid_here if mid_part is None else mid_part + mid_here
        ff_grads.append((both_grad, hidden))
    mid_grad = mid_part[:rows] + swap(mid_part[rows:].astype(bf16), "head", 1).astype(f32)
    mid_back, mlp_gain_part = norm_back(mid_grad, resid_mid, scale_mid, mlp_gain)
    resid_grad = cotangent.astype(f32) + mid_back
    branch_grad = resid_grad.astype(bf16)
    mixed_grad = jnp.stack([dot(branch_grad, out_t[j]) for j in range(n_head)]).astype(bf16)
    mixed_grad = lax.all_to_all(
        mixed_grad, "head", split_axis=0, concat_axis=0, tiled=True
    ).reshape(length, unit)
    layer_output = (
        resid_mid + out_part[:rows] + swap(out_part[rows:].astype(bf16), "head", 1).astype(f32)
    ).astype(bf16)

    ff_sums = [
        lax.psum_scatter(
            jnp.concatenate([dot(pair_mid, both, TN), dot(pair_cot, hidden, TN)], axis=1).astype(
                bf16
            ),
            "batch",
            scatter_dimension=0,
            tiled=True,
        )
        for both, hidden in reversed(ff_grads)
    ]
    branch_rows, mixed_grad = lax.optimization_barrier((branch_grad, mixed_grad))
    branch_rows = direct_gather(branch_rows, "head").reshape(length, width)

    raw_low, taps_grad, bias_grad, gain_grad = mixer_backward(
        mixed_grad, raw, aux, segrow, saved, taps, bias, gain, local_heads, BWD_CHUNKS
    )
    total = dot(raw_low, proj_w, NT)
    in_grad = line_scatter(total.astype(bf16).reshape(n_head, rows, width), "head")
    mix_gain_part = jnp.sum(total * (all_in * scale_all), axis=0)
    mix_sum = jnp.concatenate([dot(rows_in, raw_low, TN), dot(branch_rows, mixed_low, TN)], axis=1)
    mix_total = tree_scatter(
        mix_sum.astype(bf16).reshape(n_batch, width // n_batch, mix_cols + unit), "batch"
    )
    in_back, _ = norm_back(in_grad, resid_in, row_scale(resid_in), mix_gain)
    input_grad = resid_grad + in_back

    ff_total = ff_sums
    for bit in reversed(bits_of(n_head)[1:]):
        half = len(ff_total) // 2
        ff_total = [
            kept.astype(f32) + swap(sent.astype(bf16), "head", bit).astype(f32)
            for sent, kept in zip(ff_total[:half], ff_total[half:])
        ]
    ff_total = ff_total[0].astype(f32)

    own_bias_grad = bias_grad[0, : 3 * local_heads].reshape(local_heads, 3)[:, 2]
    small = [
        taps_grad[:, :unit].reshape(-1),
        taps_grad[:, unit : 3 * unit].reshape(-1),
        taps_grad[:, 3 * unit :].reshape(-1),
        own_bias_grad,
        gain_grad[0],
        mlp_gain_part,
        mix_gain_part,
    ]
    lengths = [part.shape[0] for part in small]
    packed = pack(small)
    for bit in bits_of(n_batch):
        packed = packed + swap(packed, "batch", bit)
    small = unpack(packed, lengths)

    def place_cols(table_shape, local_part, per_head):
        local_part = local_part.reshape(table_shape[:-1] + (-1,))
        return lax.dynamic_update_slice_in_dim(
            jnp.zeros(table_shape, f32),
            local_part,
            head_index * local_heads * per_head,
            axis=len(table_shape) - 1,
        ).reshape(-1)

    tables = [
        place_cols(conv_query.shape, small[0], HEAD_DIM),
        place_cols(conv_key.shape, small[1], 2 * HEAD_DIM),
        place_cols(conv_value.shape, small[2], 2 * HEAD_DIM),
        place_cols(decay_bias.shape, small[3], 1),
    ] + small[4:]
    lengths = [part.shape[0] for part in tables]
    packed = pack(tables)
    for bit in bits_of(n_head):
        packed = packed + swap(packed, "head", bit)
    tables = unpack(packed, lengths)
    return (
        layer_output,
        input_grad,
        tables[6],
        mix_total[:, :unit],
        mix_total[:, unit : 3 * unit],
        mix_total[:, 3 * unit : 5 * unit],
        mix_total[:, 5 * unit : 6 * unit],
        mix_total[:, 6 * unit : 6 * unit + rate_weight.shape[1]],
        tables[0].reshape(conv_query.shape),
        tables[1].reshape(conv_key.shape),
        tables[2].reshape(conv_value.shape),
        tables[3],
        tables[4],
        mix_total[:, mix_cols:].T,
        tables[5],
        ff_total[:, :ff],
        ff_total[:, ff_pad : ff_pad + ff],
        ff_total[:, 2 * ff_pad : 2 * ff_pad + ff].T,
    )


def pack(parts):
    flat = jnp.concatenate(parts)
    return jnp.pad(flat, (0, -flat.shape[0] % (8 * LANE))).reshape(-1, LANE)


def unpack(packed, lengths):
    flat = packed.reshape(-1)
    out, at = [], 0
    for size in lengths:
        out.append(flat[at : at + size])
        at += size
    return out


def solution(mesh):
    placed = (
        P(("batch", "head"), None),
        P(("batch", "head"), None),
        P("batch"),
        P(),
        P("batch", "head"),
        P("batch", "head"),
        P("batch", "head"),
        P("batch", "head"),
        P("batch", "head"),
        P(),
        P(),
        P(),
        P(),
        P(),
        P("head", "batch"),
        P(),
        P("batch", "head"),
        P("batch", "head"),
        P("head", "batch"),
    )
    return jax.shard_map(
        body,
        mesh=mesh,
        in_specs=placed,
        out_specs=(
            P(("batch", "head"), None),
            P(("batch", "head"), None),
            P(),
            P("batch", "head"),
            P("batch", "head"),
            P("batch", "head"),
            P("batch", "head"),
            P("batch", "head"),
            P(),
            P(),
            P(),
            P(),
            P(),
            P("head", "batch"),
            P(),
            P("batch", "head"),
            P("batch", "head"),
            P("head", "batch"),
        ),
        check_vma=False,
    )
```

```python
from functools import partial

import jax
import jax.numpy as jnp
from jax import lax
from jax.experimental import pallas as pl
from jax.experimental.pallas import tpu as pltpu
from jax.sharding import PartitionSpec as P

HEAD_DIM = 128
EPS = 1e-06
EXACT = lax.Precision.HIGHEST
HIGH = lax.Precision.HIGH
FAST = lax.Precision.DEFAULT
NN = ((1,), (0,))
NT = ((1,), (1,))
TN = ((0,), (0,))
LANE = 128
CHUNK = 64
ROWS = 2 * CHUNK
FWD_CHUNKS = 4
BWD_CHUNKS = 2
SPANS = 2


def mm(left, right, dims=NN, precision=HIGH):
    return lax.dot_general(
        left, right, (dims, ((), ())), precision=precision, preferred_element_type=jnp.float32
    )


def softplus(x):
    return jnp.maximum(x, 0.0) + jnp.log1p(jnp.exp(-jnp.abs(x)))


def chunk_masks():
    row = lax.broadcasted_iota(jnp.int32, (ROWS, ROWS), 0)
    col = lax.broadcasted_iota(jnp.int32, (ROWS, ROWS), 1)
    row_tok, col_tok = row & (CHUNK - 1), col & (CHUNK - 1)
    later = row_tok > col_tok
    same_tok = row_tok == col_tok
    pair = same_tok & (row > col)
    levels = []
    size = 1
    while size < CHUNK:
        upper = (row_tok & size) > (col_tok & size)
        together = (row_tok & (-2 * size)) == (col_tok & (-2 * size))
        levels.append(upper & together)
        size *= 2
    return row, col, later | same_tok, later | pair, pair, levels


def invert(lowers, ident, pair, levels, precision):
    inverses = [ident - jnp.where(pair, lower, 0.0) for lower in lowers]
    for level in levels:
        steps = [
            mm(jnp.where(level, lower, 0.0), inverse, NN, precision)
            for lower, inverse in zip(lowers, inverses)
        ]
        inverses = [
            inverse - mm(inverse, step, NN, precision) for inverse, step in zip(inverses, steps)
        ]
    return inverses


def col_sum(x):
    return jnp.sum(x, axis=-1, keepdims=True)


def twice(x):
    return jnp.concatenate([x, x], axis=0)


def unit_slices(heads, head):
    names = [heads + 2 * head, heads + 2 * head + 1, 3 * heads + 2 * head, 3 * heads + 2 * head + 1]
    names += [head, 5 * heads + head]
    return [slice(n * HEAD_DIM, (n + 1) * HEAD_DIM) for n in names]


def decays_of(cumul, cumul_t, beta_rows, aux, same, lane):
    c_tok = cumul[:, lane + 2 : lane + 3]
    c_end = cumul[CHUNK - 1 :, lane + 2 : lane + 3]
    decay = jnp.where(
        same, jnp.exp(jnp.minimum(twice(c_tok) - cumul_t[lane + 2 : lane + 3, :], 0.0)), 0.0
    )
    beta = jnp.concatenate(
        [beta_rows[:, lane : lane + 1], beta_rows[:, lane + 1 : lane + 2]], axis=0
    )
    start = aux[:, 0:1] * jnp.exp(c_tok)
    final = twice(aux[:, 1:2] * jnp.exp(c_end - c_tok))
    total = aux[CHUNK - 1 :, 0:1] * jnp.exp(c_end)
    return decay, beta, start, final, total


def fwd_kernel(
    heads, per_step, raw_ref, aux_ref, segrow_ref, taps_ref, bias_ref, gain_ref, mem_in, tail_in,
    mixed_ref, pre_ref, recall_ref, inv_ref, prox_ref, state_ref, move_ref, probe_ref,
    mem_ref, tail_ref, act_ref,
):
    width = HEAD_DIM
    block = per_step * CHUNK

    @pl.when(pl.program_id(0) == 0)
    def _():
        mem_ref[...] = mem_in[...]
        tail_ref[...] = tail_in[...]

    masks = [aux_ref[:, 2 + s : 3 + s] for s in range(3)]
    for tile in range(5 * heads):
        cols = slice(tile * width, (tile + 1) * width)
        raw = raw_ref[:, cols]
        joined = jnp.concatenate([tail_ref[:, cols], raw], axis=0)
        pre = raw * taps_ref[0:1, cols]
        for s in range(1, 4):
            shifted = pltpu.roll(joined, s, 0)[8:]
            pre = pre + shifted * masks[s - 1] * taps_ref[s : s + 1, cols]
        pre_ref[:, cols] = pre
        tail_ref[:, cols] = raw[block - 8 :]
        act = pre * jax.nn.sigmoid(pre)
        if tile < 3 * heads:
            act = act * lax.rsqrt(col_sum(act * act) + EPS)
        act_ref[:, cols] = act

    row, col, lower_eq, strict, pair, levels = chunk_masks()
    ident = (row == col).astype(jnp.float32)
    tri = (row[:CHUNK, :CHUNK] >= col[:CHUNK, :CHUNK]).astype(jnp.float32)
    rates = raw_ref[:, 6 * heads * width :]
    beta_tile = jax.nn.sigmoid(rates)
    log_tile = -softplus(rates + bias_ref[...])
    units = [(part, head) for part in range(per_step) for head in range(heads)]
    spans = [slice(part * CHUNK, (part + 1) * CHUNK) for part in range(per_step)]
    cumuls = [mm(tri, log_tile[rows], NN, EXACT) for rows in spans]
    cumul_ts = [twice(cumul).T for cumul in cumuls]
    sames = [
        (twice(aux_ref[rows, 8:9]) == segrow_ref[part]) & lower_eq
        for part, rows in enumerate(spans)
    ]
    keys, queries, decays, lowers, scores = [], [], [], [], []
    for part, head in units:
        k1, k2, v1, v2, q0, g0 = unit_slices(heads, head)
        rows = spans[part]
        key = jnp.concatenate([act_ref[rows, k1], act_ref[rows, k2]], axis=0)
        query = act_ref[rows, q0]
        decay = decays_of(
            cumuls[part], cumul_ts[part], beta_tile[rows], aux_ref[rows], sames[part], 3 * head
        )
        dots = mm(jnp.concatenate([key, query], axis=0), key, NT)
        keys.append(key)
        queries.append(query)
        decays.append(decay)
        lowers.append(jnp.where(strict, decay[1] * decay[0] * dots[:ROWS], 0.0))
        scores.append(decay[0][CHUNK:] * dots[ROWS:])
    inverses = invert(lowers, ident, pair, levels, HIGH)
    solved = []
    for u, (part, head) in enumerate(units):
        k1, k2, v1, v2, q0, g0 = unit_slices(heads, head)
        rows = spans[part]
        decay, beta, start, final, total = decays[u]
        inv_ref[u] = inverses[u]
        value = jnp.concatenate([act_ref[rows, v1], act_ref[rows, v2]], axis=0)
        solved.append(
            mm(
                inverses[u],
                jnp.concatenate([beta * value, beta * twice(start) * keys[u]], axis=1),
            )
        )
    moves = [mm(decays[u][3] * keys[u], solved[u], TN) for u in range(len(units))]
    reads = [mm(scores[u], solved[u]) for u in range(len(units))]
    for u, (part, head) in enumerate(units):
        memory = mem_ref[head]
        state_ref[u] = memory
        move_ref[u] = moves[u][:, width:]
        mem_ref[head] = (
            decays[u][4] * memory + moves[u][:, :width] - mm(moves[u][:, width:], memory)
        )
    for u, (part, head) in enumerate(units):
        probe = decays[u][2] * queries[u] - reads[u][:, width:]
        probe_ref[u] = probe
        seen = mm(jnp.concatenate([solved[u][:, width:], probe], axis=0), state_ref[u])
        prox_ref[u] = solved[u][:, :width] - seen[:ROWS]
        recall = reads[u][:, :width] + seen[ROWS:]
        rows = spans[part]
        cols = slice(head * width, (head + 1) * width)
        recall_ref[rows, cols] = recall
        scale = lax.rsqrt(jnp.mean(recall * recall, axis=-1, keepdims=True) + EPS)
        gate = raw_ref[rows, unit_slices(heads, head)[5]]
        mixed = recall * scale * gain_ref[...] * (gate * jax.nn.sigmoid(gate))
        mixed_ref[rows, cols] = mixed.astype(jnp.bfloat16)


def bwd_kernel(
    heads, per_step, grad_ref, raw_ref, aux_ref, segrow_ref, pre_ref, recall_ref, inv_ref,
    prox_ref, state_ref, move_ref, probe_ref, taps_ref, bias_ref, gain_ref,
    adj_in, head_in, taps_grad_in, bias_grad_in, gain_grad_in, low_in,
    low_ref, taps_grad_ref, bias_grad_ref, gain_grad_ref, adj_ref, head_ref,
    act_ref, norm_ref, dact_ref, keep_ref,
):
    width = HEAD_DIM
    block = per_step * CHUNK

    @pl.when(pl.program_id(0) == 0)
    def _():
        adj_ref[...] = adj_in[...]
        head_ref[...] = head_in[...]
        taps_grad_ref[...] = taps_grad_in[...]
        bias_grad_ref[...] = bias_grad_in[...]
        gain_grad_ref[...] = gain_grad_in[...]

    row, col, lower_eq, strict, pair, levels = chunk_masks()
    tri = (row[:CHUNK, :CHUNK] >= col[:CHUNK, :CHUNK]).astype(jnp.float32)
    tri_t = (row[:CHUNK, :CHUNK] <= col[:CHUNK, :CHUNK]).astype(jnp.float32)
    lanes = col[:CHUNK, :]
    rates = raw_ref[:, 6 * heads * width :]
    beta_tile = jax.nn.sigmoid(rates)
    keep_in = rates + bias_ref[...]
    log_tile = -softplus(keep_in)
    units = [(part, head) for part in reversed(range(per_step)) for head in range(heads)]
    spans = [slice(part * CHUNK, (part + 1) * CHUNK) for part in range(per_step)]
    cumuls = [mm(tri, log_tile[rows], NN, EXACT) for rows in spans]
    cumul_ts = [twice(cumul).T for cumul in cumuls]
    sames = [
        (twice(aux_ref[rows, 8:9]) == segrow_ref[part]) & lower_eq
        for part, rows in enumerate(spans)
    ]
    gain_total = jnp.zeros((1, width), jnp.float32)
    out_grads = []
    for part, head in units:
        rows = spans[part]
        q0, g0 = unit_slices(heads, head)[4:]
        recall = recall_ref[rows, q0]
        grad = grad_ref[rows, q0].astype(jnp.float32)
        gate = raw_ref[rows, g0]
        gate_sig = jax.nn.sigmoid(gate)
        silu_gate = gate * gate_sig
        scale = lax.rsqrt(jnp.mean(recall * recall, axis=-1, keepdims=True) + EPS)
        normed = recall * scale
        gain_total = gain_total + jnp.sum(grad * normed * silu_gate, axis=0, keepdims=True)
        weighted = grad * gain_ref[...]
        low_ref[rows, g0] = (
            weighted * normed * gate_sig * (1.0 + gate * (1.0 - gate_sig))
        ).astype(jnp.bfloat16)
        normed_grad = weighted * silu_gate
        out_grads.append(
            scale * (normed_grad - normed * jnp.mean(normed_grad * normed, axis=-1, keepdims=True))
        )
    gain_grad_ref[...] += gain_total
    reads = [
        mm(probe_ref[part * heads + head], out_grads[u], TN) for u, (part, head) in enumerate(units)
    ]
    for u, (part, head) in enumerate(units):
        spot = part * heads + head
        c_end = cumuls[part][CHUNK - 1 :, 3 * head + 2 : 3 * head + 3]
        total = aux_ref[(part + 1) * CHUNK - 1 : (part + 1) * CHUNK, 0:1] * jnp.exp(c_end)
        adjoint = adj_ref[head]
        keep_ref[spot] = adjoint
        adj_ref[head] = total * adjoint + reads[u] - mm(move_ref[spot], adjoint, TN)
    for tile in range(5 * heads):
        cols = slice(tile * width, (tile + 1) * width)
        pre = pre_ref[:, cols]
        act = pre * jax.nn.sigmoid(pre)
        if tile < 3 * heads:
            scale = lax.rsqrt(col_sum(act * act) + EPS)
            norm_ref[:, cols] = jnp.broadcast_to(scale, act.shape)
            act = act * scale
        act_ref[:, cols] = act
    keys, decays, dots = [], [], []
    for u, (part, head) in enumerate(units):
        k1, k2, v1, v2, q0, g0 = unit_slices(heads, head)
        rows = spans[part]
        key = jnp.concatenate([act_ref[rows, k1], act_ref[rows, k2]], axis=0)
        keys.append(key)
        decays.append(
            decays_of(
                cumuls[part], cumul_ts[part], beta_tile[rows], aux_ref[rows], sames[part], 3 * head
            )
        )
        dots.append(mm(jnp.concatenate([key, act_ref[rows, q0]], axis=0), key, NT))
    scores = [decays[u][0][CHUNK:] * dots[u][ROWS:] for u in range(len(units))]
    proxy_grads = [
        mm(scores[u], out_grads[u], TN)
        + mm(decays[u][3] * keys[u], keep_ref[part * heads + head])
        for u, (part, head) in enumerate(units)
    ]
    both_grads = [
        jnp.concatenate(
            [mm(inv_ref[part * heads + head], proxy_grads[u], TN), out_grads[u]], axis=0
        )
        for u, (part, head) in enumerate(units)
    ]
    outers = [
        mm(both_grads[u], prox_ref[part * heads + head], NT)
        for u, (part, head) in enumerate(units)
    ]
    throughs = [
        mm(both_grads[u], state_ref[part * heads + head], NT)
        for u, (part, head) in enumerate(units)
    ]
    finals = [
        decays[u][3] * mm(prox_ref[part * heads + head], keep_ref[part * heads + head], NT)
        for u, (part, head) in enumerate(units)
    ]
    score_grads, inners, beta_parts, log_cols = [], [], [], []
    for u, (part, head) in enumerate(units):
        decay, beta, start, final, total = decays[u]
        key_decay = jnp.where(strict, decay * dots[u][:ROWS], 0.0)
        lower_grad = -outers[u][:ROWS]
        beta_part = lower_grad * key_decay
        dots_grad = jnp.where(strict, lower_grad * beta * decay, 0.0)
        score_grad = outers[u][ROWS:] * decay[CHUNK:]
        log_part = beta_part * beta
        log_part = jnp.concatenate(
            [log_part[:CHUNK], log_part[CHUNK:] + outers[u][ROWS:] * scores[u]], axis=0
        )
        log_cols.append(col_sum(log_part - log_part.T))
        beta_parts.append(col_sum(beta_part))
        score_grads.append(score_grad)
        inners.append(
            mm(jnp.concatenate([dots_grad + dots_grad.T, score_grad], axis=0), keys[u])
        )
    zero = jnp.zeros((CHUNK, width), jnp.float32)
    beta_grads, cumul_grads, end_grads = [zero] * per_step, [zero] * per_step, [zero] * per_step
    for u, (part, head) in enumerate(units):
        k1, k2, v1, v2, q0, g0 = unit_slices(heads, head)
        rows = spans[part]
        spot = part * heads + head
        lane = 3 * head
        decay, beta, start, final, total = decays[u]
        through, final_part, right_grad = throughs[u], finals[u], both_grads[u][:ROWS]
        query = act_ref[rows, q0]
        value = jnp.concatenate([act_ref[rows, v1], act_ref[rows, v2]], axis=0)
        beta_start = beta * twice(start)
        key_through = col_sum(keys[u] * through[:ROWS])
        query_through = start * col_sum(query * through[ROWS:])
        final_sum = col_sum(keys[u] * final_part)
        key_grad = (
            inners[u][:ROWS]
            + mm(score_grads[u], query, TN)
            - beta_start * through[:ROWS]
            + final_part
        )
        dact_ref[rows, k1] = key_grad[:CHUNK]
        dact_ref[rows, k2] = key_grad[CHUNK:]
        value_grad = beta * right_grad
        dact_ref[rows, v1] = value_grad[:CHUNK]
        dact_ref[rows, v2] = value_grad[CHUNK:]
        dact_ref[rows, q0] = inners[u][ROWS:] + start * through[ROWS:]
        beta_col = col_sum(right_grad * value) - twice(start) * key_through + beta_parts[u]
        c_grad = log_cols[u] - beta_start * key_through - final_sum
        c_grad = c_grad[:CHUNK] + c_grad[CHUNK:] + query_through
        end_part = jnp.sum(final_sum, axis=0, keepdims=True) + total * jnp.sum(
            col_sum(state_ref[spot] * keep_ref[spot]), axis=0, keepdims=True
        )
        beta_grads[part] = jnp.where(
            lanes == lane,
            beta_col[:CHUNK],
            jnp.where(lanes == lane + 1, beta_col[CHUNK:], beta_grads[part]),
        )
        cumul_grads[part] = jnp.where(lanes == lane + 2, c_grad, cumul_grads[part])
        end_grads[part] = jnp.where(lanes == lane + 2, end_part, end_grads[part])
    bias_total = jnp.zeros((1, width), jnp.float32)
    for part, rows in enumerate(spans):
        log_grad = mm(tri_t, cumul_grads[part], NN, EXACT) + end_grads[part]
        beta_rows = beta_tile[rows]
        keep_grad = -log_grad * jax.nn.sigmoid(keep_in[rows]) * aux_ref[rows, 2:3]
        rate_grad = beta_grads[part] * beta_rows * (1.0 - beta_rows) + keep_grad
        bias_total = bias_total + jnp.sum(keep_grad, axis=0, keepdims=True)
        low_ref[rows, 6 * heads * width :] = rate_grad.astype(jnp.bfloat16)
    bias_grad_ref[...] += bias_total

    masks = [aux_ref[:, 5 + s : 6 + s] for s in range(3)]
    for tile in range(5 * heads):
        cols = slice(tile * width, (tile + 1) * width)
        pre = pre_ref[:, cols]
        sig = jax.nn.sigmoid(pre)
        grad = dact_ref[:, cols]
        if tile < 3 * heads:
            act = act_ref[:, cols]
            grad = norm_ref[:, cols] * (grad - act * col_sum(grad * act))
        grad = grad * sig * (1.0 + pre * (1.0 - sig))
        raw = raw_ref[:, cols]
        joined = jnp.concatenate([grad, head_ref[:, cols]], axis=0)
        head_ref[:, cols] = grad[:8]
        raw_grad = grad * taps_ref[0:1, cols]
        taps_grad_ref[0:1, cols] += jnp.sum(raw * grad, axis=0, keepdims=True)
        for s in range(1, 4):
            shifted = pltpu.roll(joined, block + 8 - s, 0)[:block] * masks[s - 1]
            raw_grad = raw_grad + shifted * taps_ref[s : s + 1, cols]
            taps_grad_ref[s : s + 1, cols] += jnp.sum(raw * shifted, axis=0, keepdims=True)
        low_ref[:, cols] = raw_grad.astype(jnp.bfloat16)


def token_aux(segments):
    length = segments.shape[0]
    seg = segments.astype(jnp.int32)
    chunks = seg.reshape(length // CHUNK, CHUNK)
    last = chunks[:, -1]
    before = jnp.concatenate([jnp.full((1,), -1, jnp.int32), last[:-1]])
    columns = [
        (chunks == before[:, None]).reshape(length),
        (chunks == last[:, None]).reshape(length),
    ]
    for s in range(1, 4):
        columns.append(jnp.pad(seg, (s, 0), constant_values=-1)[:length] == seg)
    for s in range(1, 4):
        columns.append(jnp.pad(seg, (0, s), constant_values=-1)[s:] == seg)
    columns.append(seg)
    columns += [jnp.zeros_like(seg)] * 7
    aux = jnp.stack([c.astype(jnp.float32) for c in columns], axis=1)
    row = chunks.astype(jnp.float32)
    return aux, jnp.concatenate([row, row], axis=1)[:, None, :]


def kernel_params():
    return pltpu.CompilerParams(
        dimension_semantics=("arbitrary",), vmem_limit_bytes=48 * 1024 * 1024
    )


def whole(shape):
    zeros = (0,) * len(shape)
    return pl.BlockSpec(shape, lambda i: zeros)


def mixer_forward(raw, aux, segrow, taps, bias, gain, carry, heads, per_step, part, parts):
    width = HEAD_DIM
    block = per_step * CHUNK
    length = raw.shape[0] // parts
    steps = length // block
    first = part * steps
    units = per_step * heads
    total_units = steps * units
    cols = raw.shape[1]
    f32 = jnp.float32
    if carry is None:
        carry = (jnp.zeros((heads, width, width), f32), jnp.zeros((8, 5 * heads * width), f32))
    memory, tail = carry
    read = lambda i: (first + i, 0)
    read_cube = lambda i: (first + i, 0, 0)
    tiles = lambda i: (i, 0)
    cubes = lambda i: (i, 0, 0)
    unit_spec = pl.BlockSpec((units, ROWS, width), cubes)
    unit_shape = pltpu.HBM((total_units, ROWS, width), f32)
    out = pl.pallas_call(
        partial(fwd_kernel, heads, per_step),
        grid=(steps,),
        in_specs=[
            pl.BlockSpec((block, cols), read),
            pl.BlockSpec((block, 16), read),
            pl.BlockSpec((per_step, 1, ROWS), read_cube),
            whole(taps.shape),
            whole((1, width)),
            whole((1, width)),
            whole(memory.shape),
            whole(tail.shape),
        ],
        out_specs=[
            pl.BlockSpec((block, heads * width), tiles),
            pl.BlockSpec((block, 5 * heads * width), tiles),
            pl.BlockSpec((block, heads * width), tiles),
            unit_spec,
            unit_spec,
            unit_spec,
            unit_spec,
            pl.BlockSpec((units, CHUNK, width), cubes),
            whole(memory.shape),
            whole(tail.shape),
        ],
        out_shape=[
            jax.ShapeDtypeStruct((length, heads * width), jnp.bfloat16),
            pltpu.HBM((length, 5 * heads * width), f32),
            pltpu.HBM((length, heads * width), f32),
            unit_shape,
            unit_shape,
            unit_shape,
            unit_shape,
            pltpu.HBM((total_units, CHUNK, width), f32),
            jax.ShapeDtypeStruct(memory.shape, f32),
            jax.ShapeDtypeStruct(tail.shape, f32),
        ],
        scratch_shapes=[pltpu.VMEM((block, 5 * heads * width), f32)],
        compiler_params=kernel_params(),
        name="mixer_forward",
    )(raw, aux, segrow, taps, bias, gain, memory, tail)
    return out[0], out[1:8], (out[8], out[9])


def mixer_backward(grad, raw, aux, segrow, saved, taps, bias, gain, carry, heads, per_step, part, parts):
    width = HEAD_DIM
    block = per_step * CHUNK
    length = raw.shape[0] // parts
    steps = length // block
    last = (part + 1) * steps - 1
    units = per_step * heads
    cols = raw.shape[1]
    f32 = jnp.float32
    shapes = [
        (heads, width, width),
        (8, 5 * heads * width),
        taps.shape,
        (1, width),
        (1, width),
    ]
    low_shape = jax.ShapeDtypeStruct(raw.shape, jnp.bfloat16)
    if carry is None:
        carry = [jnp.zeros(shape, f32) for shape in shapes] + [jnp.zeros((16, width), jnp.bfloat16)]
        aliases = {}
    else:
        aliases = {19: 0}
    read = lambda i: (last - i, 0)
    read_cube = lambda i: (last - i, 0, 0)
    tiles = lambda i: (steps - 1 - i, 0)
    cubes = lambda i: (steps - 1 - i, 0, 0)
    unit_spec = pl.BlockSpec((units, ROWS, width), cubes)
    out = pl.pallas_call(
        partial(bwd_kernel, heads, per_step),
        grid=(steps,),
        in_specs=[
            pl.BlockSpec((block, heads * width), read),
            pl.BlockSpec((block, cols), read),
            pl.BlockSpec((block, 16), read),
            pl.BlockSpec((per_step, 1, ROWS), read_cube),
            pl.BlockSpec((block, 5 * heads * width), tiles),
            pl.BlockSpec((block, heads * width), tiles),
            unit_spec,
            unit_spec,
            unit_spec,
            unit_spec,
            pl.BlockSpec((units, CHUNK, width), cubes),
            whole(taps.shape),
            whole((1, width)),
            whole((1, width)),
        ]
        + [whole(shape) for shape in shapes]
        + [pl.BlockSpec(memory_space=pl.ANY)],
        out_specs=[
            pl.BlockSpec((block, cols), read),
            whole(taps.shape),
            whole((1, width)),
            whole((1, width)),
            whole(shapes[0]),
            whole(shapes[1]),
        ],
        out_shape=[
            low_shape,
            jax.ShapeDtypeStruct(taps.shape, f32),
            jax.ShapeDtypeStruct((1, width), f32),
            jax.ShapeDtypeStruct((1, width), f32),
            jax.ShapeDtypeStruct(shapes[0], f32),
            jax.ShapeDtypeStruct(shapes[1], f32),
        ],
        scratch_shapes=[
            pltpu.VMEM((block, 5 * heads * width), f32),
            pltpu.VMEM((block, 3 * heads * width), f32),
            pltpu.VMEM((block, 5 * heads * width), f32),
            pltpu.VMEM((units, width, width), f32),
        ],
        input_output_aliases=aliases,
        compiler_params=kernel_params(),
        name="mixer_backward",
    )(grad, raw, aux, segrow, *saved, taps, bias, gain, *carry)
    low, taps_grad, bias_grad, gain_grad, adjoint, head = out
    return [adjoint, head, taps_grad, bias_grad, gain_grad, low]


def up_to(x, multiple):
    return -(-x // multiple) * multiple


def row_scale(values):
    return lax.rsqrt(jnp.mean(values * values, axis=-1, keepdims=True) + EPS)


def norm_back(grad, values, scale, gain):
    normed = values * scale
    gain_grad = jnp.sum(grad * normed, axis=0)
    weighted = grad * gain
    value_grad = scale * (weighted - normed * jnp.mean(weighted * normed, axis=-1, keepdims=True))
    return (value_grad, gain_grad)


def dot(left, right, dims=NN):
    return lax.dot_general(left, right, (dims, ((), ())), preferred_element_type=jnp.float32)


def swap(x, axis, bit):
    size = lax.axis_size(axis)
    return lax.ppermute(x, axis, [(i, i ^ bit) for i in range(size)])


def share(x, axis):
    size = lax.axis_size(axis)
    copies = jnp.broadcast_to(x[None], (size,) + x.shape)
    return lax.all_to_all(copies, axis, split_axis=0, concat_axis=0, tiled=True)


def trade(blocks, axis):
    return lax.all_to_all(blocks, axis, split_axis=0, concat_axis=0, tiled=True)


def total_of(blocks):
    return jnp.sum(blocks.astype(jnp.float32), axis=0)


def bits_of(size):
    return [1 << b for b in range(size.bit_length() - 1)]


def plane_scatter(left, right, axis):
    size = lax.axis_size(axis)
    index = lax.axis_index(axis)
    core, chip = index % 2, index // 2
    width = left.shape[1] // size
    even = jnp.concatenate(
        [left[:, j * width : (j + 1) * width] for j in range(0, size, 2)], axis=1
    )
    odd = jnp.concatenate([left[:, j * width : (j + 1) * width] for j in range(1, size, 2)], axis=1)
    got = swap(dot(jnp.where(core == 0, odd, even), right, TN).astype(jnp.bfloat16), axis, 1)
    held = dot(jnp.where(core == 0, even, odd), right, TN) + got.astype(jnp.float32)
    held = held.astype(jnp.bfloat16)

    def block(j):
        return lax.dynamic_slice_in_dim(held, j * width, width, axis=0)

    total = block(chip).astype(jnp.float32)
    for step in range(1, size // 2):
        total = total + swap(block(chip ^ step), axis, 2 * step).astype(jnp.float32)
    return total


def body(
    layer_input,
    cotangent,
    segments,
    mix_gain,
    query_weight,
    key_weight,
    value_weight,
    outgate_weight,
    rate_weight,
    conv_query,
    conv_key,
    conv_value,
    decay_bias,
    out_gain,
    out_weight,
    mlp_gain,
    gate_weight,
    up_weight,
    down_weight,
):
    f32, bf16 = jnp.float32, jnp.bfloat16
    head_index = lax.axis_index("head")
    n_head, n_batch = lax.axis_size("head"), lax.axis_size("batch")
    rows, width = layer_input.shape
    length = rows * n_head
    local_heads = query_weight.shape[1] // HEAD_DIM
    unit = local_heads * HEAD_DIM
    mix_cols = 6 * unit + HEAD_DIM
    ff = gate_weight.shape[1]
    ff_pad = up_to(ff, LANE)

    copies = jnp.broadcast_to(layer_input[None], (n_head,) + layer_input.shape)
    copies, query_weight, key_weight, value_weight, outgate_weight = lax.optimization_barrier(
        (copies, query_weight, key_weight, value_weight, outgate_weight)
    )
    tokens = trade(copies, "head")
    own_mix = jnp.concatenate(
        [
            query_weight,
            key_weight,
            value_weight,
            outgate_weight,
            jnp.pad(rate_weight, ((0, 0), (0, HEAD_DIM - rate_weight.shape[1]))),
        ],
        axis=1,
    )
    proj_w = lax.all_gather(own_mix, "batch", axis=0, tiled=True)

    pad = ((0, 0), (0, ff_pad - ff))
    own_ff = jnp.concatenate(
        [jnp.pad(gate_weight, pad), jnp.pad(up_weight, pad), jnp.pad(down_weight.T, pad)], axis=1
    )
    ff_sets = [lax.all_gather(own_ff, "batch", axis=0, tiled=True)]
    tokens, later_ff, later_out, later_cot = lax.optimization_barrier(
        (tokens, own_ff, out_weight.T, cotangent)
    )
    out_shards = jnp.stack([later_out] + [swap(later_out, "head", j) for j in range(1, n_head)])
    out_shards = [
        lax.dynamic_index_in_dim(out_shards, head_index ^ j, 0, keepdims=False)
        for j in range(n_head)
    ]
    shards = [later_ff]
    for bit in bits_of(n_head)[1:]:
        shards = shards + [swap(shard, "head", bit) for shard in shards]
    pair_grad = swap(later_cot, "head", 1)

    all_in = tokens.reshape(length, width).astype(f32)
    scale_all = row_scale(all_in)
    rows_in = (all_in * scale_all * mix_gain).astype(bf16)
    rows_in, out_shards = lax.optimization_barrier((rows_in, out_shards))
    out_all = lax.all_gather(
        jnp.concatenate(out_shards, axis=1), "batch", axis=0, tiled=True
    )
    raw, ff_sets[0] = lax.optimization_barrier((dot(rows_in, proj_w), ff_sets[0]))

    def head_cols(table, per_head):
        return lax.dynamic_slice_in_dim(
            table, head_index * local_heads * per_head, local_heads * per_head, axis=table.ndim - 1
        )

    taps = jnp.concatenate(
        [
            head_cols(conv_query, HEAD_DIM),
            head_cols(conv_key, 2 * HEAD_DIM),
            head_cols(conv_value, 2 * HEAD_DIM),
        ],
        axis=1,
    )
    own_bias = head_cols(decay_bias, 1)
    bias = jnp.stack([jnp.zeros_like(own_bias), jnp.zeros_like(own_bias), own_bias], axis=1)
    bias = jnp.pad(bias.reshape(-1), (0, HEAD_DIM - 3 * local_heads))[None]
    aux, segrow = token_aux(segments)
    gain = out_gain[None]
    consts = (raw, aux, segrow, taps, bias, gain)
    carry, mixed_parts, saved = None, [], []
    for part in range(SPANS):
        if part == SPANS - 1:
            carry, shards = lax.optimization_barrier((carry, shards))
        mixed_part, kept, carry = mixer_forward(*consts, carry, local_heads, FWD_CHUNKS, part, SPANS)
        mixed_parts.append(mixed_part)
        saved.append(kept)
    mixed_parts, pair_grad = lax.optimization_barrier((mixed_parts, pair_grad))
    mixed_low = jnp.concatenate(mixed_parts, axis=0)
    ff_sets += [lax.all_gather(shard, "batch", axis=0, tiled=True) for shard in shards[1:]]

    mixed_all = trade(mixed_low.reshape(n_head, rows, unit), "head")
    mixed_all = jnp.concatenate([mixed_all[j] for j in range(n_head)], axis=1)
    resid_in = layer_input.astype(f32)
    resid_mid = resid_in + dot(mixed_all, out_all, NT)
    scale_mid = row_scale(resid_mid)
    normed_mid = (resid_mid * scale_mid * mlp_gain).astype(bf16)
    pair_mid = swap(normed_mid, "head", 1)

    def feed_forward(mid, cot):
        mid_part = None
        grads = []
        for ff_set in ff_sets:
            gate_up = dot(mid, ff_set[:, : 2 * ff_pad])
            gate_pre, up_pre = gate_up[:, :ff_pad], gate_up[:, ff_pad:]
            gate_sig = jax.nn.sigmoid(gate_pre)
            silu_gate = gate_pre * gate_sig
            hidden = (silu_gate * up_pre).astype(bf16)
            hidden_grad = dot(cot, ff_set[:, 2 * ff_pad : 3 * ff_pad])
            gate_grad = (
                hidden_grad * up_pre * gate_sig * (1.0 + gate_pre * (1.0 - gate_sig))
            ).astype(bf16)
            up_grad = (hidden_grad * silu_gate).astype(bf16)
            both_grad = jnp.concatenate([gate_grad, up_grad], axis=1)
            mid_here = dot(both_grad, ff_set[:, : 2 * ff_pad], NT)
            mid_part = mid_here if mid_part is None else mid_part + mid_here
            grads.append((both_grad, hidden))
        return mid_part, grads

    mid_own, grads_own = feed_forward(normed_mid, cotangent)
    mid_pair, grads_pair = feed_forward(pair_mid, pair_grad)
    both_mid = jnp.concatenate([normed_mid, pair_mid], axis=0)
    both_cot = jnp.concatenate([cotangent, pair_grad], axis=0)
    ff_parts = [
        [
            dot(both_mid, jnp.concatenate([both, pair_both], axis=0), TN),
            dot(both_cot, jnp.concatenate([hidden, pair_hidden], axis=0), TN),
        ]
        for (both, hidden), (pair_both, pair_hidden) in zip(grads_own, grads_pair)
    ]
    ff_parts = [jnp.concatenate(parts, axis=1).astype(bf16) for parts in reversed(ff_parts)]
    mid_swap, ff_parts[0] = lax.optimization_barrier(
        (swap(mid_pair.astype(bf16), "head", 1), ff_parts[0])
    )
    mid_grad = mid_own + mid_swap.astype(f32)
    mid_back, mlp_gain_part = norm_back(mid_grad, resid_mid, scale_mid, mlp_gain)
    resid_grad = cotangent.astype(f32) + mid_back
    branch_grad = resid_grad.astype(bf16)
    mixed_grad = dot(branch_grad, out_all).astype(bf16)
    mixed_grad = jnp.stack([mixed_grad[:, j * unit : (j + 1) * unit] for j in range(n_head)])
    mixed_grad = trade(mixed_grad, "head").reshape(length, unit)
    ff_parts[-1] = jnp.concatenate(
        [ff_parts[-1], dot(branch_grad.T, mixed_all).astype(bf16)], axis=1
    )
    ff_sums = [
        lax.psum_scatter(part, "batch", scatter_dimension=0, tiled=True) for part in ff_parts
    ]
    half = len(ff_sums) // 2
    downs = [ff_set[:, 2 * ff_pad : 3 * ff_pad] for ff_set in ff_sets]
    out_pair = sum(dot(hidden, down, NT) for (_, hidden), down in zip(grads_pair, downs))
    out_swap = swap(out_pair.astype(bf16), "head", 1)
    mixed_grad, _ = lax.optimization_barrier((mixed_grad, ff_parts))

    carry, ff_first = None, ff_sums[:half]
    for part in reversed(range(SPANS)):
        if part == 0:
            carry, ff_first = lax.optimization_barrier((carry, ff_first))
        carry = mixer_backward(
            mixed_grad, raw, aux, segrow, saved[part], taps, bias, gain, carry,
            local_heads, BWD_CHUNKS, part, SPANS,
        )
    _, _, taps_grad, bias_grad, gain_grad, raw_low = carry
    raw_low, out_swap, *sent = lax.optimization_barrier(
        (raw_low, out_swap, *[swap(part, "head", bits_of(n_head)[-1]) for part in ff_first])
    )
    total = dot(raw_low, proj_w, NT)
    received = trade(total.astype(bf16).reshape(n_head, rows, width), "head")
    in_grad = total_of(received)
    mix_gain_part = jnp.sum(total * (all_in * scale_all), axis=0)
    mix_total = plane_scatter(rows_in, raw_low, "batch")
    in_back, _ = norm_back(in_grad, resid_in, row_scale(resid_in), mix_gain)
    input_grad = resid_grad + in_back

    hiddens, _ = lax.optimization_barrier(([hidden for _, hidden in grads_own], raw_low))
    out_own = sum(dot(own, down, NT) for own, down in zip(hiddens, downs))
    layer_output = (resid_mid + out_own + out_swap.astype(f32)).astype(bf16)
    ff_kept, mix_total = lax.optimization_barrier((ff_sums[half:], mix_total))
    out_sum = ff_kept[-1][:, 3 * ff_pad :]
    ff_kept[-1] = ff_kept[-1][:, : 3 * ff_pad]
    out_blocks = jnp.stack([out_sum[:, j * unit : (j + 1) * unit] for j in range(n_head)])
    out_total = lax.dynamic_index_in_dim(out_blocks, head_index, 0, keepdims=False).astype(f32)
    for step in range(1, n_head):
        part = lax.dynamic_index_in_dim(out_blocks, head_index ^ step, 0, keepdims=False)
        out_total = out_total + swap(part, "head", step).astype(f32)
    ff_total = [got.astype(f32) + kept.astype(f32) for got, kept in zip(sent, ff_kept)]
    for bit in reversed(bits_of(n_head)[1:-1]):
        half = len(ff_total) // 2
        ff_total = [
            kept + swap(part.astype(bf16), "head", bit).astype(f32)
            for part, kept in zip(ff_total[:half], ff_total[half:])
        ]
    ff_total = ff_total[0]

    own_bias_grad = bias_grad[0, : 3 * local_heads].reshape(local_heads, 3)[:, 2]
    small = [
        taps_grad[:, :unit].reshape(-1),
        taps_grad[:, unit : 3 * unit].reshape(-1),
        taps_grad[:, 3 * unit :].reshape(-1),
        own_bias_grad,
        gain_grad[0],
        mlp_gain_part,
        mix_gain_part,
    ]
    lengths = [part.shape[0] for part in small]
    packed = pack(small)
    for bit in bits_of(n_batch):
        packed = packed + swap(packed, "batch", bit)
    small = unpack(packed, lengths)

    def place_cols(table_shape, local_part, per_head):
        local_part = local_part.reshape(table_shape[:-1] + (-1,))
        return lax.dynamic_update_slice_in_dim(
            jnp.zeros(table_shape, f32),
            local_part,
            head_index * local_heads * per_head,
            axis=len(table_shape) - 1,
        ).reshape(-1)

    tables = [
        place_cols(conv_query.shape, small[0], HEAD_DIM),
        place_cols(conv_key.shape, small[1], 2 * HEAD_DIM),
        place_cols(conv_value.shape, small[2], 2 * HEAD_DIM),
        place_cols(decay_bias.shape, small[3], 1),
    ] + small[4:]
    lengths = [part.shape[0] for part in tables]
    packed, *_ = lax.optimization_barrier((pack(tables), received))
    for bit in bits_of(n_head):
        packed = packed + swap(packed, "head", bit)
    tables = unpack(packed, lengths)
    return (
        layer_output,
        input_grad,
        tables[6],
        mix_total[:, :unit],
        mix_total[:, unit : 3 * unit],
        mix_total[:, 3 * unit : 5 * unit],
        mix_total[:, 5 * unit : 6 * unit],
        mix_total[:, 6 * unit : 6 * unit + rate_weight.shape[1]],
        tables[0].reshape(conv_query.shape),
        tables[1].reshape(conv_key.shape),
        tables[2].reshape(conv_value.shape),
        tables[3],
        tables[4],
        out_total.T,
        tables[5],
        ff_total[:, :ff],
        ff_total[:, ff_pad : ff_pad + ff],
        ff_total[:, 2 * ff_pad : 2 * ff_pad + ff].T,
    )


def pack(parts):
    flat = jnp.concatenate(parts)
    return jnp.pad(flat, (0, -flat.shape[0] % (8 * LANE))).reshape(-1, LANE)


def unpack(packed, lengths):
    flat = packed.reshape(-1)
    out, at = [], 0
    for size in lengths:
        out.append(flat[at : at + size])
        at += size
    return out


def solution(mesh):
    placed = (
        P(("batch", "head"), None),
        P(("batch", "head"), None),
        P("batch"),
        P(),
        P("batch", "head"),
        P("batch", "head"),
        P("batch", "head"),
        P("batch", "head"),
        P("batch", "head"),
        P(),
        P(),
        P(),
        P(),
        P(),
        P("head", "batch"),
        P(),
        P("batch", "head"),
        P("batch", "head"),
        P("head", "batch"),
    )
    return jax.shard_map(
        body,
        mesh=mesh,
        in_specs=placed,
        out_specs=(
            P(("batch", "head"), None),
            P(("batch", "head"), None),
            P(),
            P("batch", "head"),
            P("batch", "head"),
            P("batch", "head"),
            P("batch", "head"),
            P("batch", "head"),
            P(),
            P(),
            P(),
            P(),
            P(),
            P("head", "batch"),
            P(),
            P("batch", "head"),
            P("batch", "head"),
            P("head", "batch"),
        ),
        check_vma=False,
    )
```

```python
from functools import partial

import jax
import jax.numpy as jnp
from jax import lax
from jax.experimental import pallas as pl
from jax.experimental.pallas import tpu as pltpu
from jax.sharding import PartitionSpec as P

HEAD_DIM = 128
EPS = 1e-06
EXACT = lax.Precision.HIGHEST
HIGH = lax.Precision.HIGH
FAST = lax.Precision.DEFAULT
NN = ((1,), (0,))
NT = ((1,), (1,))
TN = ((0,), (0,))
LANE = 128
CHUNK = 64
ROWS = 2 * CHUNK
FWD_CHUNKS = 4
BWD_CHUNKS = 2
SPANS = 2


def mm(left, right, dims=NN, precision=HIGH):
    return lax.dot_general(
        left, right, (dims, ((), ())), precision=precision, preferred_element_type=jnp.float32
    )


def softplus(x):
    return jnp.maximum(x, 0.0) + jnp.log1p(jnp.exp(-jnp.abs(x)))


def chunk_masks():
    row = lax.broadcasted_iota(jnp.int32, (ROWS, ROWS), 0)
    col = lax.broadcasted_iota(jnp.int32, (ROWS, ROWS), 1)
    row_tok, col_tok = row & (CHUNK - 1), col & (CHUNK - 1)
    later = row_tok > col_tok
    same_tok = row_tok == col_tok
    pair = same_tok & (row > col)
    levels = []
    size = 1
    while size < CHUNK:
        upper = (row_tok & size) > (col_tok & size)
        together = (row_tok & (-2 * size)) == (col_tok & (-2 * size))
        levels.append(upper & together)
        size *= 2
    return row, col, later | same_tok, later | pair, pair, levels


def invert(lowers, ident, pair, levels, precision):
    inverses = [ident - jnp.where(pair, lower, 0.0) for lower in lowers]
    for level in levels:
        steps = [
            mm(jnp.where(level, lower, 0.0), inverse, NN, precision)
            for lower, inverse in zip(lowers, inverses)
        ]
        inverses = [
            inverse - mm(inverse, step, NN, precision) for inverse, step in zip(inverses, steps)
        ]
    return inverses


def col_sum(x):
    return jnp.sum(x, axis=-1, keepdims=True)


def twice(x):
    return jnp.concatenate([x, x], axis=0)


def unit_slices(heads, head):
    names = [heads + 2 * head, heads + 2 * head + 1, 3 * heads + 2 * head, 3 * heads + 2 * head + 1]
    names += [head, 5 * heads + head]
    return [slice(n * HEAD_DIM, (n + 1) * HEAD_DIM) for n in names]


def decays_of(cumul, cumul_t, beta_rows, aux, same, lane):
    c_tok = cumul[:, lane + 2 : lane + 3]
    c_end = cumul[CHUNK - 1 :, lane + 2 : lane + 3]
    decay = jnp.where(
        same, jnp.exp(jnp.minimum(twice(c_tok) - cumul_t[lane + 2 : lane + 3, :], 0.0)), 0.0
    )
    beta = jnp.concatenate(
        [beta_rows[:, lane : lane + 1], beta_rows[:, lane + 1 : lane + 2]], axis=0
    )
    start = aux[:, 0:1] * jnp.exp(c_tok)
    final = twice(aux[:, 1:2] * jnp.exp(c_end - c_tok))
    total = aux[CHUNK - 1 :, 0:1] * jnp.exp(c_end)
    return decay, beta, start, final, total


def fwd_kernel(
    heads, per_step, raw_ref, aux_ref, segrow_ref, taps_ref, bias_ref, gain_ref, mem_in, tail_in,
    mixed_ref, pre_ref, recall_ref, inv_ref, prox_ref, state_ref, move_ref, probe_ref,
    mem_ref, tail_ref, act_ref,
):
    width = HEAD_DIM
    block = per_step * CHUNK

    @pl.when(pl.program_id(0) == 0)
    def _():
        mem_ref[...] = mem_in[...]
        tail_ref[...] = tail_in[...]

    masks = [aux_ref[:, 2 + s : 3 + s] for s in range(3)]
    for tile in range(5 * heads):
        cols = slice(tile * width, (tile + 1) * width)
        raw = raw_ref[:, cols]
        joined = jnp.concatenate([tail_ref[:, cols], raw], axis=0)
        pre = raw * taps_ref[0:1, cols]
        for s in range(1, 4):
            shifted = pltpu.roll(joined, s, 0)[8:]
            pre = pre + shifted * masks[s - 1] * taps_ref[s : s + 1, cols]
        pre_ref[:, cols] = pre
        tail_ref[:, cols] = raw[block - 8 :]
        act = pre * jax.nn.sigmoid(pre)
        if tile < 3 * heads:
            act = act * lax.rsqrt(col_sum(act * act) + EPS)
        act_ref[:, cols] = act

    row, col, lower_eq, strict, pair, levels = chunk_masks()
    ident = (row == col).astype(jnp.float32)
    tri = (row[:CHUNK, :CHUNK] >= col[:CHUNK, :CHUNK]).astype(jnp.float32)
    rates = raw_ref[:, 6 * heads * width :]
    beta_tile = jax.nn.sigmoid(rates)
    log_tile = -softplus(rates + bias_ref[...])
    units = [(part, head) for part in range(per_step) for head in range(heads)]
    spans = [slice(part * CHUNK, (part + 1) * CHUNK) for part in range(per_step)]
    cumuls = [mm(tri, log_tile[rows], NN, EXACT) for rows in spans]
    cumul_ts = [twice(cumul).T for cumul in cumuls]
    sames = [
        (twice(aux_ref[rows, 8:9]) == segrow_ref[part]) & lower_eq
        for part, rows in enumerate(spans)
    ]
    keys, queries, decays, lowers, scores = [], [], [], [], []
    for part, head in units:
        k1, k2, v1, v2, q0, g0 = unit_slices(heads, head)
        rows = spans[part]
        key = jnp.concatenate([act_ref[rows, k1], act_ref[rows, k2]], axis=0)
        query = act_ref[rows, q0]
        decay = decays_of(
            cumuls[part], cumul_ts[part], beta_tile[rows], aux_ref[rows], sames[part], 3 * head
        )
        dots = mm(jnp.concatenate([key, query], axis=0), key, NT)
        keys.append(key)
        queries.append(query)
        decays.append(decay)
        lowers.append(jnp.where(strict, decay[1] * decay[0] * dots[:ROWS], 0.0))
        scores.append(decay[0][CHUNK:] * dots[ROWS:])
    inverses = invert(lowers, ident, pair, levels, HIGH)
    solved = []
    for u, (part, head) in enumerate(units):
        k1, k2, v1, v2, q0, g0 = unit_slices(heads, head)
        rows = spans[part]
        decay, beta, start, final, total = decays[u]
        inv_ref[u] = inverses[u]
        value = jnp.concatenate([act_ref[rows, v1], act_ref[rows, v2]], axis=0)
        solved.append(
            mm(
                inverses[u],
                jnp.concatenate([beta * value, beta * twice(start) * keys[u]], axis=1),
            )
        )
    moves = [mm(decays[u][3] * keys[u], solved[u], TN) for u in range(len(units))]
    reads = [mm(scores[u], solved[u]) for u in range(len(units))]
    for u, (part, head) in enumerate(units):
        memory = mem_ref[head]
        state_ref[u] = memory
        move_ref[u] = moves[u][:, width:]
        mem_ref[head] = (
            decays[u][4] * memory + moves[u][:, :width] - mm(moves[u][:, width:], memory)
        )
    for u, (part, head) in enumerate(units):
        probe = decays[u][2] * queries[u] - reads[u][:, width:]
        probe_ref[u] = probe
        seen = mm(jnp.concatenate([solved[u][:, width:], probe], axis=0), state_ref[u])
        prox_ref[u] = solved[u][:, :width] - seen[:ROWS]
        recall = reads[u][:, :width] + seen[ROWS:]
        rows = spans[part]
        cols = slice(head * width, (head + 1) * width)
        recall_ref[rows, cols] = recall
        scale = lax.rsqrt(jnp.mean(recall * recall, axis=-1, keepdims=True) + EPS)
        gate = raw_ref[rows, unit_slices(heads, head)[5]]
        mixed = recall * scale * gain_ref[...] * (gate * jax.nn.sigmoid(gate))
        mixed_ref[rows, cols] = mixed.astype(jnp.bfloat16)


def bwd_kernel(
    heads, per_step, grad_ref, raw_ref, aux_ref, segrow_ref, pre_ref, recall_ref, inv_ref,
    prox_ref, state_ref, move_ref, probe_ref, taps_ref, bias_ref, gain_ref,
    adj_in, head_in, taps_grad_in, bias_grad_in, gain_grad_in, low_in,
    low_ref, taps_grad_ref, bias_grad_ref, gain_grad_ref, adj_ref, head_ref,
    act_ref, norm_ref, dact_ref, keep_ref,
):
    width = HEAD_DIM
    block = per_step * CHUNK

    @pl.when(pl.program_id(0) == 0)
    def _():
        adj_ref[...] = adj_in[...]
        head_ref[...] = head_in[...]
        taps_grad_ref[...] = taps_grad_in[...]
        bias_grad_ref[...] = bias_grad_in[...]
        gain_grad_ref[...] = gain_grad_in[...]

    row, col, lower_eq, strict, pair, levels = chunk_masks()
    tri = (row[:CHUNK, :CHUNK] >= col[:CHUNK, :CHUNK]).astype(jnp.float32)
    tri_t = (row[:CHUNK, :CHUNK] <= col[:CHUNK, :CHUNK]).astype(jnp.float32)
    lanes = col[:CHUNK, :]
    rates = raw_ref[:, 6 * heads * width :]
    beta_tile = jax.nn.sigmoid(rates)
    keep_in = rates + bias_ref[...]
    log_tile = -softplus(keep_in)
    units = [(part, head) for part in reversed(range(per_step)) for head in range(heads)]
    spans = [slice(part * CHUNK, (part + 1) * CHUNK) for part in range(per_step)]
    cumuls = [mm(tri, log_tile[rows], NN, EXACT) for rows in spans]
    cumul_ts = [twice(cumul).T for cumul in cumuls]
    sames = [
        (twice(aux_ref[rows, 8:9]) == segrow_ref[part]) & lower_eq
        for part, rows in enumerate(spans)
    ]
    gain_total = jnp.zeros((1, width), jnp.float32)
    out_grads = []
    for part, head in units:
        rows = spans[part]
        q0, g0 = unit_slices(heads, head)[4:]
        recall = recall_ref[rows, q0]
        grad = grad_ref[rows, q0].astype(jnp.float32)
        gate = raw_ref[rows, g0]
        gate_sig = jax.nn.sigmoid(gate)
        silu_gate = gate * gate_sig
        scale = lax.rsqrt(jnp.mean(recall * recall, axis=-1, keepdims=True) + EPS)
        normed = recall * scale
        gain_total = gain_total + jnp.sum(grad * normed * silu_gate, axis=0, keepdims=True)
        weighted = grad * gain_ref[...]
        low_ref[rows, g0] = (
            weighted * normed * gate_sig * (1.0 + gate * (1.0 - gate_sig))
        ).astype(jnp.bfloat16)
        normed_grad = weighted * silu_gate
        out_grads.append(
            scale * (normed_grad - normed * jnp.mean(normed_grad * normed, axis=-1, keepdims=True))
        )
    gain_grad_ref[...] += gain_total
    reads = [
        mm(probe_ref[part * heads + head], out_grads[u], TN) for u, (part, head) in enumerate(units)
    ]
    for u, (part, head) in enumerate(units):
        spot = part * heads + head
        c_end = cumuls[part][CHUNK - 1 :, 3 * head + 2 : 3 * head + 3]
        total = aux_ref[(part + 1) * CHUNK - 1 : (part + 1) * CHUNK, 0:1] * jnp.exp(c_end)
        adjoint = adj_ref[head]
        keep_ref[spot] = adjoint
        adj_ref[head] = total * adjoint + reads[u] - mm(move_ref[spot], adjoint, TN)
    for tile in range(5 * heads):
        cols = slice(tile * width, (tile + 1) * width)
        pre = pre_ref[:, cols]
        act = pre * jax.nn.sigmoid(pre)
        if tile < 3 * heads:
            scale = lax.rsqrt(col_sum(act * act) + EPS)
            norm_ref[:, cols] = jnp.broadcast_to(scale, act.shape)
            act = act * scale
        act_ref[:, cols] = act
    keys, decays, dots = [], [], []
    for u, (part, head) in enumerate(units):
        k1, k2, v1, v2, q0, g0 = unit_slices(heads, head)
        rows = spans[part]
        key = jnp.concatenate([act_ref[rows, k1], act_ref[rows, k2]], axis=0)
        keys.append(key)
        decays.append(
            decays_of(
                cumuls[part], cumul_ts[part], beta_tile[rows], aux_ref[rows], sames[part], 3 * head
            )
        )
        dots.append(mm(jnp.concatenate([key, act_ref[rows, q0]], axis=0), key, NT))
    scores = [decays[u][0][CHUNK:] * dots[u][ROWS:] for u in range(len(units))]
    proxy_grads = [
        mm(scores[u], out_grads[u], TN)
        + mm(decays[u][3] * keys[u], keep_ref[part * heads + head])
        for u, (part, head) in enumerate(units)
    ]
    both_grads = [
        jnp.concatenate(
            [mm(inv_ref[part * heads + head], proxy_grads[u], TN), out_grads[u]], axis=0
        )
        for u, (part, head) in enumerate(units)
    ]
    outers = [
        mm(both_grads[u], prox_ref[part * heads + head], NT)
        for u, (part, head) in enumerate(units)
    ]
    throughs = [
        mm(both_grads[u], state_ref[part * heads + head], NT)
        for u, (part, head) in enumerate(units)
    ]
    finals = [
        decays[u][3] * mm(prox_ref[part * heads + head], keep_ref[part * heads + head], NT)
        for u, (part, head) in enumerate(units)
    ]
    score_grads, inners, beta_parts, log_cols = [], [], [], []
    for u, (part, head) in enumerate(units):
        decay, beta, start, final, total = decays[u]
        key_decay = jnp.where(strict, decay * dots[u][:ROWS], 0.0)
        lower_grad = -outers[u][:ROWS]
        beta_part = lower_grad * key_decay
        dots_grad = jnp.where(strict, lower_grad * beta * decay, 0.0)
        score_grad = outers[u][ROWS:] * decay[CHUNK:]
        log_part = beta_part * beta
        log_part = jnp.concatenate(
            [log_part[:CHUNK], log_part[CHUNK:] + outers[u][ROWS:] * scores[u]], axis=0
        )
        log_cols.append(col_sum(log_part - log_part.T))
        beta_parts.append(col_sum(beta_part))
        score_grads.append(score_grad)
        inners.append(
            mm(jnp.concatenate([dots_grad + dots_grad.T, score_grad], axis=0), keys[u])
        )
    zero = jnp.zeros((CHUNK, width), jnp.float32)
    beta_grads, cumul_grads, end_grads = [zero] * per_step, [zero] * per_step, [zero] * per_step
    for u, (part, head) in enumerate(units):
        k1, k2, v1, v2, q0, g0 = unit_slices(heads, head)
        rows = spans[part]
        spot = part * heads + head
        lane = 3 * head
        decay, beta, start, final, total = decays[u]
        through, final_part, right_grad = throughs[u], finals[u], both_grads[u][:ROWS]
        query = act_ref[rows, q0]
        value = jnp.concatenate([act_ref[rows, v1], act_ref[rows, v2]], axis=0)
        beta_start = beta * twice(start)
        key_through = col_sum(keys[u] * through[:ROWS])
        query_through = start * col_sum(query * through[ROWS:])
        final_sum = col_sum(keys[u] * final_part)
        key_grad = (
            inners[u][:ROWS]
            + mm(score_grads[u], query, TN)
            - beta_start * through[:ROWS]
            + final_part
        )
        dact_ref[rows, k1] = key_grad[:CHUNK]
        dact_ref[rows, k2] = key_grad[CHUNK:]
        value_grad = beta * right_grad
        dact_ref[rows, v1] = value_grad[:CHUNK]
        dact_ref[rows, v2] = value_grad[CHUNK:]
        dact_ref[rows, q0] = inners[u][ROWS:] + start * through[ROWS:]
        beta_col = col_sum(right_grad * value) - twice(start) * key_through + beta_parts[u]
        c_grad = log_cols[u] - beta_start * key_through - final_sum
        c_grad = c_grad[:CHUNK] + c_grad[CHUNK:] + query_through
        end_part = jnp.sum(final_sum, axis=0, keepdims=True) + total * jnp.sum(
            col_sum(state_ref[spot] * keep_ref[spot]), axis=0, keepdims=True
        )
        beta_grads[part] = jnp.where(
            lanes == lane,
            beta_col[:CHUNK],
            jnp.where(lanes == lane + 1, beta_col[CHUNK:], beta_grads[part]),
        )
        cumul_grads[part] = jnp.where(lanes == lane + 2, c_grad, cumul_grads[part])
        end_grads[part] = jnp.where(lanes == lane + 2, end_part, end_grads[part])
    bias_total = jnp.zeros((1, width), jnp.float32)
    for part, rows in enumerate(spans):
        log_grad = mm(tri_t, cumul_grads[part], NN, EXACT) + end_grads[part]
        beta_rows = beta_tile[rows]
        keep_grad = -log_grad * jax.nn.sigmoid(keep_in[rows]) * aux_ref[rows, 2:3]
        rate_grad = beta_grads[part] * beta_rows * (1.0 - beta_rows) + keep_grad
        bias_total = bias_total + jnp.sum(keep_grad, axis=0, keepdims=True)
        low_ref[rows, 6 * heads * width :] = rate_grad.astype(jnp.bfloat16)
    bias_grad_ref[...] += bias_total

    masks = [aux_ref[:, 5 + s : 6 + s] for s in range(3)]
    for tile in range(5 * heads):
        cols = slice(tile * width, (tile + 1) * width)
        pre = pre_ref[:, cols]
        sig = jax.nn.sigmoid(pre)
        grad = dact_ref[:, cols]
        if tile < 3 * heads:
            act = act_ref[:, cols]
            grad = norm_ref[:, cols] * (grad - act * col_sum(grad * act))
        grad = grad * sig * (1.0 + pre * (1.0 - sig))
        raw = raw_ref[:, cols]
        joined = jnp.concatenate([grad, head_ref[:, cols]], axis=0)
        head_ref[:, cols] = grad[:8]
        raw_grad = grad * taps_ref[0:1, cols]
        taps_grad_ref[0:1, cols] += jnp.sum(raw * grad, axis=0, keepdims=True)
        for s in range(1, 4):
            shifted = pltpu.roll(joined, block + 8 - s, 0)[:block] * masks[s - 1]
            raw_grad = raw_grad + shifted * taps_ref[s : s + 1, cols]
            taps_grad_ref[s : s + 1, cols] += jnp.sum(raw * shifted, axis=0, keepdims=True)
        low_ref[:, cols] = raw_grad.astype(jnp.bfloat16)


def token_aux(segments):
    length = segments.shape[0]
    seg = segments.astype(jnp.int32)
    chunks = seg.reshape(length // CHUNK, CHUNK)
    last = chunks[:, -1]
    before = jnp.concatenate([jnp.full((1,), -1, jnp.int32), last[:-1]])
    columns = [
        (chunks == before[:, None]).reshape(length),
        (chunks == last[:, None]).reshape(length),
    ]
    for s in range(1, 4):
        columns.append(jnp.pad(seg, (s, 0), constant_values=-1)[:length] == seg)
    for s in range(1, 4):
        columns.append(jnp.pad(seg, (0, s), constant_values=-1)[s:] == seg)
    columns.append(seg)
    columns += [jnp.zeros_like(seg)] * 7
    aux = jnp.stack([c.astype(jnp.float32) for c in columns], axis=1)
    row = chunks.astype(jnp.float32)
    return aux, jnp.concatenate([row, row], axis=1)[:, None, :]


def kernel_params():
    return pltpu.CompilerParams(
        dimension_semantics=("arbitrary",), vmem_limit_bytes=48 * 1024 * 1024
    )


def pin(array):
    return pltpu.with_memory_space_constraint(array, pltpu.HBM)


def whole(shape):
    zeros = (0,) * len(shape)
    return pl.BlockSpec(shape, lambda i: zeros)


def mixer_forward(raw, aux, segrow, taps, bias, gain, carry, heads, per_step, part, parts):
    width = HEAD_DIM
    block = per_step * CHUNK
    length = raw.shape[0] // parts
    steps = length // block
    first = part * steps
    units = per_step * heads
    total_units = steps * units
    cols = raw.shape[1]
    f32 = jnp.float32
    if carry is None:
        carry = (jnp.zeros((heads, width, width), f32), jnp.zeros((8, 5 * heads * width), f32))
    memory, tail = carry
    read = lambda i: (first + i, 0)
    read_cube = lambda i: (first + i, 0, 0)
    tiles = lambda i: (i, 0)
    cubes = lambda i: (i, 0, 0)
    unit_spec = pl.BlockSpec((units, ROWS, width), cubes)
    unit_shape = pltpu.HBM((total_units, ROWS, width), f32)
    out = pl.pallas_call(
        partial(fwd_kernel, heads, per_step),
        grid=(steps,),
        in_specs=[
            pl.BlockSpec((block, cols), read),
            pl.BlockSpec((block, 16), read),
            pl.BlockSpec((per_step, 1, ROWS), read_cube),
            whole(taps.shape),
            whole((1, width)),
            whole((1, width)),
            whole(memory.shape),
            whole(tail.shape),
        ],
        out_specs=[
            pl.BlockSpec((block, heads * width), tiles),
            pl.BlockSpec((block, 5 * heads * width), tiles),
            pl.BlockSpec((block, heads * width), tiles),
            unit_spec,
            unit_spec,
            unit_spec,
            unit_spec,
            pl.BlockSpec((units, CHUNK, width), cubes),
            whole(memory.shape),
            whole(tail.shape),
        ],
        out_shape=[
            jax.ShapeDtypeStruct((length, heads * width), jnp.bfloat16),
            pltpu.HBM((length, 5 * heads * width), f32),
            pltpu.HBM((length, heads * width), f32),
            unit_shape,
            unit_shape,
            unit_shape,
            unit_shape,
            pltpu.HBM((total_units, CHUNK, width), f32),
            jax.ShapeDtypeStruct(memory.shape, f32),
            jax.ShapeDtypeStruct(tail.shape, f32),
        ],
        scratch_shapes=[pltpu.VMEM((block, 5 * heads * width), f32)],
        compiler_params=kernel_params(),
        name="mixer_forward",
    )(raw, aux, segrow, taps, bias, gain, memory, tail)
    return out[0], out[1:8], (out[8], out[9])


def mixer_backward(grad, raw, aux, segrow, saved, taps, bias, gain, carry, heads, per_step, part, parts):
    width = HEAD_DIM
    block = per_step * CHUNK
    length = raw.shape[0] // parts
    steps = length // block
    last = (part + 1) * steps - 1
    units = per_step * heads
    cols = raw.shape[1]
    f32 = jnp.float32
    shapes = [
        (heads, width, width),
        (8, 5 * heads * width),
        taps.shape,
        (1, width),
        (1, width),
    ]
    low_shape = pltpu.HBM(raw.shape, jnp.bfloat16)
    if carry is None:
        carry = [jnp.zeros(shape, f32) for shape in shapes] + [jnp.zeros((16, width), jnp.bfloat16)]
        aliases = {}
    else:
        aliases = {19: 0}
    read = lambda i: (last - i, 0)
    read_cube = lambda i: (last - i, 0, 0)
    tiles = lambda i: (steps - 1 - i, 0)
    cubes = lambda i: (steps - 1 - i, 0, 0)
    unit_spec = pl.BlockSpec((units, ROWS, width), cubes)
    out = pl.pallas_call(
        partial(bwd_kernel, heads, per_step),
        grid=(steps,),
        in_specs=[
            pl.BlockSpec((block, heads * width), read),
            pl.BlockSpec((block, cols), read),
            pl.BlockSpec((block, 16), read),
            pl.BlockSpec((per_step, 1, ROWS), read_cube),
            pl.BlockSpec((block, 5 * heads * width), tiles),
            pl.BlockSpec((block, heads * width), tiles),
            unit_spec,
            unit_spec,
            unit_spec,
            unit_spec,
            pl.BlockSpec((units, CHUNK, width), cubes),
            whole(taps.shape),
            whole((1, width)),
            whole((1, width)),
        ]
        + [whole(shape) for shape in shapes]
        + [pl.BlockSpec(memory_space=pl.ANY)],
        out_specs=[
            pl.BlockSpec((block, cols), read),
            whole(taps.shape),
            whole((1, width)),
            whole((1, width)),
            whole(shapes[0]),
            whole(shapes[1]),
        ],
        out_shape=[
            low_shape,
            jax.ShapeDtypeStruct(taps.shape, f32),
            jax.ShapeDtypeStruct((1, width), f32),
            jax.ShapeDtypeStruct((1, width), f32),
            jax.ShapeDtypeStruct(shapes[0], f32),
            jax.ShapeDtypeStruct(shapes[1], f32),
        ],
        scratch_shapes=[
            pltpu.VMEM((block, 5 * heads * width), f32),
            pltpu.VMEM((block, 3 * heads * width), f32),
            pltpu.VMEM((block, 5 * heads * width), f32),
            pltpu.VMEM((units, width, width), f32),
        ],
        input_output_aliases=aliases,
        compiler_params=kernel_params(),
        name="mixer_backward",
    )(grad, raw, aux, segrow, *[pin(array) for array in saved], taps, bias, gain, *carry)
    low, taps_grad, bias_grad, gain_grad, adjoint, head = out
    return [adjoint, head, taps_grad, bias_grad, gain_grad, low]


def up_to(x, multiple):
    return -(-x // multiple) * multiple


def row_scale(values):
    return lax.rsqrt(jnp.mean(values * values, axis=-1, keepdims=True) + EPS)


def norm_back(grad, values, scale, gain):
    normed = values * scale
    gain_grad = jnp.sum(grad * normed, axis=0)
    weighted = grad * gain
    value_grad = scale * (weighted - normed * jnp.mean(weighted * normed, axis=-1, keepdims=True))
    return (value_grad, gain_grad)


def dot(left, right, dims=NN):
    return lax.dot_general(left, right, (dims, ((), ())), preferred_element_type=jnp.float32)


def swap(x, axis, bit):
    size = lax.axis_size(axis)
    return lax.ppermute(x, axis, [(i, i ^ bit) for i in range(size)])


def exchange(blocks, axis):
    return lax.all_to_all(blocks, axis, split_axis=0, concat_axis=0, tiled=True)


def trade(blocks, axis):
    return [blocks[0]] + [swap(block, axis, r) for r, block in enumerate(blocks) if r > 0]


def rows_of(array, index, rows):
    return lax.dynamic_slice_in_dim(array, index * rows, rows, axis=0)


def in_order(blocks, index):
    rows = blocks[0].shape[0]
    out = jnp.zeros((rows * len(blocks),) + blocks[0].shape[1:], blocks[0].dtype)
    for r, block in enumerate(blocks):
        out = lax.dynamic_update_slice_in_dim(out, block, (index ^ r) * rows, axis=0)
    return out


def bits_of(size):
    return [1 << b for b in range(size.bit_length() - 1)]


def chip_sum(left, right, axis):
    size = lax.axis_size(axis)
    core = lax.axis_index(axis) % 2
    width = left.shape[1] // size
    even = jnp.concatenate(
        [left[:, j * width : (j + 1) * width] for j in range(0, size, 2)], axis=1
    )
    odd = jnp.concatenate([left[:, j * width : (j + 1) * width] for j in range(1, size, 2)], axis=1)
    got = swap(dot(jnp.where(core == 0, odd, even), right, TN).astype(jnp.bfloat16), axis, 1)
    held = dot(jnp.where(core == 0, even, odd), right, TN) + got.astype(jnp.float32)
    return held.astype(jnp.bfloat16)


def plane_scatter(held, axis):
    chips = lax.axis_size(axis) // 2
    chip = lax.axis_index(axis) // 2
    width = held.shape[0] // chips
    total = rows_of(held, chip, width).astype(jnp.float32)
    for step in range(1, chips):
        total = total + swap(rows_of(held, chip ^ step, width), axis, 2 * step).astype(jnp.float32)
    return total


def body(
    layer_input,
    cotangent,
    segments,
    mix_gain,
    query_weight,
    key_weight,
    value_weight,
    outgate_weight,
    rate_weight,
    conv_query,
    conv_key,
    conv_value,
    decay_bias,
    out_gain,
    out_weight,
    mlp_gain,
    gate_weight,
    up_weight,
    down_weight,
):
    f32, bf16 = jnp.float32, jnp.bfloat16
    head_index = lax.axis_index("head")
    n_head, n_batch = lax.axis_size("head"), lax.axis_size("batch")
    rows, width = layer_input.shape
    length = rows * n_head
    local_heads = query_weight.shape[1] // HEAD_DIM
    unit = local_heads * HEAD_DIM
    mix_cols = 6 * unit + HEAD_DIM
    ff = gate_weight.shape[1]
    ff_pad = up_to(ff, LANE)

    copies = jnp.broadcast_to(layer_input[None], (n_head,) + layer_input.shape)
    copies, query_weight, key_weight, value_weight, outgate_weight = lax.optimization_barrier(
        (copies, query_weight, key_weight, value_weight, outgate_weight)
    )
    tokens = exchange(copies, "head")
    own_mix = jnp.concatenate(
        [
            query_weight,
            key_weight,
            value_weight,
            outgate_weight,
            jnp.pad(rate_weight, ((0, 0), (0, HEAD_DIM - rate_weight.shape[1]))),
        ],
        axis=1,
    )
    proj_w = lax.all_gather(own_mix, "batch", axis=0, tiled=True)

    pad = ((0, 0), (0, ff_pad - ff))
    own_ff = jnp.concatenate(
        [jnp.pad(gate_weight, pad), jnp.pad(up_weight, pad), jnp.pad(down_weight.T, pad)], axis=1
    )
    ff_sets = [lax.all_gather(own_ff, "batch", axis=0, tiled=True)]
    def head_cols(table, per_head):
        return lax.dynamic_slice_in_dim(
            table, head_index * local_heads * per_head, local_heads * per_head, axis=table.ndim - 1
        )

    taps = jnp.concatenate(
        [
            head_cols(conv_query, HEAD_DIM),
            head_cols(conv_key, 2 * HEAD_DIM),
            head_cols(conv_value, 2 * HEAD_DIM),
        ],
        axis=1,
    )
    own_bias = head_cols(decay_bias, 1)
    bias = jnp.stack([jnp.zeros_like(own_bias), jnp.zeros_like(own_bias), own_bias], axis=1)
    bias = jnp.pad(bias.reshape(-1), (0, HEAD_DIM - 3 * local_heads))[None]
    aux, segrow = token_aux(segments)
    tokens, later_ff, later_out, later_cot, aux, segrow, taps, bias = lax.optimization_barrier(
        (tokens, own_ff, out_weight.T, cotangent, aux, segrow, taps, bias)
    )
    out_shards = trade([later_out] * n_head, "head")
    shards = [later_ff]
    for bit in bits_of(n_head)[1:]:
        shards = shards + [swap(shard, "head", bit) for shard in shards]
    pair_grad = swap(later_cot, "head", 1)

    all_in = tokens.reshape(length, width).astype(f32)
    scale_all = row_scale(all_in)
    rows_in = (all_in * scale_all * mix_gain).astype(bf16)
    rows_in, out_shards = lax.optimization_barrier((rows_in, out_shards))
    out_all = lax.all_gather(
        jnp.concatenate(out_shards, axis=1), "batch", axis=0, tiled=True
    )
    raw, ff_sets[0] = lax.optimization_barrier((dot(rows_in, proj_w), ff_sets[0]))

    gain = out_gain[None]
    consts = (raw, aux, segrow, taps, bias, gain)
    carry, mixed_parts, saved = None, [], []
    for part in range(SPANS):
        if part == SPANS - 1:
            carry, shards = lax.optimization_barrier((carry, shards))
        mixed_part, kept, carry = mixer_forward(*consts, carry, local_heads, FWD_CHUNKS, part, SPANS)
        mixed_parts.append(mixed_part)
        saved.append(kept)
    mixed_parts, pair_grad = lax.optimization_barrier((mixed_parts, pair_grad))
    mixed_low = jnp.concatenate(mixed_parts, axis=0)
    ff_sets += [lax.all_gather(shard, "batch", axis=0, tiled=True) for shard in shards[1:]]

    mixed_all = jnp.concatenate(
        trade([rows_of(mixed_low, head_index ^ r, rows) for r in range(n_head)], "head"), axis=1
    )
    resid_in = layer_input.astype(f32)
    resid_mid = resid_in + dot(mixed_all, out_all, NT)
    scale_mid = row_scale(resid_mid)
    normed_mid = (resid_mid * scale_mid * mlp_gain).astype(bf16)
    pair_mid = swap(normed_mid, "head", 1)

    def feed_forward(mid, cot):
        mid_part = None
        grads = []
        for ff_set in ff_sets:
            gate_up = dot(mid, ff_set[:, : 2 * ff_pad])
            gate_pre, up_pre = gate_up[:, :ff_pad], gate_up[:, ff_pad:]
            gate_sig = jax.nn.sigmoid(gate_pre)
            silu_gate = gate_pre * gate_sig
            hidden = (silu_gate * up_pre).astype(bf16)
            hidden_grad = dot(cot, ff_set[:, 2 * ff_pad : 3 * ff_pad])
            gate_grad = (
                hidden_grad * up_pre * gate_sig * (1.0 + gate_pre * (1.0 - gate_sig))
            ).astype(bf16)
            up_grad = (hidden_grad * silu_gate).astype(bf16)
            both_grad = jnp.concatenate([gate_grad, up_grad], axis=1)
            mid_here = dot(both_grad, ff_set[:, : 2 * ff_pad], NT)
            mid_part = mid_here if mid_part is None else mid_part + mid_here
            grads.append((both_grad, hidden))
        return mid_part, grads

    mid_own, grads_own = feed_forward(normed_mid, cotangent)
    pair_mid, grads_own[0] = lax.optimization_barrier((pair_mid, grads_own[0]))
    mid_pair, grads_pair = feed_forward(pair_mid, pair_grad)
    both_mid = jnp.concatenate([normed_mid, pair_mid], axis=0)
    both_cot = jnp.concatenate([cotangent, pair_grad], axis=0)

    def weight_sums(mid, cot, own, pair):
        both, hidden = [jnp.concatenate(pieces, axis=0) for pieces in zip(own, pair)]
        return jnp.concatenate([dot(mid, both, TN), dot(cot, hidden, TN)], axis=1).astype(bf16)

    half = len(ff_sets) // 2
    ff_grads = list(zip(grads_own, grads_pair))
    ff_first = [weight_sums(both_mid, both_cot, *grads) for grads in reversed(ff_grads[half:])]
    mid_swap, ff_first, mid_own = lax.optimization_barrier(
        (swap(mid_pair.astype(bf16), "head", 1), ff_first, mid_own)
    )
    mid_grad = mid_own + mid_swap.astype(f32)
    mid_back, mlp_gain_part = norm_back(mid_grad, resid_mid, scale_mid, mlp_gain)
    resid_grad = cotangent.astype(f32) + mid_back
    branch_grad = resid_grad.astype(bf16)
    mixed_grad = dot(branch_grad, out_all).astype(bf16)
    mixed_grad = trade([mixed_grad[:, r * unit : (r + 1) * unit] for r in range(n_head)], "head")
    mixed_grad[1], out_hidden = lax.optimization_barrier(
        (mixed_grad[1], [hidden for _, hidden in grads_pair])
    )
    mixed_grad = in_order(mixed_grad, head_index)
    ff_first = [
        lax.psum_scatter(part, "batch", scatter_dimension=0, tiled=True) for part in ff_first
    ]
    downs = [ff_set[:, 2 * ff_pad : 3 * ff_pad] for ff_set in ff_sets]
    out_pair = sum(dot(hidden, down, NT) for hidden, down in zip(out_hidden, downs))
    out_swap = swap(out_pair.astype(bf16), "head", 1)

    carry = None
    for part in reversed(range(SPANS)):
        if part == 0:
            carry, branch_rows, both_mid, both_cot, ff_grads = lax.optimization_barrier(
                (carry, branch_grad, both_mid, both_cot, ff_grads[:half])
            )
            ff_last = [weight_sums(both_mid, both_cot, *grads) for grads in reversed(ff_grads)]
            ff_last[-1] = jnp.concatenate(
                [ff_last[-1], dot(branch_rows.T, mixed_all).astype(bf16)], axis=1
            )
            carry, _, ff_first = lax.optimization_barrier((carry, ff_last, ff_first))
            ff_last = [
                lax.psum_scatter(rest, "batch", scatter_dimension=0, tiled=True)
                for rest in ff_last
            ]
        carry = mixer_backward(
            mixed_grad, raw, aux, segrow, saved[part], taps, bias, gain, carry,
            local_heads, BWD_CHUNKS, part, SPANS,
        )
    _, _, taps_grad, bias_grad, gain_grad, raw_low = carry
    raw_low, taps_grad, bias_grad, gain_grad, out_swap, sent = lax.optimization_barrier(
        (
            raw_low,
            taps_grad,
            bias_grad,
            gain_grad,
            out_swap,
            [swap(part, "head", bits_of(n_head)[-1]) for part in ff_first],
        )
    )
    total = dot(raw_low, proj_w, NT).astype(bf16)
    total, later_low = lax.optimization_barrier((total, raw_low))
    received = exchange(total.reshape(n_head, rows, width), "head")
    held = chip_sum(rows_in, later_low, "batch")
    mix_rows, late_tokens, late_scale, held = lax.optimization_barrier(
        (total, tokens, scale_all, held)
    )
    normed_all = late_tokens.reshape(length, width).astype(f32) * late_scale
    mix_gain_part = jnp.sum(mix_rows.astype(f32) * normed_all, axis=0)
    mix_total = plane_scatter(held, "batch")
    hiddens, _ = lax.optimization_barrier(([hidden for _, hidden in grads_own], held))
    out_own = sum(dot(own, down, NT) for own, down in zip(hiddens, downs))
    layer_output = (resid_mid + out_own + out_swap.astype(f32)).astype(bf16)
    ff_kept, _ = lax.optimization_barrier((ff_last, held))
    ff_total = [got.astype(f32) + kept.astype(f32) for got, kept in zip(sent, [kept[:, : 3 * ff_pad] for kept in ff_kept])]
    for bit in reversed(bits_of(n_head)[1:-1]):
        half = len(ff_total) // 2
        ff_total = [
            kept + swap(part.astype(bf16), "head", bit).astype(f32)
            for part, kept in zip(ff_total[:half], ff_total[half:])
        ]
    ff_total = ff_total[0].T
    done = (
        layer_output,
        mix_total[:, :unit],
        mix_total[:, unit : 3 * unit],
        mix_total[:, 3 * unit : 5 * unit],
        mix_total[:, 5 * unit : 6 * unit],
        mix_total[:, 6 * unit : 6 * unit + rate_weight.shape[1]],
        ff_total[:ff].T,
        ff_total[ff_pad : ff_pad + ff].T,
        ff_total[2 * ff_pad : 2 * ff_pad + ff],
    )

    own_bias_grad = bias_grad[0, : 3 * local_heads].reshape(local_heads, 3)[:, 2]
    small = [
        taps_grad[:, :unit].reshape(-1),
        taps_grad[:, unit : 3 * unit].reshape(-1),
        taps_grad[:, 3 * unit :].reshape(-1),
        own_bias_grad,
        gain_grad[0],
        mlp_gain_part,
        mix_gain_part,
    ]
    lengths = [part.shape[0] for part in small]
    packed, mix_total, out_sum = lax.optimization_barrier(
        (pack(small), mix_total, ff_kept[-1][:, 3 * ff_pad :])
    )
    out_blocks = trade([out_sum[:, r * unit : (r + 1) * unit] for r in range(n_head)], "head")
    for bit in bits_of(n_batch):
        packed = packed + swap(packed, "batch", bit)
    small = unpack(packed, lengths)

    def place_cols(table_shape, local_part, per_head):
        local_part = local_part.reshape(table_shape[:-1] + (-1,))
        return lax.dynamic_update_slice_in_dim(
            jnp.zeros(table_shape, f32),
            local_part,
            head_index * local_heads * per_head,
            axis=len(table_shape) - 1,
        ).reshape(-1)

    tables = [
        place_cols(conv_query.shape, small[0], HEAD_DIM),
        place_cols(conv_key.shape, small[1], 2 * HEAD_DIM),
        place_cols(conv_value.shape, small[2], 2 * HEAD_DIM),
        place_cols(decay_bias.shape, small[3], 1),
    ] + small[4:]
    lengths = [part.shape[0] for part in tables]
    packed, received, done = lax.optimization_barrier((pack(tables), received, done))
    for bit in bits_of(n_head):
        packed = packed + swap(packed, "head", bit)
    tables = unpack(packed, lengths)
    in_grad = jnp.sum(received.astype(f32), axis=0)
    in_back, _ = norm_back(in_grad, resid_in, row_scale(resid_in), mix_gain)
    input_grad = resid_grad + in_back

    out_total = sum(block.astype(f32) for block in out_blocks)
    return (
        done[0],
        input_grad,
        tables[6],
        *done[1:6],
        tables[0].reshape(conv_query.shape),
        tables[1].reshape(conv_key.shape),
        tables[2].reshape(conv_value.shape),
        tables[3],
        tables[4],
        out_total.T,
        tables[5],
        *done[6:],
    )


def pack(parts):
    flat = jnp.concatenate(parts)
    return jnp.pad(flat, (0, -flat.shape[0] % (8 * LANE))).reshape(-1, LANE)


def unpack(packed, lengths):
    flat = packed.reshape(-1)
    out, at = [], 0
    for size in lengths:
        out.append(flat[at : at + size])
        at += size
    return out


def solution(mesh):
    placed = (
        P(("batch", "head"), None),
        P(("batch", "head"), None),
        P("batch"),
        P(),
        P("batch", "head"),
        P("batch", "head"),
        P("batch", "head"),
        P("batch", "head"),
        P("batch", "head"),
        P(),
        P(),
        P(),
        P(),
        P(),
        P("head", "batch"),
        P(),
        P("batch", "head"),
        P("batch", "head"),
        P("head", "batch"),
    )
    return jax.shard_map(
        body,
        mesh=mesh,
        in_specs=placed,
        out_specs=(
            P(("batch", "head"), None),
            P(("batch", "head"), None),
            P(),
            P("batch", "head"),
            P("batch", "head"),
            P("batch", "head"),
            P("batch", "head"),
            P("batch", "head"),
            P(),
            P(),
            P(),
            P(),
            P(),
            P("head", "batch"),
            P(),
            P("batch", "head"),
            P("batch", "head"),
            P("head", "batch"),
        ),
        check_vma=False,
    )
```

```python
from functools import partial

import jax
import jax.numpy as jnp
from jax import lax
from jax.experimental import pallas as pl
from jax.experimental.pallas import tpu as pltpu
from jax.sharding import PartitionSpec as P

HEAD_DIM = 128
EPS = 1e-06
EXACT = lax.Precision.HIGHEST
HIGH = lax.Precision.HIGH
FAST = lax.Precision.DEFAULT
NN = ((1,), (0,))
NT = ((1,), (1,))
TN = ((0,), (0,))
LANE = 128
CHUNK = 64
ROWS = 2 * CHUNK
FWD_CHUNKS = 4
BWD_CHUNKS = 2
SPANS = 2


def mm(left, right, dims=NN, precision=HIGH):
    return lax.dot_general(
        left, right, (dims, ((), ())), precision=precision, preferred_element_type=jnp.float32
    )


def softplus(x):
    return jnp.maximum(x, 0.0) + jnp.log1p(jnp.exp(-jnp.abs(x)))


def chunk_masks():
    row = lax.broadcasted_iota(jnp.int32, (ROWS, ROWS), 0)
    col = lax.broadcasted_iota(jnp.int32, (ROWS, ROWS), 1)
    row_tok, col_tok = row & (CHUNK - 1), col & (CHUNK - 1)
    later = row_tok > col_tok
    same_tok = row_tok == col_tok
    pair = same_tok & (row > col)
    levels = []
    size = 1
    while size < CHUNK:
        upper = (row_tok & size) > (col_tok & size)
        together = (row_tok & (-2 * size)) == (col_tok & (-2 * size))
        levels.append(upper & together)
        size *= 2
    return row, col, later | same_tok, later | pair, pair, levels


def invert(lowers, ident, pair, levels, precision):
    inverses = [ident - jnp.where(pair, lower, 0.0) for lower in lowers]
    for level in levels:
        steps = [
            mm(jnp.where(level, lower, 0.0), inverse, NN, precision)
            for lower, inverse in zip(lowers, inverses)
        ]
        inverses = [
            inverse - mm(inverse, step, NN, precision) for inverse, step in zip(inverses, steps)
        ]
    return inverses


def col_sum(x):
    return jnp.sum(x, axis=-1, keepdims=True)


def twice(x):
    return jnp.concatenate([x, x], axis=0)


def unit_slices(heads, head):
    names = [heads + 2 * head, heads + 2 * head + 1, 3 * heads + 2 * head, 3 * heads + 2 * head + 1]
    names += [head, 5 * heads + head]
    return [slice(n * HEAD_DIM, (n + 1) * HEAD_DIM) for n in names]


def decays_of(cumul, cumul_t, beta_rows, aux, same, lane):
    c_tok = cumul[:, lane + 2 : lane + 3]
    c_end = cumul[CHUNK - 1 :, lane + 2 : lane + 3]
    decay = jnp.where(
        same, jnp.exp(jnp.minimum(twice(c_tok) - cumul_t[lane + 2 : lane + 3, :], 0.0)), 0.0
    )
    beta = jnp.concatenate(
        [beta_rows[:, lane : lane + 1], beta_rows[:, lane + 1 : lane + 2]], axis=0
    )
    start = aux[:, 0:1] * jnp.exp(c_tok)
    final = twice(aux[:, 1:2] * jnp.exp(c_end - c_tok))
    total = aux[CHUNK - 1 :, 0:1] * jnp.exp(c_end)
    return decay, beta, start, final, total


def fwd_kernel(
    heads, per_step, raw_ref, aux_ref, segrow_ref, taps_ref, bias_ref, gain_ref, mem_in, tail_in,
    mixed_ref, pre_ref, recall_ref, inv_ref, prox_ref, state_ref, move_ref, probe_ref,
    mem_ref, tail_ref, act_ref,
):
    width = HEAD_DIM
    block = per_step * CHUNK

    @pl.when(pl.program_id(0) == 0)
    def _():
        mem_ref[...] = mem_in[...]
        tail_ref[...] = tail_in[...]

    masks = [aux_ref[:, 2 + s : 3 + s] for s in range(3)]
    for tile in range(5 * heads):
        cols = slice(tile * width, (tile + 1) * width)
        raw = raw_ref[:, cols]
        joined = jnp.concatenate([tail_ref[:, cols], raw], axis=0)
        pre = raw * taps_ref[0:1, cols]
        for s in range(1, 4):
            shifted = pltpu.roll(joined, s, 0)[8:]
            pre = pre + shifted * masks[s - 1] * taps_ref[s : s + 1, cols]
        pre_ref[:, cols] = pre
        tail_ref[:, cols] = raw[block - 8 :]
        act = pre * jax.nn.sigmoid(pre)
        if tile < 3 * heads:
            act = act * lax.rsqrt(col_sum(act * act) + EPS)
        act_ref[:, cols] = act

    row, col, lower_eq, strict, pair, levels = chunk_masks()
    ident = (row == col).astype(jnp.float32)
    tri = (row[:CHUNK, :CHUNK] >= col[:CHUNK, :CHUNK]).astype(jnp.float32)
    rates = raw_ref[:, 6 * heads * width :]
    beta_tile = jax.nn.sigmoid(rates)
    log_tile = -softplus(rates + bias_ref[...])
    units = [(part, head) for part in range(per_step) for head in range(heads)]
    spans = [slice(part * CHUNK, (part + 1) * CHUNK) for part in range(per_step)]
    cumuls = [mm(tri, log_tile[rows], NN, EXACT) for rows in spans]
    cumul_ts = [twice(cumul).T for cumul in cumuls]
    sames = [
        (twice(aux_ref[rows, 8:9]) == segrow_ref[part]) & lower_eq
        for part, rows in enumerate(spans)
    ]
    keys, queries, decays, lowers, scores = [], [], [], [], []
    for part, head in units:
        k1, k2, v1, v2, q0, g0 = unit_slices(heads, head)
        rows = spans[part]
        key = jnp.concatenate([act_ref[rows, k1], act_ref[rows, k2]], axis=0)
        query = act_ref[rows, q0]
        decay = decays_of(
            cumuls[part], cumul_ts[part], beta_tile[rows], aux_ref[rows], sames[part], 3 * head
        )
        dots = mm(jnp.concatenate([key, query], axis=0), key, NT)
        keys.append(key)
        queries.append(query)
        decays.append(decay)
        lowers.append(jnp.where(strict, decay[1] * decay[0] * dots[:ROWS], 0.0))
        scores.append(decay[0][CHUNK:] * dots[ROWS:])
    inverses = invert(lowers, ident, pair, levels, HIGH)
    solved = []
    for u, (part, head) in enumerate(units):
        k1, k2, v1, v2, q0, g0 = unit_slices(heads, head)
        rows = spans[part]
        decay, beta, start, final, total = decays[u]
        inv_ref[u] = inverses[u]
        value = jnp.concatenate([act_ref[rows, v1], act_ref[rows, v2]], axis=0)
        solved.append(
            mm(
                inverses[u],
                jnp.concatenate([beta * value, beta * twice(start) * keys[u]], axis=1),
            )
        )
    moves = [mm(decays[u][3] * keys[u], solved[u], TN) for u in range(len(units))]
    reads = [mm(scores[u], solved[u]) for u in range(len(units))]
    for u, (part, head) in enumerate(units):
        memory = mem_ref[head]
        state_ref[u] = memory
        move_ref[u] = moves[u][:, width:]
        mem_ref[head] = (
            decays[u][4] * memory + moves[u][:, :width] - mm(moves[u][:, width:], memory)
        )
    for u, (part, head) in enumerate(units):
        probe = decays[u][2] * queries[u] - reads[u][:, width:]
        probe_ref[u] = probe
        seen = mm(jnp.concatenate([solved[u][:, width:], probe], axis=0), state_ref[u])
        prox_ref[u] = solved[u][:, :width] - seen[:ROWS]
        recall = reads[u][:, :width] + seen[ROWS:]
        rows = spans[part]
        cols = slice(head * width, (head + 1) * width)
        recall_ref[rows, cols] = recall
        scale = lax.rsqrt(jnp.mean(recall * recall, axis=-1, keepdims=True) + EPS)
        gate = raw_ref[rows, unit_slices(heads, head)[5]]
        mixed = recall * scale * gain_ref[...] * (gate * jax.nn.sigmoid(gate))
        mixed_ref[rows, cols] = mixed.astype(jnp.bfloat16)


def bwd_kernel(
    heads, per_step, grad_ref, raw_ref, aux_ref, segrow_ref, pre_ref, recall_ref, inv_ref,
    prox_ref, state_ref, move_ref, probe_ref, taps_ref, bias_ref, gain_ref,
    adj_in, head_in, taps_grad_in, bias_grad_in, gain_grad_in, low_in,
    low_ref, taps_grad_ref, bias_grad_ref, gain_grad_ref, adj_ref, head_ref,
    act_ref, norm_ref, dact_ref, keep_ref,
):
    width = HEAD_DIM
    block = per_step * CHUNK

    @pl.when(pl.program_id(0) == 0)
    def _():
        adj_ref[...] = adj_in[...]
        head_ref[...] = head_in[...]
        taps_grad_ref[...] = taps_grad_in[...]
        bias_grad_ref[...] = bias_grad_in[...]
        gain_grad_ref[...] = gain_grad_in[...]

    row, col, lower_eq, strict, pair, levels = chunk_masks()
    tri = (row[:CHUNK, :CHUNK] >= col[:CHUNK, :CHUNK]).astype(jnp.float32)
    tri_t = (row[:CHUNK, :CHUNK] <= col[:CHUNK, :CHUNK]).astype(jnp.float32)
    lanes = col[:CHUNK, :]
    rates = raw_ref[:, 6 * heads * width :]
    beta_tile = jax.nn.sigmoid(rates)
    keep_in = rates + bias_ref[...]
    log_tile = -softplus(keep_in)
    units = [(part, head) for part in reversed(range(per_step)) for head in range(heads)]
    spans = [slice(part * CHUNK, (part + 1) * CHUNK) for part in range(per_step)]
    cumuls = [mm(tri, log_tile[rows], NN, EXACT) for rows in spans]
    cumul_ts = [twice(cumul).T for cumul in cumuls]
    sames = [
        (twice(aux_ref[rows, 8:9]) == segrow_ref[part]) & lower_eq
        for part, rows in enumerate(spans)
    ]
    gain_total = jnp.zeros((1, width), jnp.float32)
    out_grads = []
    for part, head in units:
        rows = spans[part]
        q0, g0 = unit_slices(heads, head)[4:]
        recall = recall_ref[rows, q0]
        grad = grad_ref[rows, q0].astype(jnp.float32)
        gate = raw_ref[rows, g0]
        gate_sig = jax.nn.sigmoid(gate)
        silu_gate = gate * gate_sig
        scale = lax.rsqrt(jnp.mean(recall * recall, axis=-1, keepdims=True) + EPS)
        normed = recall * scale
        gain_total = gain_total + jnp.sum(grad * normed * silu_gate, axis=0, keepdims=True)
        weighted = grad * gain_ref[...]
        low_ref[rows, g0] = (
            weighted * normed * gate_sig * (1.0 + gate * (1.0 - gate_sig))
        ).astype(jnp.bfloat16)
        normed_grad = weighted * silu_gate
        out_grads.append(
            scale * (normed_grad - normed * jnp.mean(normed_grad * normed, axis=-1, keepdims=True))
        )
    gain_grad_ref[...] += gain_total
    reads = [
        mm(probe_ref[part * heads + head], out_grads[u], TN) for u, (part, head) in enumerate(units)
    ]
    for u, (part, head) in enumerate(units):
        spot = part * heads + head
        c_end = cumuls[part][CHUNK - 1 :, 3 * head + 2 : 3 * head + 3]
        total = aux_ref[(part + 1) * CHUNK - 1 : (part + 1) * CHUNK, 0:1] * jnp.exp(c_end)
        adjoint = adj_ref[head]
        keep_ref[spot] = adjoint
        adj_ref[head] = total * adjoint + reads[u] - mm(move_ref[spot], adjoint, TN)
    for tile in range(5 * heads):
        cols = slice(tile * width, (tile + 1) * width)
        pre = pre_ref[:, cols]
        act = pre * jax.nn.sigmoid(pre)
        if tile < 3 * heads:
            scale = lax.rsqrt(col_sum(act * act) + EPS)
            norm_ref[:, cols] = jnp.broadcast_to(scale, act.shape)
            act = act * scale
        act_ref[:, cols] = act
    keys, decays, dots = [], [], []
    for u, (part, head) in enumerate(units):
        k1, k2, v1, v2, q0, g0 = unit_slices(heads, head)
        rows = spans[part]
        key = jnp.concatenate([act_ref[rows, k1], act_ref[rows, k2]], axis=0)
        keys.append(key)
        decays.append(
            decays_of(
                cumuls[part], cumul_ts[part], beta_tile[rows], aux_ref[rows], sames[part], 3 * head
            )
        )
        dots.append(mm(jnp.concatenate([key, act_ref[rows, q0]], axis=0), key, NT))
    scores = [decays[u][0][CHUNK:] * dots[u][ROWS:] for u in range(len(units))]
    proxy_grads = [
        mm(scores[u], out_grads[u], TN)
        + mm(decays[u][3] * keys[u], keep_ref[part * heads + head])
        for u, (part, head) in enumerate(units)
    ]
    both_grads = [
        jnp.concatenate(
            [mm(inv_ref[part * heads + head], proxy_grads[u], TN), out_grads[u]], axis=0
        )
        for u, (part, head) in enumerate(units)
    ]
    outers = [
        mm(both_grads[u], prox_ref[part * heads + head], NT)
        for u, (part, head) in enumerate(units)
    ]
    throughs = [
        mm(both_grads[u], state_ref[part * heads + head], NT)
        for u, (part, head) in enumerate(units)
    ]
    finals = [
        decays[u][3] * mm(prox_ref[part * heads + head], keep_ref[part * heads + head], NT)
        for u, (part, head) in enumerate(units)
    ]
    score_grads, inners, beta_parts, log_cols = [], [], [], []
    for u, (part, head) in enumerate(units):
        decay, beta, start, final, total = decays[u]
        key_decay = jnp.where(strict, decay * dots[u][:ROWS], 0.0)
        lower_grad = -outers[u][:ROWS]
        beta_part = lower_grad * key_decay
        dots_grad = jnp.where(strict, lower_grad * beta * decay, 0.0)
        score_grad = outers[u][ROWS:] * decay[CHUNK:]
        log_part = beta_part * beta
        log_part = jnp.concatenate(
            [log_part[:CHUNK], log_part[CHUNK:] + outers[u][ROWS:] * scores[u]], axis=0
        )
        log_cols.append(col_sum(log_part - log_part.T))
        beta_parts.append(col_sum(beta_part))
        score_grads.append(score_grad)
        inners.append(
            mm(jnp.concatenate([dots_grad + dots_grad.T, score_grad], axis=0), keys[u])
        )
    zero = jnp.zeros((CHUNK, width), jnp.float32)
    beta_grads, cumul_grads, end_grads = [zero] * per_step, [zero] * per_step, [zero] * per_step
    for u, (part, head) in enumerate(units):
        k1, k2, v1, v2, q0, g0 = unit_slices(heads, head)
        rows = spans[part]
        spot = part * heads + head
        lane = 3 * head
        decay, beta, start, final, total = decays[u]
        through, final_part, right_grad = throughs[u], finals[u], both_grads[u][:ROWS]
        query = act_ref[rows, q0]
        value = jnp.concatenate([act_ref[rows, v1], act_ref[rows, v2]], axis=0)
        beta_start = beta * twice(start)
        key_through = col_sum(keys[u] * through[:ROWS])
        query_through = start * col_sum(query * through[ROWS:])
        final_sum = col_sum(keys[u] * final_part)
        key_grad = (
            inners[u][:ROWS]
            + mm(score_grads[u], query, TN)
            - beta_start * through[:ROWS]
            + final_part
        )
        dact_ref[rows, k1] = key_grad[:CHUNK]
        dact_ref[rows, k2] = key_grad[CHUNK:]
        value_grad = beta * right_grad
        dact_ref[rows, v1] = value_grad[:CHUNK]
        dact_ref[rows, v2] = value_grad[CHUNK:]
        dact_ref[rows, q0] = inners[u][ROWS:] + start * through[ROWS:]
        beta_col = col_sum(right_grad * value) - twice(start) * key_through + beta_parts[u]
        c_grad = log_cols[u] - beta_start * key_through - final_sum
        c_grad = c_grad[:CHUNK] + c_grad[CHUNK:] + query_through
        end_part = jnp.sum(final_sum, axis=0, keepdims=True) + total * jnp.sum(
            col_sum(state_ref[spot] * keep_ref[spot]), axis=0, keepdims=True
        )
        beta_grads[part] = jnp.where(
            lanes == lane,
            beta_col[:CHUNK],
            jnp.where(lanes == lane + 1, beta_col[CHUNK:], beta_grads[part]),
        )
        cumul_grads[part] = jnp.where(lanes == lane + 2, c_grad, cumul_grads[part])
        end_grads[part] = jnp.where(lanes == lane + 2, end_part, end_grads[part])
    bias_total = jnp.zeros((1, width), jnp.float32)
    for part, rows in enumerate(spans):
        log_grad = mm(tri_t, cumul_grads[part], NN, EXACT) + end_grads[part]
        beta_rows = beta_tile[rows]
        keep_grad = -log_grad * jax.nn.sigmoid(keep_in[rows]) * aux_ref[rows, 2:3]
        rate_grad = beta_grads[part] * beta_rows * (1.0 - beta_rows) + keep_grad
        bias_total = bias_total + jnp.sum(keep_grad, axis=0, keepdims=True)
        low_ref[rows, 6 * heads * width :] = rate_grad.astype(jnp.bfloat16)
    bias_grad_ref[...] += bias_total

    masks = [aux_ref[:, 5 + s : 6 + s] for s in range(3)]
    for tile in range(5 * heads):
        cols = slice(tile * width, (tile + 1) * width)
        pre = pre_ref[:, cols]
        sig = jax.nn.sigmoid(pre)
        grad = dact_ref[:, cols]
        if tile < 3 * heads:
            act = act_ref[:, cols]
            grad = norm_ref[:, cols] * (grad - act * col_sum(grad * act))
        grad = grad * sig * (1.0 + pre * (1.0 - sig))
        raw = raw_ref[:, cols]
        joined = jnp.concatenate([grad, head_ref[:, cols]], axis=0)
        head_ref[:, cols] = grad[:8]
        raw_grad = grad * taps_ref[0:1, cols]
        taps_grad_ref[0:1, cols] += jnp.sum(raw * grad, axis=0, keepdims=True)
        for s in range(1, 4):
            shifted = pltpu.roll(joined, block + 8 - s, 0)[:block] * masks[s - 1]
            raw_grad = raw_grad + shifted * taps_ref[s : s + 1, cols]
            taps_grad_ref[s : s + 1, cols] += jnp.sum(raw * shifted, axis=0, keepdims=True)
        low_ref[:, cols] = raw_grad.astype(jnp.bfloat16)


def token_aux(segments):
    length = segments.shape[0]
    seg = segments.astype(jnp.int32)
    chunks = seg.reshape(length // CHUNK, CHUNK)
    last = chunks[:, -1]
    before = jnp.concatenate([jnp.full((1,), -1, jnp.int32), last[:-1]])
    columns = [
        (chunks == before[:, None]).reshape(length),
        (chunks == last[:, None]).reshape(length),
    ]
    for s in range(1, 4):
        columns.append(jnp.pad(seg, (s, 0), constant_values=-1)[:length] == seg)
    for s in range(1, 4):
        columns.append(jnp.pad(seg, (0, s), constant_values=-1)[s:] == seg)
    columns.append(seg)
    columns += [jnp.zeros_like(seg)] * 7
    aux = jnp.stack([c.astype(jnp.float32) for c in columns], axis=1)
    row = chunks.astype(jnp.float32)
    return aux, jnp.concatenate([row, row], axis=1)[:, None, :]


def kernel_params():
    return pltpu.CompilerParams(
        dimension_semantics=("arbitrary",), vmem_limit_bytes=48 * 1024 * 1024
    )


def pin(array):
    return pltpu.with_memory_space_constraint(array, pltpu.HBM)


def whole(shape):
    zeros = (0,) * len(shape)
    return pl.BlockSpec(shape, lambda i: zeros)


def mixer_forward(raw, aux, segrow, taps, bias, gain, carry, heads, per_step, part, parts):
    width = HEAD_DIM
    block = per_step * CHUNK
    length = raw.shape[0] // parts
    steps = length // block
    first = part * steps
    units = per_step * heads
    total_units = steps * units
    cols = raw.shape[1]
    f32 = jnp.float32
    if carry is None:
        carry = (jnp.zeros((heads, width, width), f32), jnp.zeros((8, 5 * heads * width), f32))
    memory, tail = carry
    read = lambda i: (first + i, 0)
    read_cube = lambda i: (first + i, 0, 0)
    tiles = lambda i: (i, 0)
    cubes = lambda i: (i, 0, 0)
    unit_spec = pl.BlockSpec((units, ROWS, width), cubes)
    unit_shape = pltpu.HBM((total_units, ROWS, width), f32)
    out = pl.pallas_call(
        partial(fwd_kernel, heads, per_step),
        grid=(steps,),
        in_specs=[
            pl.BlockSpec((block, cols), read),
            pl.BlockSpec((block, 16), read),
            pl.BlockSpec((per_step, 1, ROWS), read_cube),
            whole(taps.shape),
            whole((1, width)),
            whole((1, width)),
            whole(memory.shape),
            whole(tail.shape),
        ],
        out_specs=[
            pl.BlockSpec((block, heads * width), tiles),
            pl.BlockSpec((block, 5 * heads * width), tiles),
            pl.BlockSpec((block, heads * width), tiles),
            unit_spec,
            unit_spec,
            unit_spec,
            unit_spec,
            pl.BlockSpec((units, CHUNK, width), cubes),
            whole(memory.shape),
            whole(tail.shape),
        ],
        out_shape=[
            jax.ShapeDtypeStruct((length, heads * width), jnp.bfloat16),
            pltpu.HBM((length, 5 * heads * width), f32),
            pltpu.HBM((length, heads * width), f32),
            unit_shape,
            unit_shape,
            unit_shape,
            unit_shape,
            pltpu.HBM((total_units, CHUNK, width), f32),
            jax.ShapeDtypeStruct(memory.shape, f32),
            jax.ShapeDtypeStruct(tail.shape, f32),
        ],
        scratch_shapes=[pltpu.VMEM((block, 5 * heads * width), f32)],
        compiler_params=kernel_params(),
        name="mixer_forward",
    )(raw, aux, segrow, taps, bias, gain, memory, tail)
    return out[0], out[1:8], (out[8], out[9])


def mixer_backward(grad, raw, aux, segrow, saved, taps, bias, gain, carry, heads, per_step, part, parts):
    width = HEAD_DIM
    block = per_step * CHUNK
    length = raw.shape[0] // parts
    steps = length // block
    last = (part + 1) * steps - 1
    units = per_step * heads
    cols = raw.shape[1]
    f32 = jnp.float32
    shapes = [
        (heads, width, width),
        (8, 5 * heads * width),
        taps.shape,
        (1, width),
        (1, width),
    ]
    low_shape = pltpu.HBM(raw.shape, jnp.bfloat16)
    if carry is None:
        carry = [jnp.zeros(shape, f32) for shape in shapes] + [jnp.zeros((16, width), jnp.bfloat16)]
        aliases = {}
    else:
        aliases = {19: 0}
    read = lambda i: (last - i, 0)
    read_cube = lambda i: (last - i, 0, 0)
    tiles = lambda i: (steps - 1 - i, 0)
    cubes = lambda i: (steps - 1 - i, 0, 0)
    unit_spec = pl.BlockSpec((units, ROWS, width), cubes)
    out = pl.pallas_call(
        partial(bwd_kernel, heads, per_step),
        grid=(steps,),
        in_specs=[
            pl.BlockSpec((block, heads * width), read),
            pl.BlockSpec((block, cols), read),
            pl.BlockSpec((block, 16), read),
            pl.BlockSpec((per_step, 1, ROWS), read_cube),
            pl.BlockSpec((block, 5 * heads * width), tiles),
            pl.BlockSpec((block, heads * width), tiles),
            unit_spec,
            unit_spec,
            unit_spec,
            unit_spec,
            pl.BlockSpec((units, CHUNK, width), cubes),
            whole(taps.shape),
            whole((1, width)),
            whole((1, width)),
        ]
        + [whole(shape) for shape in shapes]
        + [pl.BlockSpec(memory_space=pl.ANY)],
        out_specs=[
            pl.BlockSpec((block, cols), read),
            whole(taps.shape),
            whole((1, width)),
            whole((1, width)),
            whole(shapes[0]),
            whole(shapes[1]),
        ],
        out_shape=[
            low_shape,
            jax.ShapeDtypeStruct(taps.shape, f32),
            jax.ShapeDtypeStruct((1, width), f32),
            jax.ShapeDtypeStruct((1, width), f32),
            jax.ShapeDtypeStruct(shapes[0], f32),
            jax.ShapeDtypeStruct(shapes[1], f32),
        ],
        scratch_shapes=[
            pltpu.VMEM((block, 5 * heads * width), f32),
            pltpu.VMEM((block, 3 * heads * width), f32),
            pltpu.VMEM((block, 5 * heads * width), f32),
            pltpu.VMEM((units, width, width), f32),
        ],
        input_output_aliases=aliases,
        compiler_params=kernel_params(),
        name="mixer_backward",
    )(grad, raw, aux, segrow, *[pin(array) for array in saved], taps, bias, gain, *carry)
    low, taps_grad, bias_grad, gain_grad, adjoint, head = out
    return [adjoint, head, taps_grad, bias_grad, gain_grad, low]


def up_to(x, multiple):
    return -(-x // multiple) * multiple


def row_scale(values):
    return lax.rsqrt(jnp.mean(values * values, axis=-1, keepdims=True) + EPS)


def norm_back(grad, values, scale, gain):
    normed = values * scale
    gain_grad = jnp.sum(grad * normed, axis=0)
    weighted = grad * gain
    value_grad = scale * (weighted - normed * jnp.mean(weighted * normed, axis=-1, keepdims=True))
    return (value_grad, gain_grad)


def dot(left, right, dims=NN):
    return lax.dot_general(left, right, (dims, ((), ())), preferred_element_type=jnp.float32)


def swap(x, axis, bit):
    size = lax.axis_size(axis)
    return lax.ppermute(x, axis, [(i, i ^ bit) for i in range(size)])


def exchange(blocks, axis):
    return lax.all_to_all(blocks, axis, split_axis=0, concat_axis=0, tiled=True)


def trade(blocks, axis):
    return [blocks[0]] + [swap(block, axis, r) for r, block in enumerate(blocks) if r > 0]


def rows_of(array, index, rows):
    return lax.dynamic_slice_in_dim(array, index * rows, rows, axis=0)


def in_order(blocks, index):
    rows = blocks[0].shape[0]
    out = jnp.zeros((rows * len(blocks),) + blocks[0].shape[1:], blocks[0].dtype)
    for r, block in enumerate(blocks):
        out = lax.dynamic_update_slice_in_dim(out, block, (index ^ r) * rows, axis=0)
    return out


def bits_of(size):
    return [1 << b for b in range(size.bit_length() - 1)]


def chip_sum(left, right, axis):
    size = lax.axis_size(axis)
    core = lax.axis_index(axis) % 2
    width = left.shape[1] // size
    even = jnp.concatenate(
        [left[:, j * width : (j + 1) * width] for j in range(0, size, 2)], axis=1
    )
    odd = jnp.concatenate([left[:, j * width : (j + 1) * width] for j in range(1, size, 2)], axis=1)
    got = swap(dot(jnp.where(core == 0, odd, even), right, TN).astype(jnp.bfloat16), axis, 1)
    held = dot(jnp.where(core == 0, even, odd), right, TN) + got.astype(jnp.float32)
    return held.astype(jnp.bfloat16)


def plane_scatter(held, axis):
    chips = lax.axis_size(axis) // 2
    chip = lax.axis_index(axis) // 2
    width = held.shape[0] // chips
    total = rows_of(held, chip, width).astype(jnp.float32)
    for step in range(1, chips):
        total = total + swap(rows_of(held, chip ^ step, width), axis, 2 * step).astype(jnp.float32)
    return total


def body(
    layer_input,
    cotangent,
    segments,
    mix_gain,
    query_weight,
    key_weight,
    value_weight,
    outgate_weight,
    rate_weight,
    conv_query,
    conv_key,
    conv_value,
    decay_bias,
    out_gain,
    out_weight,
    mlp_gain,
    gate_weight,
    up_weight,
    down_weight,
):
    f32, bf16 = jnp.float32, jnp.bfloat16
    head_index = lax.axis_index("head")
    n_head, n_batch = lax.axis_size("head"), lax.axis_size("batch")
    rows, width = layer_input.shape
    length = rows * n_head
    local_heads = query_weight.shape[1] // HEAD_DIM
    unit = local_heads * HEAD_DIM
    mix_cols = 6 * unit + HEAD_DIM
    ff = gate_weight.shape[1]
    ff_pad = up_to(ff, LANE)

    copies = jnp.broadcast_to(layer_input[None], (n_head,) + layer_input.shape)
    copies, query_weight, key_weight, value_weight, outgate_weight = lax.optimization_barrier(
        (copies, query_weight, key_weight, value_weight, outgate_weight)
    )
    tokens = exchange(copies, "head")
    own_mix = jnp.concatenate(
        [
            query_weight,
            key_weight,
            value_weight,
            outgate_weight,
            jnp.pad(rate_weight, ((0, 0), (0, HEAD_DIM - rate_weight.shape[1]))),
        ],
        axis=1,
    )
    proj_w = lax.all_gather(own_mix, "batch", axis=0, tiled=True)

    pad = ((0, 0), (0, ff_pad - ff))
    own_ff = jnp.concatenate(
        [jnp.pad(gate_weight, pad), jnp.pad(up_weight, pad), jnp.pad(down_weight.T, pad)], axis=1
    )
    ff_sets = [lax.all_gather(own_ff, "batch", axis=0, tiled=True)]
    def head_cols(table, per_head):
        return lax.dynamic_slice_in_dim(
            table, head_index * local_heads * per_head, local_heads * per_head, axis=table.ndim - 1
        )

    taps = jnp.concatenate(
        [
            head_cols(conv_query, HEAD_DIM),
            head_cols(conv_key, 2 * HEAD_DIM),
            head_cols(conv_value, 2 * HEAD_DIM),
        ],
        axis=1,
    )
    own_bias = head_cols(decay_bias, 1)
    bias = jnp.stack([jnp.zeros_like(own_bias), jnp.zeros_like(own_bias), own_bias], axis=1)
    bias = jnp.pad(bias.reshape(-1), (0, HEAD_DIM - 3 * local_heads))[None]
    aux, segrow = token_aux(segments)
    tokens, later_ff, later_out, later_cot, aux, segrow, taps, bias = lax.optimization_barrier(
        (tokens, own_ff, out_weight.T, cotangent, aux, segrow, taps, bias)
    )
    out_shards = trade([later_out] * n_head, "head")
    shards = [later_ff]
    for bit in bits_of(n_head)[1:]:
        shards = shards + [swap(shard, "head", bit) for shard in shards]
    pair_grad = swap(later_cot, "head", 1)

    all_in = tokens.reshape(length, width).astype(f32)
    scale_all = row_scale(all_in)
    rows_in = (all_in * scale_all * mix_gain).astype(bf16)
    rows_in, out_shards = lax.optimization_barrier((rows_in, out_shards))
    out_all = lax.all_gather(
        jnp.concatenate(out_shards, axis=1), "batch", axis=0, tiled=True
    )
    raw, ff_sets[0] = lax.optimization_barrier((dot(rows_in, proj_w), ff_sets[0]))

    gain = out_gain[None]
    consts = (raw, aux, segrow, taps, bias, gain)
    carry, mixed_parts, saved = None, [], []
    for part in range(SPANS):
        if part == SPANS - 1:
            carry, shards = lax.optimization_barrier((carry, shards))
        mixed_part, kept, carry = mixer_forward(*consts, carry, local_heads, FWD_CHUNKS, part, SPANS)
        mixed_parts.append(mixed_part)
        saved.append(kept)
    mixed_parts, pair_grad = lax.optimization_barrier((mixed_parts, pair_grad))
    mixed_low = jnp.concatenate(mixed_parts, axis=0)
    ff_sets += [lax.all_gather(shard, "batch", axis=0, tiled=True) for shard in shards[1:]]

    mixed_all = jnp.concatenate(
        trade([rows_of(mixed_low, head_index ^ r, rows) for r in range(n_head)], "head"), axis=1
    )
    resid_in = layer_input.astype(f32)
    resid_mid = resid_in + dot(mixed_all, out_all, NT)
    scale_mid = row_scale(resid_mid)
    normed_mid = (resid_mid * scale_mid * mlp_gain).astype(bf16)
    pair_mid = swap(normed_mid, "head", 1)

    def feed_forward(mid, cot):
        mid_part = None
        grads = []
        for ff_set in ff_sets:
            gate_up = dot(mid, ff_set[:, : 2 * ff_pad])
            gate_pre, up_pre = gate_up[:, :ff_pad], gate_up[:, ff_pad:]
            gate_sig = jax.nn.sigmoid(gate_pre)
            silu_gate = gate_pre * gate_sig
            hidden = (silu_gate * up_pre).astype(bf16)
            hidden_grad = dot(cot, ff_set[:, 2 * ff_pad : 3 * ff_pad])
            gate_grad = (
                hidden_grad * up_pre * gate_sig * (1.0 + gate_pre * (1.0 - gate_sig))
            ).astype(bf16)
            up_grad = (hidden_grad * silu_gate).astype(bf16)
            both_grad = jnp.concatenate([gate_grad, up_grad], axis=1)
            mid_here = dot(both_grad, ff_set[:, : 2 * ff_pad], NT)
            mid_part = mid_here if mid_part is None else mid_part + mid_here
            grads.append((both_grad, hidden))
        return mid_part, grads

    mid_own, grads_own = feed_forward(normed_mid, cotangent)
    pair_mid, grads_own[0] = lax.optimization_barrier((pair_mid, grads_own[0]))
    mid_pair, grads_pair = feed_forward(pair_mid, pair_grad)
    both_mid = jnp.concatenate([normed_mid, pair_mid], axis=0)
    both_cot = jnp.concatenate([cotangent, pair_grad], axis=0)

    def weight_sums(mid, cot, own, pair):
        both, hidden = [jnp.concatenate(pieces, axis=0) for pieces in zip(own, pair)]
        return jnp.concatenate([dot(mid, both, TN), dot(cot, hidden, TN)], axis=1).astype(bf16)

    half = len(ff_sets) // 2
    ff_grads = list(zip(grads_own, grads_pair))
    ff_first = [weight_sums(both_mid, both_cot, *grads) for grads in reversed(ff_grads[half:])]
    mid_swap, ff_first, mid_own = lax.optimization_barrier(
        (swap(mid_pair.astype(bf16), "head", 1), ff_first, mid_own)
    )
    mid_grad = mid_own + mid_swap.astype(f32)
    mid_back, mlp_gain_part = norm_back(mid_grad, resid_mid, scale_mid, mlp_gain)
    resid_grad = cotangent.astype(f32) + mid_back
    branch_grad = resid_grad.astype(bf16)
    mixed_grad = dot(branch_grad, out_all).astype(bf16)
    mixed_grad = trade([mixed_grad[:, r * unit : (r + 1) * unit] for r in range(n_head)], "head")
    mixed_grad[1], out_hidden = lax.optimization_barrier(
        (mixed_grad[1], [hidden for _, hidden in grads_pair])
    )
    mixed_grad = in_order(mixed_grad, head_index)
    ff_first = [
        lax.psum_scatter(part, "batch", scatter_dimension=0, tiled=True) for part in ff_first
    ]
    downs = [ff_set[:, 2 * ff_pad : 3 * ff_pad] for ff_set in ff_sets]
    out_pair = sum(dot(hidden, down, NT) for hidden, down in zip(out_hidden, downs))
    out_pair, mixed_grad = lax.optimization_barrier((out_pair.astype(bf16), mixed_grad))
    out_swap = swap(out_pair, "head", 1)

    carry = None
    for part in reversed(range(SPANS)):
        if part == 0:
            carry, branch_rows, both_mid, both_cot, ff_grads = lax.optimization_barrier(
                (carry, branch_grad, both_mid, both_cot, ff_grads[:half])
            )
            ff_last = [weight_sums(both_mid, both_cot, *grads) for grads in reversed(ff_grads)]
            ff_last[-1] = jnp.concatenate(
                [ff_last[-1], dot(branch_rows.T, mixed_all).astype(bf16)], axis=1
            )
            carry, _, ff_first = lax.optimization_barrier((carry, ff_last, ff_first))
            ff_last = [
                lax.psum_scatter(rest, "batch", scatter_dimension=0, tiled=True)
                for rest in ff_last
            ]
        carry = mixer_backward(
            mixed_grad, raw, aux, segrow, saved[part], taps, bias, gain, carry,
            local_heads, BWD_CHUNKS, part, SPANS,
        )
    _, _, taps_grad, bias_grad, gain_grad, raw_low = carry
    raw_low, taps_grad, bias_grad, gain_grad, out_swap, sent = lax.optimization_barrier(
        (
            raw_low,
            taps_grad,
            bias_grad,
            gain_grad,
            out_swap,
            [swap(part, "head", bits_of(n_head)[-1]) for part in ff_first],
        )
    )
    total = dot(raw_low, proj_w, NT).astype(bf16)
    total, later_low = lax.optimization_barrier((total, raw_low))
    received = exchange(total.reshape(n_head, rows, width), "head")
    held = chip_sum(rows_in, later_low, "batch")
    mix_rows, late_tokens, late_scale, held = lax.optimization_barrier(
        (total, tokens, scale_all, held)
    )
    normed_all = late_tokens.reshape(length, width).astype(f32) * late_scale
    mix_gain_part = jnp.sum(mix_rows.astype(f32) * normed_all, axis=0)
    mix_total = plane_scatter(held, "batch")
    hiddens, _ = lax.optimization_barrier(([hidden for _, hidden in grads_own], held))
    out_own = sum(dot(own, down, NT) for own, down in zip(hiddens, downs))
    layer_output = (resid_mid + out_own + out_swap.astype(f32)).astype(bf16)
    ff_kept, _ = lax.optimization_barrier((ff_last, held))
    ff_total = [got.astype(f32) + kept.astype(f32) for got, kept in zip(sent, [kept[:, : 3 * ff_pad] for kept in ff_kept])]
    for bit in reversed(bits_of(n_head)[1:-1]):
        half = len(ff_total) // 2
        ff_total = [
            kept + swap(part.astype(bf16), "head", bit).astype(f32)
            for part, kept in zip(ff_total[:half], ff_total[half:])
        ]
    ff_total = ff_total[0].T
    done = (
        layer_output,
        mix_total[:, :unit],
        mix_total[:, unit : 3 * unit],
        mix_total[:, 3 * unit : 5 * unit],
        mix_total[:, 5 * unit : 6 * unit],
        mix_total[:, 6 * unit : 6 * unit + rate_weight.shape[1]],
        ff_total[:ff].T,
        ff_total[ff_pad : ff_pad + ff].T,
        ff_total[2 * ff_pad : 2 * ff_pad + ff],
    )

    own_bias_grad = bias_grad[0, : 3 * local_heads].reshape(local_heads, 3)[:, 2]
    small = [
        taps_grad[:, :unit].reshape(-1),
        taps_grad[:, unit : 3 * unit].reshape(-1),
        taps_grad[:, 3 * unit :].reshape(-1),
        own_bias_grad,
        gain_grad[0],
        mlp_gain_part,
        mix_gain_part,
    ]
    lengths = [part.shape[0] for part in small]
    packed, mix_total, out_sum = lax.optimization_barrier(
        (pack(small), mix_total, ff_kept[-1][:, 3 * ff_pad :])
    )
    out_blocks = trade([out_sum[:, r * unit : (r + 1) * unit] for r in range(n_head)], "head")
    for bit in bits_of(n_batch):
        packed = packed + swap(packed, "batch", bit)
    small = unpack(packed, lengths)

    def place_cols(table_shape, local_part, per_head):
        local_part = local_part.reshape(table_shape[:-1] + (-1,))
        return lax.dynamic_update_slice_in_dim(
            jnp.zeros(table_shape, f32),
            local_part,
            head_index * local_heads * per_head,
            axis=len(table_shape) - 1,
        ).reshape(-1)

    tables = [
        place_cols(conv_query.shape, small[0], HEAD_DIM),
        place_cols(conv_key.shape, small[1], 2 * HEAD_DIM),
        place_cols(conv_value.shape, small[2], 2 * HEAD_DIM),
        place_cols(decay_bias.shape, small[3], 1),
    ] + small[4:]
    lengths = [part.shape[0] for part in tables]
    packed, received, done = lax.optimization_barrier((pack(tables), received, done))
    for bit in bits_of(n_head):
        packed = packed + swap(packed, "head", bit)
    tables = unpack(packed, lengths)
    in_grad = jnp.sum(received.astype(f32), axis=0)
    in_back, _ = norm_back(in_grad, resid_in, row_scale(resid_in), mix_gain)
    input_grad = resid_grad + in_back

    out_total = sum(block.astype(f32) for block in out_blocks)
    return (
        done[0],
        input_grad,
        tables[6],
        *done[1:6],
        tables[0].reshape(conv_query.shape),
        tables[1].reshape(conv_key.shape),
        tables[2].reshape(conv_value.shape),
        tables[3],
        tables[4],
        out_total.T,
        tables[5],
        *done[6:],
    )


def pack(parts):
    flat = jnp.concatenate(parts)
    return jnp.pad(flat, (0, -flat.shape[0] % (8 * LANE))).reshape(-1, LANE)


def unpack(packed, lengths):
    flat = packed.reshape(-1)
    out, at = [], 0
    for size in lengths:
        out.append(flat[at : at + size])
        at += size
    return out


def solution(mesh):
    placed = (
        P(("batch", "head"), None),
        P(("batch", "head"), None),
        P("batch"),
        P(),
        P("batch", "head"),
        P("batch", "head"),
        P("batch", "head"),
        P("batch", "head"),
        P("batch", "head"),
        P(),
        P(),
        P(),
        P(),
        P(),
        P("head", "batch"),
        P(),
        P("batch", "head"),
        P("batch", "head"),
        P("head", "batch"),
    )
    return jax.shard_map(
        body,
        mesh=mesh,
        in_specs=placed,
        out_specs=(
            P(("batch", "head"), None),
            P(("batch", "head"), None),
            P(),
            P("batch", "head"),
            P("batch", "head"),
            P("batch", "head"),
            P("batch", "head"),
            P("batch", "head"),
            P(),
            P(),
            P(),
            P(),
            P(),
            P("head", "batch"),
            P(),
            P("batch", "head"),
            P("batch", "head"),
            P("head", "batch"),
        ),
        check_vma=False,
    )
```

```python
from functools import partial

import jax
import jax.numpy as jnp
from jax import lax
from jax.experimental import pallas as pl
from jax.experimental.pallas import tpu as pltpu
from jax.sharding import PartitionSpec as P

HEAD_DIM = 128
EPS = 1e-06
EXACT = lax.Precision.HIGHEST
HIGH = lax.Precision.HIGH
FAST = lax.Precision.DEFAULT
NN = ((1,), (0,))
NT = ((1,), (1,))
TN = ((0,), (0,))
LANE = 128
CHUNK = 64
ROWS = 2 * CHUNK
FWD_CHUNKS = 4
BWD_CHUNKS = 2
SPANS = 2


def mm(left, right, dims=NN, precision=HIGH):
    return lax.dot_general(
        left, right, (dims, ((), ())), precision=precision, preferred_element_type=jnp.float32
    )


def softplus(x):
    return jnp.maximum(x, 0.0) + jnp.log1p(jnp.exp(-jnp.abs(x)))


def chunk_masks():
    row = lax.broadcasted_iota(jnp.int32, (ROWS, ROWS), 0)
    col = lax.broadcasted_iota(jnp.int32, (ROWS, ROWS), 1)
    row_tok, col_tok = row & (CHUNK - 1), col & (CHUNK - 1)
    later = row_tok > col_tok
    same_tok = row_tok == col_tok
    pair = same_tok & (row > col)
    levels = []
    size = 1
    while size < CHUNK:
        upper = (row_tok & size) > (col_tok & size)
        together = (row_tok & (-2 * size)) == (col_tok & (-2 * size))
        levels.append(upper & together)
        size *= 2
    return row, col, later | same_tok, later | pair, pair, levels


def invert(lowers, ident, pair, levels, precision):
    inverses = [ident - jnp.where(pair, lower, 0.0) for lower in lowers]
    for level in levels:
        steps = [
            mm(jnp.where(level, lower, 0.0), inverse, NN, precision)
            for lower, inverse in zip(lowers, inverses)
        ]
        inverses = [
            inverse - mm(inverse, step, NN, precision) for inverse, step in zip(inverses, steps)
        ]
    return inverses


def col_sum(x):
    return jnp.sum(x, axis=-1, keepdims=True)


def twice(x):
    return jnp.concatenate([x, x], axis=0)


def unit_slices(heads, head):
    names = [heads + 2 * head, heads + 2 * head + 1, 3 * heads + 2 * head, 3 * heads + 2 * head + 1]
    names += [head, 5 * heads + head]
    return [slice(n * HEAD_DIM, (n + 1) * HEAD_DIM) for n in names]


def decays_of(cumul, cumul_t, beta_rows, aux, same, lane):
    c_tok = cumul[:, lane + 2 : lane + 3]
    c_end = cumul[CHUNK - 1 :, lane + 2 : lane + 3]
    decay = jnp.where(
        same, jnp.exp(jnp.minimum(twice(c_tok) - cumul_t[lane + 2 : lane + 3, :], 0.0)), 0.0
    )
    beta = jnp.concatenate(
        [beta_rows[:, lane : lane + 1], beta_rows[:, lane + 1 : lane + 2]], axis=0
    )
    start = aux[:, 0:1] * jnp.exp(c_tok)
    final = twice(aux[:, 1:2] * jnp.exp(c_end - c_tok))
    total = aux[CHUNK - 1 :, 0:1] * jnp.exp(c_end)
    return decay, beta, start, final, total


def fwd_kernel(
    heads, per_step, raw_ref, aux_ref, segrow_ref, taps_ref, bias_ref, gain_ref, mem_in, tail_in,
    mixed_ref, pre_ref, recall_ref, inv_ref, prox_ref, state_ref, move_ref, probe_ref,
    mem_ref, tail_ref, act_ref,
):
    width = HEAD_DIM
    block = per_step * CHUNK

    @pl.when(pl.program_id(0) == 0)
    def _():
        mem_ref[...] = mem_in[...]
        tail_ref[...] = tail_in[...]

    masks = [aux_ref[:, 2 + s : 3 + s] for s in range(3)]
    for tile in range(5 * heads):
        cols = slice(tile * width, (tile + 1) * width)
        raw = raw_ref[:, cols]
        joined = jnp.concatenate([tail_ref[:, cols], raw], axis=0)
        pre = raw * taps_ref[0:1, cols]
        for s in range(1, 4):
            shifted = pltpu.roll(joined, s, 0)[8:]
            pre = pre + shifted * masks[s - 1] * taps_ref[s : s + 1, cols]
        pre_ref[:, cols] = pre
        tail_ref[:, cols] = raw[block - 8 :]
        act = pre * jax.nn.sigmoid(pre)
        if tile < 3 * heads:
            act = act * lax.rsqrt(col_sum(act * act) + EPS)
        act_ref[:, cols] = act

    row, col, lower_eq, strict, pair, levels = chunk_masks()
    ident = (row == col).astype(jnp.float32)
    tri = (row[:CHUNK, :CHUNK] >= col[:CHUNK, :CHUNK]).astype(jnp.float32)
    rates = raw_ref[:, 6 * heads * width :]
    beta_tile = jax.nn.sigmoid(rates)
    log_tile = -softplus(rates + bias_ref[...])
    units = [(part, head) for part in range(per_step) for head in range(heads)]
    spans = [slice(part * CHUNK, (part + 1) * CHUNK) for part in range(per_step)]
    cumuls = [mm(tri, log_tile[rows], NN, EXACT) for rows in spans]
    cumul_ts = [twice(cumul).T for cumul in cumuls]
    sames = [
        (twice(aux_ref[rows, 8:9]) == segrow_ref[part]) & lower_eq
        for part, rows in enumerate(spans)
    ]
    keys, queries, decays, lowers, scores = [], [], [], [], []
    for part, head in units:
        k1, k2, v1, v2, q0, g0 = unit_slices(heads, head)
        rows = spans[part]
        key = jnp.concatenate([act_ref[rows, k1], act_ref[rows, k2]], axis=0)
        query = act_ref[rows, q0]
        decay = decays_of(
            cumuls[part], cumul_ts[part], beta_tile[rows], aux_ref[rows], sames[part], 3 * head
        )
        dots = mm(jnp.concatenate([key, query], axis=0), key, NT)
        keys.append(key)
        queries.append(query)
        decays.append(decay)
        lowers.append(jnp.where(strict, decay[1] * decay[0] * dots[:ROWS], 0.0))
        scores.append(decay[0][CHUNK:] * dots[ROWS:])
    inverses = invert(lowers, ident, pair, levels, HIGH)
    solved = []
    for u, (part, head) in enumerate(units):
        k1, k2, v1, v2, q0, g0 = unit_slices(heads, head)
        rows = spans[part]
        decay, beta, start, final, total = decays[u]
        inv_ref[u] = inverses[u]
        value = jnp.concatenate([act_ref[rows, v1], act_ref[rows, v2]], axis=0)
        solved.append(
            mm(
                inverses[u],
                jnp.concatenate([beta * value, beta * twice(start) * keys[u]], axis=1),
            )
        )
    moves = [mm(decays[u][3] * keys[u], solved[u], TN) for u in range(len(units))]
    reads = [mm(scores[u], solved[u]) for u in range(len(units))]
    for u, (part, head) in enumerate(units):
        memory = mem_ref[head]
        state_ref[u] = memory
        move_ref[u] = moves[u][:, width:]
        mem_ref[head] = (
            decays[u][4] * memory + moves[u][:, :width] - mm(moves[u][:, width:], memory)
        )
    for u, (part, head) in enumerate(units):
        probe = decays[u][2] * queries[u] - reads[u][:, width:]
        probe_ref[u] = probe
        seen = mm(jnp.concatenate([solved[u][:, width:], probe], axis=0), state_ref[u])
        prox_ref[u] = solved[u][:, :width] - seen[:ROWS]
        recall = reads[u][:, :width] + seen[ROWS:]
        rows = spans[part]
        cols = slice(head * width, (head + 1) * width)
        recall_ref[rows, cols] = recall
        scale = lax.rsqrt(jnp.mean(recall * recall, axis=-1, keepdims=True) + EPS)
        gate = raw_ref[rows, unit_slices(heads, head)[5]]
        mixed = recall * scale * gain_ref[...] * (gate * jax.nn.sigmoid(gate))
        mixed_ref[rows, cols] = mixed.astype(jnp.bfloat16)


def bwd_kernel(
    heads, per_step, grad_ref, raw_ref, aux_ref, segrow_ref, pre_ref, recall_ref, inv_ref,
    prox_ref, state_ref, move_ref, probe_ref, taps_ref, bias_ref, gain_ref,
    adj_in, head_in, taps_grad_in, bias_grad_in, gain_grad_in, low_in,
    low_ref, taps_grad_ref, bias_grad_ref, gain_grad_ref, adj_ref, head_ref,
    act_ref, norm_ref, dact_ref, keep_ref,
):
    width = HEAD_DIM
    block = per_step * CHUNK

    @pl.when(pl.program_id(0) == 0)
    def _():
        adj_ref[...] = adj_in[...]
        head_ref[...] = head_in[...]
        taps_grad_ref[...] = taps_grad_in[...]
        bias_grad_ref[...] = bias_grad_in[...]
        gain_grad_ref[...] = gain_grad_in[...]

    row, col, lower_eq, strict, pair, levels = chunk_masks()
    tri = (row[:CHUNK, :CHUNK] >= col[:CHUNK, :CHUNK]).astype(jnp.float32)
    tri_t = (row[:CHUNK, :CHUNK] <= col[:CHUNK, :CHUNK]).astype(jnp.float32)
    lanes = col[:CHUNK, :]
    rates = raw_ref[:, 6 * heads * width :]
    beta_tile = jax.nn.sigmoid(rates)
    keep_in = rates + bias_ref[...]
    log_tile = -softplus(keep_in)
    units = [(part, head) for part in reversed(range(per_step)) for head in range(heads)]
    spans = [slice(part * CHUNK, (part + 1) * CHUNK) for part in range(per_step)]
    cumuls = [mm(tri, log_tile[rows], NN, EXACT) for rows in spans]
    cumul_ts = [twice(cumul).T for cumul in cumuls]
    sames = [
        (twice(aux_ref[rows, 8:9]) == segrow_ref[part]) & lower_eq
        for part, rows in enumerate(spans)
    ]
    gain_total = jnp.zeros((1, width), jnp.float32)
    out_grads = []
    for part, head in units:
        rows = spans[part]
        q0, g0 = unit_slices(heads, head)[4:]
        recall = recall_ref[rows, q0]
        grad = grad_ref[rows, q0].astype(jnp.float32)
        gate = raw_ref[rows, g0]
        gate_sig = jax.nn.sigmoid(gate)
        silu_gate = gate * gate_sig
        scale = lax.rsqrt(jnp.mean(recall * recall, axis=-1, keepdims=True) + EPS)
        normed = recall * scale
        gain_total = gain_total + jnp.sum(grad * normed * silu_gate, axis=0, keepdims=True)
        weighted = grad * gain_ref[...]
        low_ref[rows, g0] = (
            weighted * normed * gate_sig * (1.0 + gate * (1.0 - gate_sig))
        ).astype(jnp.bfloat16)
        normed_grad = weighted * silu_gate
        out_grads.append(
            scale * (normed_grad - normed * jnp.mean(normed_grad * normed, axis=-1, keepdims=True))
        )
    gain_grad_ref[...] += gain_total
    reads = [
        mm(probe_ref[part * heads + head], out_grads[u], TN) for u, (part, head) in enumerate(units)
    ]
    for u, (part, head) in enumerate(units):
        spot = part * heads + head
        c_end = cumuls[part][CHUNK - 1 :, 3 * head + 2 : 3 * head + 3]
        total = aux_ref[(part + 1) * CHUNK - 1 : (part + 1) * CHUNK, 0:1] * jnp.exp(c_end)
        adjoint = adj_ref[head]
        keep_ref[spot] = adjoint
        adj_ref[head] = total * adjoint + reads[u] - mm(move_ref[spot], adjoint, TN)
    for tile in range(5 * heads):
        cols = slice(tile * width, (tile + 1) * width)
        pre = pre_ref[:, cols]
        act = pre * jax.nn.sigmoid(pre)
        if tile < 3 * heads:
            scale = lax.rsqrt(col_sum(act * act) + EPS)
            norm_ref[:, cols] = jnp.broadcast_to(scale, act.shape)
            act = act * scale
        act_ref[:, cols] = act
    keys, decays, dots = [], [], []
    for u, (part, head) in enumerate(units):
        k1, k2, v1, v2, q0, g0 = unit_slices(heads, head)
        rows = spans[part]
        key = jnp.concatenate([act_ref[rows, k1], act_ref[rows, k2]], axis=0)
        keys.append(key)
        decays.append(
            decays_of(
                cumuls[part], cumul_ts[part], beta_tile[rows], aux_ref[rows], sames[part], 3 * head
            )
        )
        dots.append(mm(jnp.concatenate([key, act_ref[rows, q0]], axis=0), key, NT))
    scores = [decays[u][0][CHUNK:] * dots[u][ROWS:] for u in range(len(units))]
    proxy_grads = [
        mm(scores[u], out_grads[u], TN)
        + mm(decays[u][3] * keys[u], keep_ref[part * heads + head])
        for u, (part, head) in enumerate(units)
    ]
    both_grads = [
        jnp.concatenate(
            [mm(inv_ref[part * heads + head], proxy_grads[u], TN), out_grads[u]], axis=0
        )
        for u, (part, head) in enumerate(units)
    ]
    outers = [
        mm(both_grads[u], prox_ref[part * heads + head], NT)
        for u, (part, head) in enumerate(units)
    ]
    throughs = [
        mm(both_grads[u], state_ref[part * heads + head], NT)
        for u, (part, head) in enumerate(units)
    ]
    finals = [
        decays[u][3] * mm(prox_ref[part * heads + head], keep_ref[part * heads + head], NT)
        for u, (part, head) in enumerate(units)
    ]
    score_grads, inners, beta_parts, log_cols = [], [], [], []
    for u, (part, head) in enumerate(units):
        decay, beta, start, final, total = decays[u]
        key_decay = jnp.where(strict, decay * dots[u][:ROWS], 0.0)
        lower_grad = -outers[u][:ROWS]
        beta_part = lower_grad * key_decay
        dots_grad = jnp.where(strict, lower_grad * beta * decay, 0.0)
        score_grad = outers[u][ROWS:] * decay[CHUNK:]
        log_part = beta_part * beta
        log_part = jnp.concatenate(
            [log_part[:CHUNK], log_part[CHUNK:] + outers[u][ROWS:] * scores[u]], axis=0
        )
        log_cols.append(col_sum(log_part - log_part.T))
        beta_parts.append(col_sum(beta_part))
        score_grads.append(score_grad)
        inners.append(
            mm(jnp.concatenate([dots_grad + dots_grad.T, score_grad], axis=0), keys[u])
        )
    zero = jnp.zeros((CHUNK, width), jnp.float32)
    beta_grads, cumul_grads, end_grads = [zero] * per_step, [zero] * per_step, [zero] * per_step
    for u, (part, head) in enumerate(units):
        k1, k2, v1, v2, q0, g0 = unit_slices(heads, head)
        rows = spans[part]
        spot = part * heads + head
        lane = 3 * head
        decay, beta, start, final, total = decays[u]
        through, final_part, right_grad = throughs[u], finals[u], both_grads[u][:ROWS]
        query = act_ref[rows, q0]
        value = jnp.concatenate([act_ref[rows, v1], act_ref[rows, v2]], axis=0)
        beta_start = beta * twice(start)
        key_through = col_sum(keys[u] * through[:ROWS])
        query_through = start * col_sum(query * through[ROWS:])
        final_sum = col_sum(keys[u] * final_part)
        key_grad = (
            inners[u][:ROWS]
            + mm(score_grads[u], query, TN)
            - beta_start * through[:ROWS]
            + final_part
        )
        dact_ref[rows, k1] = key_grad[:CHUNK]
        dact_ref[rows, k2] = key_grad[CHUNK:]
        value_grad = beta * right_grad
        dact_ref[rows, v1] = value_grad[:CHUNK]
        dact_ref[rows, v2] = value_grad[CHUNK:]
        dact_ref[rows, q0] = inners[u][ROWS:] + start * through[ROWS:]
        beta_col = col_sum(right_grad * value) - twice(start) * key_through + beta_parts[u]
        c_grad = log_cols[u] - beta_start * key_through - final_sum
        c_grad = c_grad[:CHUNK] + c_grad[CHUNK:] + query_through
        end_part = jnp.sum(final_sum, axis=0, keepdims=True) + total * jnp.sum(
            col_sum(state_ref[spot] * keep_ref[spot]), axis=0, keepdims=True
        )
        beta_grads[part] = jnp.where(
            lanes == lane,
            beta_col[:CHUNK],
            jnp.where(lanes == lane + 1, beta_col[CHUNK:], beta_grads[part]),
        )
        cumul_grads[part] = jnp.where(lanes == lane + 2, c_grad, cumul_grads[part])
        end_grads[part] = jnp.where(lanes == lane + 2, end_part, end_grads[part])
    bias_total = jnp.zeros((1, width), jnp.float32)
    for part, rows in enumerate(spans):
        log_grad = mm(tri_t, cumul_grads[part], NN, EXACT) + end_grads[part]
        beta_rows = beta_tile[rows]
        keep_grad = -log_grad * jax.nn.sigmoid(keep_in[rows]) * aux_ref[rows, 2:3]
        rate_grad = beta_grads[part] * beta_rows * (1.0 - beta_rows) + keep_grad
        bias_total = bias_total + jnp.sum(keep_grad, axis=0, keepdims=True)
        low_ref[rows, 6 * heads * width :] = rate_grad.astype(jnp.bfloat16)
    bias_grad_ref[...] += bias_total

    masks = [aux_ref[:, 5 + s : 6 + s] for s in range(3)]
    for tile in range(5 * heads):
        cols = slice(tile * width, (tile + 1) * width)
        pre = pre_ref[:, cols]
        sig = jax.nn.sigmoid(pre)
        grad = dact_ref[:, cols]
        if tile < 3 * heads:
            act = act_ref[:, cols]
            grad = norm_ref[:, cols] * (grad - act * col_sum(grad * act))
        grad = grad * sig * (1.0 + pre * (1.0 - sig))
        raw = raw_ref[:, cols]
        joined = jnp.concatenate([grad, head_ref[:, cols]], axis=0)
        head_ref[:, cols] = grad[:8]
        raw_grad = grad * taps_ref[0:1, cols]
        taps_grad_ref[0:1, cols] += jnp.sum(raw * grad, axis=0, keepdims=True)
        for s in range(1, 4):
            shifted = pltpu.roll(joined, block + 8 - s, 0)[:block] * masks[s - 1]
            raw_grad = raw_grad + shifted * taps_ref[s : s + 1, cols]
            taps_grad_ref[s : s + 1, cols] += jnp.sum(raw * shifted, axis=0, keepdims=True)
        low_ref[:, cols] = raw_grad.astype(jnp.bfloat16)


def token_aux(segments):
    length = segments.shape[0]
    seg = segments.astype(jnp.int32)
    chunks = seg.reshape(length // CHUNK, CHUNK)
    last = chunks[:, -1]
    before = jnp.concatenate([jnp.full((1,), -1, jnp.int32), last[:-1]])
    columns = [
        (chunks == before[:, None]).reshape(length),
        (chunks == last[:, None]).reshape(length),
    ]
    for s in range(1, 4):
        columns.append(jnp.pad(seg, (s, 0), constant_values=-1)[:length] == seg)
    for s in range(1, 4):
        columns.append(jnp.pad(seg, (0, s), constant_values=-1)[s:] == seg)
    columns.append(seg)
    columns += [jnp.zeros_like(seg)] * 7
    aux = jnp.stack([c.astype(jnp.float32) for c in columns], axis=1)
    row = chunks.astype(jnp.float32)
    return aux, jnp.concatenate([row, row], axis=1)[:, None, :]


def kernel_params():
    return pltpu.CompilerParams(
        dimension_semantics=("arbitrary",), vmem_limit_bytes=48 * 1024 * 1024
    )


def pin(array):
    return pltpu.with_memory_space_constraint(array, pltpu.HBM)


def whole(shape):
    zeros = (0,) * len(shape)
    return pl.BlockSpec(shape, lambda i: zeros)


def mixer_forward(raw, aux, segrow, taps, bias, gain, carry, heads, per_step, part, parts):
    width = HEAD_DIM
    block = per_step * CHUNK
    length = raw.shape[0] // parts
    steps = length // block
    first = part * steps
    units = per_step * heads
    total_units = steps * units
    cols = raw.shape[1]
    f32 = jnp.float32
    if carry is None:
        carry = (jnp.zeros((heads, width, width), f32), jnp.zeros((8, 5 * heads * width), f32))
    memory, tail = carry
    read = lambda i: (first + i, 0)
    read_cube = lambda i: (first + i, 0, 0)
    tiles = lambda i: (i, 0)
    cubes = lambda i: (i, 0, 0)
    unit_spec = pl.BlockSpec((units, ROWS, width), cubes)
    unit_shape = pltpu.HBM((total_units, ROWS, width), f32)
    out = pl.pallas_call(
        partial(fwd_kernel, heads, per_step),
        grid=(steps,),
        in_specs=[
            pl.BlockSpec((block, cols), read),
            pl.BlockSpec((block, 16), read),
            pl.BlockSpec((per_step, 1, ROWS), read_cube),
            whole(taps.shape),
            whole((1, width)),
            whole((1, width)),
            whole(memory.shape),
            whole(tail.shape),
        ],
        out_specs=[
            pl.BlockSpec((block, heads * width), tiles),
            pl.BlockSpec((block, 5 * heads * width), tiles),
            pl.BlockSpec((block, heads * width), tiles),
            unit_spec,
            unit_spec,
            unit_spec,
            unit_spec,
            pl.BlockSpec((units, CHUNK, width), cubes),
            whole(memory.shape),
            whole(tail.shape),
        ],
        out_shape=[
            jax.ShapeDtypeStruct((length, heads * width), jnp.bfloat16),
            pltpu.HBM((length, 5 * heads * width), f32),
            pltpu.HBM((length, heads * width), f32),
            unit_shape,
            unit_shape,
            unit_shape,
            unit_shape,
            pltpu.HBM((total_units, CHUNK, width), f32),
            jax.ShapeDtypeStruct(memory.shape, f32),
            jax.ShapeDtypeStruct(tail.shape, f32),
        ],
        scratch_shapes=[pltpu.VMEM((block, 5 * heads * width), f32)],
        compiler_params=kernel_params(),
        name="mixer_forward",
    )(raw, aux, segrow, taps, bias, gain, memory, tail)
    return out[0], out[1:8], (out[8], out[9])


def mixer_backward(grad, raw, aux, segrow, saved, taps, bias, gain, carry, heads, per_step, part, parts):
    width = HEAD_DIM
    block = per_step * CHUNK
    length = raw.shape[0] // parts
    steps = length // block
    last = (part + 1) * steps - 1
    units = per_step * heads
    cols = raw.shape[1]
    f32 = jnp.float32
    shapes = [
        (heads, width, width),
        (8, 5 * heads * width),
        taps.shape,
        (1, width),
        (1, width),
    ]
    low_shape = pltpu.HBM(raw.shape, jnp.bfloat16)
    if carry is None:
        carry = [jnp.zeros(shape, f32) for shape in shapes] + [jnp.zeros((16, width), jnp.bfloat16)]
        aliases = {}
    else:
        aliases = {19: 0}
    read = lambda i: (last - i, 0)
    read_cube = lambda i: (last - i, 0, 0)
    tiles, cubes = read, read_cube
    unit_spec = pl.BlockSpec((units, ROWS, width), cubes)
    out = pl.pallas_call(
        partial(bwd_kernel, heads, per_step),
        grid=(steps,),
        in_specs=[
            pl.BlockSpec((block, heads * width), read),
            pl.BlockSpec((block, cols), read),
            pl.BlockSpec((block, 16), read),
            pl.BlockSpec((per_step, 1, ROWS), read_cube),
            pl.BlockSpec((block, 5 * heads * width), tiles),
            pl.BlockSpec((block, heads * width), tiles),
            unit_spec,
            unit_spec,
            unit_spec,
            unit_spec,
            pl.BlockSpec((units, CHUNK, width), cubes),
            whole(taps.shape),
            whole((1, width)),
            whole((1, width)),
        ]
        + [whole(shape) for shape in shapes]
        + [pl.BlockSpec(memory_space=pl.ANY)],
        out_specs=[
            pl.BlockSpec((block, cols), read),
            whole(taps.shape),
            whole((1, width)),
            whole((1, width)),
            whole(shapes[0]),
            whole(shapes[1]),
        ],
        out_shape=[
            low_shape,
            jax.ShapeDtypeStruct(taps.shape, f32),
            jax.ShapeDtypeStruct((1, width), f32),
            jax.ShapeDtypeStruct((1, width), f32),
            jax.ShapeDtypeStruct(shapes[0], f32),
            jax.ShapeDtypeStruct(shapes[1], f32),
        ],
        scratch_shapes=[
            pltpu.VMEM((block, 5 * heads * width), f32),
            pltpu.VMEM((block, 3 * heads * width), f32),
            pltpu.VMEM((block, 5 * heads * width), f32),
            pltpu.VMEM((units, width, width), f32),
        ],
        input_output_aliases=aliases,
        compiler_params=kernel_params(),
        name="mixer_backward",
    )(grad, raw, aux, segrow, *[pin(array) for array in saved], taps, bias, gain, *carry)
    low, taps_grad, bias_grad, gain_grad, adjoint, head = out
    return [adjoint, head, taps_grad, bias_grad, gain_grad, low]


def up_to(x, multiple):
    return -(-x // multiple) * multiple


def row_scale(values):
    return lax.rsqrt(jnp.mean(values * values, axis=-1, keepdims=True) + EPS)


def norm_back(grad, values, scale, gain):
    normed = values * scale
    gain_grad = jnp.sum(grad * normed, axis=0)
    weighted = grad * gain
    value_grad = scale * (weighted - normed * jnp.mean(weighted * normed, axis=-1, keepdims=True))
    return (value_grad, gain_grad)


def dot(left, right, dims=NN):
    return lax.dot_general(left, right, (dims, ((), ())), preferred_element_type=jnp.float32)


def swap(x, axis, bit):
    size = lax.axis_size(axis)
    return lax.ppermute(x, axis, [(i, i ^ bit) for i in range(size)])


def exchange(blocks, axis):
    return lax.all_to_all(blocks, axis, split_axis=0, concat_axis=0, tiled=True)


def trade(blocks, axis):
    return [blocks[0]] + [swap(block, axis, r) for r, block in enumerate(blocks) if r > 0]


def rows_of(array, index, rows):
    return lax.dynamic_slice_in_dim(array, index * rows, rows, axis=0)


def in_order(blocks, index):
    rows = blocks[0].shape[0]
    out = jnp.zeros((rows * len(blocks),) + blocks[0].shape[1:], blocks[0].dtype)
    for r, block in enumerate(blocks):
        out = lax.dynamic_update_slice_in_dim(out, block, (index ^ r) * rows, axis=0)
    return out


def bits_of(size):
    return [1 << b for b in range(size.bit_length() - 1)]


def chip_sum(left, right, axis):
    size = lax.axis_size(axis)
    core = lax.axis_index(axis) % 2
    width = left.shape[1] // size
    even = jnp.concatenate(
        [left[:, j * width : (j + 1) * width] for j in range(0, size, 2)], axis=1
    )
    odd = jnp.concatenate([left[:, j * width : (j + 1) * width] for j in range(1, size, 2)], axis=1)
    got = swap(dot(jnp.where(core == 0, odd, even), right, TN).astype(jnp.bfloat16), axis, 1)
    held = dot(jnp.where(core == 0, even, odd), right, TN) + got.astype(jnp.float32)
    return held.astype(jnp.bfloat16)


def plane_scatter(held, axis):
    chips = lax.axis_size(axis) // 2
    chip = lax.axis_index(axis) // 2
    width = held.shape[0] // chips
    total = rows_of(held, chip, width).astype(jnp.float32)
    for step in range(1, chips):
        total = total + swap(rows_of(held, chip ^ step, width), axis, 2 * step).astype(jnp.float32)
    return total


def body(
    layer_input,
    cotangent,
    segments,
    mix_gain,
    query_weight,
    key_weight,
    value_weight,
    outgate_weight,
    rate_weight,
    conv_query,
    conv_key,
    conv_value,
    decay_bias,
    out_gain,
    out_weight,
    mlp_gain,
    gate_weight,
    up_weight,
    down_weight,
):
    f32, bf16 = jnp.float32, jnp.bfloat16
    head_index = lax.axis_index("head")
    n_head, n_batch = lax.axis_size("head"), lax.axis_size("batch")
    rows, width = layer_input.shape
    length = rows * n_head
    local_heads = query_weight.shape[1] // HEAD_DIM
    unit = local_heads * HEAD_DIM
    mix_cols = 6 * unit + HEAD_DIM
    ff = gate_weight.shape[1]
    ff_pad = up_to(ff, LANE)

    copies = jnp.broadcast_to(layer_input[None], (n_head,) + layer_input.shape)
    copies, query_weight, key_weight, value_weight, outgate_weight = lax.optimization_barrier(
        (copies, query_weight, key_weight, value_weight, outgate_weight)
    )
    tokens = exchange(copies, "head")
    own_mix = jnp.concatenate(
        [
            query_weight,
            key_weight,
            value_weight,
            outgate_weight,
            jnp.pad(rate_weight, ((0, 0), (0, HEAD_DIM - rate_weight.shape[1]))),
        ],
        axis=1,
    )
    proj_w = lax.all_gather(own_mix, "batch", axis=0, tiled=True)

    pad = ((0, 0), (0, ff_pad - ff))
    own_ff = jnp.concatenate(
        [jnp.pad(gate_weight, pad), jnp.pad(up_weight, pad), jnp.pad(down_weight.T, pad)], axis=1
    )
    ff_sets = [lax.all_gather(own_ff, "batch", axis=0, tiled=True)]
    def head_cols(table, per_head):
        return lax.dynamic_slice_in_dim(
            table, head_index * local_heads * per_head, local_heads * per_head, axis=table.ndim - 1
        )

    taps = jnp.concatenate(
        [
            head_cols(conv_query, HEAD_DIM),
            head_cols(conv_key, 2 * HEAD_DIM),
            head_cols(conv_value, 2 * HEAD_DIM),
        ],
        axis=1,
    )
    own_bias = head_cols(decay_bias, 1)
    bias = jnp.stack([jnp.zeros_like(own_bias), jnp.zeros_like(own_bias), own_bias], axis=1)
    bias = jnp.pad(bias.reshape(-1), (0, HEAD_DIM - 3 * local_heads))[None]
    aux, segrow = token_aux(segments)
    tokens, later_ff, later_out, later_cot, aux, segrow, taps, bias = lax.optimization_barrier(
        (tokens, own_ff, out_weight.T, cotangent, aux, segrow, taps, bias)
    )
    out_shards = trade([later_out] * n_head, "head")
    shards = [later_ff]
    for bit in bits_of(n_head)[1:]:
        shards = shards + [swap(shard, "head", bit) for shard in shards]
    pair_grad = swap(later_cot, "head", 1)

    all_in = tokens.reshape(length, width).astype(f32)
    scale_all = row_scale(all_in)
    rows_in = (all_in * scale_all * mix_gain).astype(bf16)
    rows_in, out_shards = lax.optimization_barrier((rows_in, out_shards))
    out_all = lax.all_gather(
        jnp.concatenate(out_shards, axis=1), "batch", axis=0, tiled=True
    )
    raw, ff_sets[0] = lax.optimization_barrier((dot(rows_in, proj_w), ff_sets[0]))

    gain = out_gain[None]
    consts = (raw, aux, segrow, taps, bias, gain)
    mixed_low, saved, _ = mixer_forward(*consts, None, local_heads, FWD_CHUNKS, 0, 1)
    mixed_low, pair_grad, shards = lax.optimization_barrier((mixed_low, pair_grad, shards))
    ff_sets += [lax.all_gather(shard, "batch", axis=0, tiled=True) for shard in shards[1:]]

    mixed_all = jnp.concatenate(
        trade([rows_of(mixed_low, head_index ^ r, rows) for r in range(n_head)], "head"), axis=1
    )
    resid_in = layer_input.astype(f32)
    resid_mid = resid_in + dot(mixed_all, out_all, NT)
    scale_mid = row_scale(resid_mid)
    normed_mid = (resid_mid * scale_mid * mlp_gain).astype(bf16)
    pair_mid = swap(normed_mid, "head", 1)

    def feed_forward(mid, cot):
        mid_part = None
        grads = []
        for ff_set in ff_sets:
            gate_up = dot(mid, ff_set[:, : 2 * ff_pad])
            gate_pre, up_pre = gate_up[:, :ff_pad], gate_up[:, ff_pad:]
            gate_sig = jax.nn.sigmoid(gate_pre)
            silu_gate = gate_pre * gate_sig
            hidden = (silu_gate * up_pre).astype(bf16)
            hidden_grad = dot(cot, ff_set[:, 2 * ff_pad : 3 * ff_pad])
            gate_grad = (
                hidden_grad * up_pre * gate_sig * (1.0 + gate_pre * (1.0 - gate_sig))
            ).astype(bf16)
            up_grad = (hidden_grad * silu_gate).astype(bf16)
            both_grad = jnp.concatenate([gate_grad, up_grad], axis=1)
            mid_here = dot(both_grad, ff_set[:, : 2 * ff_pad], NT)
            mid_part = mid_here if mid_part is None else mid_part + mid_here
            grads.append((both_grad, hidden))
        return mid_part, grads

    mid_own, grads_own = feed_forward(normed_mid, cotangent)
    pair_mid, grads_own[0] = lax.optimization_barrier((pair_mid, grads_own[0]))
    mid_pair, grads_pair = feed_forward(pair_mid, pair_grad)
    both_mid = jnp.concatenate([normed_mid, pair_mid], axis=0)
    both_cot = jnp.concatenate([cotangent, pair_grad], axis=0)

    def weight_sums(mid, cot, own, pair):
        both, hidden = [jnp.concatenate(pieces, axis=0) for pieces in zip(own, pair)]
        return jnp.concatenate([dot(mid, both, TN), dot(cot, hidden, TN)], axis=1).astype(bf16)

    half = len(ff_sets) // 2
    ff_grads = list(zip(grads_own, grads_pair))
    ff_first = [weight_sums(both_mid, both_cot, *grads) for grads in reversed(ff_grads[half:])]
    mid_swap, ff_first, mid_own = lax.optimization_barrier(
        (swap(mid_pair.astype(bf16), "head", 1), ff_first, mid_own)
    )
    mid_grad = mid_own + mid_swap.astype(f32)
    mid_back, mlp_gain_part = norm_back(mid_grad, resid_mid, scale_mid, mlp_gain)
    resid_grad = cotangent.astype(f32) + mid_back
    branch_grad = resid_grad.astype(bf16)
    mixed_grad = dot(branch_grad, out_all).astype(bf16)
    mixed_grad = trade([mixed_grad[:, r * unit : (r + 1) * unit] for r in range(n_head)], "head")
    mixed_grad[1], out_hidden = lax.optimization_barrier(
        (mixed_grad[1], [hidden for _, hidden in grads_pair])
    )
    mixed_grad = in_order(mixed_grad, head_index)
    ff_first = [
        lax.psum_scatter(part, "batch", scatter_dimension=0, tiled=True) for part in ff_first
    ]
    downs = [ff_set[:, 2 * ff_pad : 3 * ff_pad] for ff_set in ff_sets]
    out_pair = sum(dot(hidden, down, NT) for hidden, down in zip(out_hidden, downs))
    out_pair, mixed_grad = lax.optimization_barrier((out_pair.astype(bf16), mixed_grad))
    out_swap = swap(out_pair, "head", 1)

    carry = None
    for part in reversed(range(SPANS)):
        if part == 0:
            carry, branch_rows, both_mid, both_cot, ff_grads = lax.optimization_barrier(
                (carry, branch_grad, both_mid, both_cot, ff_grads[:half])
            )
            ff_last = [weight_sums(both_mid, both_cot, *grads) for grads in reversed(ff_grads)]
            ff_last[-1] = jnp.concatenate(
                [ff_last[-1], dot(branch_rows.T, mixed_all).astype(bf16)], axis=1
            )
            carry, _, ff_first = lax.optimization_barrier((carry, ff_last, ff_first))
            ff_last = [
                lax.psum_scatter(rest, "batch", scatter_dimension=0, tiled=True)
                for rest in ff_last
            ]
        carry = mixer_backward(
            mixed_grad, raw, aux, segrow, saved, taps, bias, gain, carry,
            local_heads, BWD_CHUNKS, part, SPANS,
        )
    _, _, taps_grad, bias_grad, gain_grad, raw_low = carry
    raw_low, taps_grad, bias_grad, gain_grad, out_swap, sent = lax.optimization_barrier(
        (
            raw_low,
            taps_grad,
            bias_grad,
            gain_grad,
            out_swap,
            [swap(part, "head", bits_of(n_head)[-1]) for part in ff_first],
        )
    )
    total = dot(raw_low, proj_w, NT).astype(bf16)
    total, later_low = lax.optimization_barrier((total, raw_low))
    received = exchange(total.reshape(n_head, rows, width), "head")
    held = chip_sum(rows_in, later_low, "batch")
    mix_rows, late_tokens, late_scale, held = lax.optimization_barrier(
        (total, tokens, scale_all, held)
    )
    normed_all = late_tokens.reshape(length, width).astype(f32) * late_scale
    mix_gain_part = jnp.sum(mix_rows.astype(f32) * normed_all, axis=0)
    mix_total = plane_scatter(held, "batch")
    hiddens, _ = lax.optimization_barrier(([hidden for _, hidden in grads_own], held))
    out_own = sum(dot(own, down, NT) for own, down in zip(hiddens, downs))
    layer_output = (resid_mid + out_own + out_swap.astype(f32)).astype(bf16)
    ff_kept, _ = lax.optimization_barrier((ff_last, held))
    ff_total = [got.astype(f32) + kept.astype(f32) for got, kept in zip(sent, [kept[:, : 3 * ff_pad] for kept in ff_kept])]
    for bit in reversed(bits_of(n_head)[1:-1]):
        half = len(ff_total) // 2
        ff_total = [
            kept + swap(part.astype(bf16), "head", bit).astype(f32)
            for part, kept in zip(ff_total[:half], ff_total[half:])
        ]
    ff_total = ff_total[0].T
    done = (
        layer_output,
        mix_total[:, :unit],
        mix_total[:, unit : 3 * unit],
        mix_total[:, 3 * unit : 5 * unit],
        mix_total[:, 5 * unit : 6 * unit],
        mix_total[:, 6 * unit : 6 * unit + rate_weight.shape[1]],
        ff_total[:ff].T,
        ff_total[ff_pad : ff_pad + ff].T,
        ff_total[2 * ff_pad : 2 * ff_pad + ff],
    )

    own_bias_grad = bias_grad[0, : 3 * local_heads].reshape(local_heads, 3)[:, 2]
    small = [
        taps_grad[:, :unit].reshape(-1),
        taps_grad[:, unit : 3 * unit].reshape(-1),
        taps_grad[:, 3 * unit :].reshape(-1),
        own_bias_grad,
        gain_grad[0],
        mlp_gain_part,
        mix_gain_part,
    ]
    lengths = [part.shape[0] for part in small]
    packed, mix_total, out_sum = lax.optimization_barrier(
        (pack(small), mix_total, ff_kept[-1][:, 3 * ff_pad :])
    )
    out_blocks = trade([out_sum[:, r * unit : (r + 1) * unit] for r in range(n_head)], "head")
    for bit in bits_of(n_batch):
        packed = packed + swap(packed, "batch", bit)
    small = unpack(packed, lengths)

    def place_cols(table_shape, local_part, per_head):
        local_part = local_part.reshape(table_shape[:-1] + (-1,))
        return lax.dynamic_update_slice_in_dim(
            jnp.zeros(table_shape, f32),
            local_part,
            head_index * local_heads * per_head,
            axis=len(table_shape) - 1,
        ).reshape(-1)

    tables = [
        place_cols(conv_query.shape, small[0], HEAD_DIM),
        place_cols(conv_key.shape, small[1], 2 * HEAD_DIM),
        place_cols(conv_value.shape, small[2], 2 * HEAD_DIM),
        place_cols(decay_bias.shape, small[3], 1),
    ] + small[4:]
    lengths = [part.shape[0] for part in tables]
    packed, received, done = lax.optimization_barrier((pack(tables), received, done))
    for bit in bits_of(n_head):
        packed = packed + swap(packed, "head", bit)
    tables = unpack(packed, lengths)
    in_grad = jnp.sum(received.astype(f32), axis=0)
    in_back, _ = norm_back(in_grad, resid_in, row_scale(resid_in), mix_gain)
    input_grad = resid_grad + in_back

    out_total = sum(block.astype(f32) for block in out_blocks)
    return (
        done[0],
        input_grad,
        tables[6],
        *done[1:6],
        tables[0].reshape(conv_query.shape),
        tables[1].reshape(conv_key.shape),
        tables[2].reshape(conv_value.shape),
        tables[3],
        tables[4],
        out_total.T,
        tables[5],
        *done[6:],
    )


def pack(parts):
    flat = jnp.concatenate(parts)
    return jnp.pad(flat, (0, -flat.shape[0] % (8 * LANE))).reshape(-1, LANE)


def unpack(packed, lengths):
    flat = packed.reshape(-1)
    out, at = [], 0
    for size in lengths:
        out.append(flat[at : at + size])
        at += size
    return out


def solution(mesh):
    placed = (
        P(("batch", "head"), None),
        P(("batch", "head"), None),
        P("batch"),
        P(),
        P("batch", "head"),
        P("batch", "head"),
        P("batch", "head"),
        P("batch", "head"),
        P("batch", "head"),
        P(),
        P(),
        P(),
        P(),
        P(),
        P("head", "batch"),
        P(),
        P("batch", "head"),
        P("batch", "head"),
        P("head", "batch"),
    )
    return jax.shard_map(
        body,
        mesh=mesh,
        in_specs=placed,
        out_specs=(
            P(("batch", "head"), None),
            P(("batch", "head"), None),
            P(),
            P("batch", "head"),
            P("batch", "head"),
            P("batch", "head"),
            P("batch", "head"),
            P("batch", "head"),
            P(),
            P(),
            P(),
            P(),
            P(),
            P("head", "batch"),
            P(),
            P("batch", "head"),
            P("batch", "head"),
            P("head", "batch"),
        ),
        check_vma=False,
    )
```

```python
from functools import partial

import jax
import jax.numpy as jnp
from jax import lax
from jax.experimental import pallas as pl
from jax.experimental.pallas import tpu as pltpu
from jax.sharding import PartitionSpec as P

HEAD_DIM = 128
EPS = 1e-06
EXACT = lax.Precision.HIGHEST
HIGH = lax.Precision.HIGH
FAST = lax.Precision.DEFAULT
NN = ((1,), (0,))
NT = ((1,), (1,))
TN = ((0,), (0,))
LANE = 128
CHUNK = 64
ROWS = 2 * CHUNK
FWD_CHUNKS = 4
BWD_CHUNKS = 2
SPANS = 2


def mm(left, right, dims=NN, precision=HIGH):
    return lax.dot_general(
        left, right, (dims, ((), ())), precision=precision, preferred_element_type=jnp.float32
    )


def softplus(x):
    return jnp.maximum(x, 0.0) + jnp.log1p(jnp.exp(-jnp.abs(x)))


def chunk_masks():
    row = lax.broadcasted_iota(jnp.int32, (ROWS, ROWS), 0)
    col = lax.broadcasted_iota(jnp.int32, (ROWS, ROWS), 1)
    row_tok, col_tok = row & (CHUNK - 1), col & (CHUNK - 1)
    later = row_tok > col_tok
    same_tok = row_tok == col_tok
    pair = same_tok & (row > col)
    levels = []
    size = 1
    while size < CHUNK:
        upper = (row_tok & size) > (col_tok & size)
        together = (row_tok & (-2 * size)) == (col_tok & (-2 * size))
        levels.append(upper & together)
        size *= 2
    return row, col, later | same_tok, later | pair, pair, levels


def invert(lowers, ident, pair, levels, precision):
    inverses = [ident - jnp.where(pair, lower, 0.0) for lower in lowers]
    for level in levels:
        steps = [
            mm(jnp.where(level, lower, 0.0), inverse, NN, precision)
            for lower, inverse in zip(lowers, inverses)
        ]
        inverses = [
            inverse - mm(inverse, step, NN, precision) for inverse, step in zip(inverses, steps)
        ]
    return inverses


def col_sum(x):
    return jnp.sum(x, axis=-1, keepdims=True)


def twice(x):
    return jnp.concatenate([x, x], axis=0)


def unit_slices(heads, head):
    names = [heads + 2 * head, heads + 2 * head + 1, 3 * heads + 2 * head, 3 * heads + 2 * head + 1]
    names += [head, 5 * heads + head]
    return [slice(n * HEAD_DIM, (n + 1) * HEAD_DIM) for n in names]


def decays_of(cumul, cumul_t, beta_rows, aux, same, lane):
    c_tok = cumul[:, lane + 2 : lane + 3]
    c_end = cumul[CHUNK - 1 :, lane + 2 : lane + 3]
    decay = jnp.where(
        same, jnp.exp(jnp.minimum(twice(c_tok) - cumul_t[lane + 2 : lane + 3, :], 0.0)), 0.0
    )
    beta = jnp.concatenate(
        [beta_rows[:, lane : lane + 1], beta_rows[:, lane + 1 : lane + 2]], axis=0
    )
    start = aux[:, 0:1] * jnp.exp(c_tok)
    final = twice(aux[:, 1:2] * jnp.exp(c_end - c_tok))
    total = aux[CHUNK - 1 :, 0:1] * jnp.exp(c_end)
    return decay, beta, start, final, total


def fwd_kernel(
    heads, per_step, raw_ref, aux_ref, segrow_ref, taps_ref, bias_ref, gain_ref, mem_in, tail_in,
    mixed_ref, pre_ref, recall_ref, inv_ref, prox_ref, state_ref, move_ref, probe_ref,
    mem_ref, tail_ref, act_ref,
):
    width = HEAD_DIM
    block = per_step * CHUNK

    @pl.when(pl.program_id(0) == 0)
    def _():
        mem_ref[...] = mem_in[...]
        tail_ref[...] = tail_in[...]

    masks = [aux_ref[:, 2 + s : 3 + s] for s in range(3)]
    for tile in range(5 * heads):
        cols = slice(tile * width, (tile + 1) * width)
        raw = raw_ref[:, cols]
        joined = jnp.concatenate([tail_ref[:, cols], raw], axis=0)
        pre = raw * taps_ref[0:1, cols]
        for s in range(1, 4):
            shifted = pltpu.roll(joined, s, 0)[8:]
            pre = pre + shifted * masks[s - 1] * taps_ref[s : s + 1, cols]
        pre_ref[:, cols] = pre
        tail_ref[:, cols] = raw[block - 8 :]
        act = pre * jax.nn.sigmoid(pre)
        if tile < 3 * heads:
            act = act * lax.rsqrt(col_sum(act * act) + EPS)
        act_ref[:, cols] = act

    row, col, lower_eq, strict, pair, levels = chunk_masks()
    ident = (row == col).astype(jnp.float32)
    tri = (row[:CHUNK, :CHUNK] >= col[:CHUNK, :CHUNK]).astype(jnp.float32)
    rates = raw_ref[:, 6 * heads * width :]
    beta_tile = jax.nn.sigmoid(rates)
    log_tile = -softplus(rates + bias_ref[...])
    units = [(part, head) for part in range(per_step) for head in range(heads)]
    spans = [slice(part * CHUNK, (part + 1) * CHUNK) for part in range(per_step)]
    cumuls = [mm(tri, log_tile[rows], NN, EXACT) for rows in spans]
    cumul_ts = [twice(cumul).T for cumul in cumuls]
    sames = [
        (twice(aux_ref[rows, 8:9]) == segrow_ref[part]) & lower_eq
        for part, rows in enumerate(spans)
    ]
    keys, queries, decays, lowers, scores = [], [], [], [], []
    for part, head in units:
        k1, k2, v1, v2, q0, g0 = unit_slices(heads, head)
        rows = spans[part]
        key = jnp.concatenate([act_ref[rows, k1], act_ref[rows, k2]], axis=0)
        query = act_ref[rows, q0]
        decay = decays_of(
            cumuls[part], cumul_ts[part], beta_tile[rows], aux_ref[rows], sames[part], 3 * head
        )
        dots = mm(jnp.concatenate([key, query], axis=0), key, NT)
        keys.append(key)
        queries.append(query)
        decays.append(decay)
        lowers.append(jnp.where(strict, decay[1] * decay[0] * dots[:ROWS], 0.0))
        scores.append(decay[0][CHUNK:] * dots[ROWS:])
    inverses = invert(lowers, ident, pair, levels, HIGH)
    solved = []
    for u, (part, head) in enumerate(units):
        k1, k2, v1, v2, q0, g0 = unit_slices(heads, head)
        rows = spans[part]
        decay, beta, start, final, total = decays[u]
        inv_ref[u] = inverses[u]
        value = jnp.concatenate([act_ref[rows, v1], act_ref[rows, v2]], axis=0)
        solved.append(
            mm(
                inverses[u],
                jnp.concatenate([beta * value, beta * twice(start) * keys[u]], axis=1),
            )
        )
    moves = [mm(decays[u][3] * keys[u], solved[u], TN) for u in range(len(units))]
    reads = [mm(scores[u], solved[u]) for u in range(len(units))]
    for u, (part, head) in enumerate(units):
        memory = mem_ref[head]
        state_ref[u] = memory
        move_ref[u] = moves[u][:, width:]
        mem_ref[head] = (
            decays[u][4] * memory + moves[u][:, :width] - mm(moves[u][:, width:], memory)
        )
    for u, (part, head) in enumerate(units):
        probe = decays[u][2] * queries[u] - reads[u][:, width:]
        probe_ref[u] = probe
        seen = mm(jnp.concatenate([solved[u][:, width:], probe], axis=0), state_ref[u])
        prox_ref[u] = solved[u][:, :width] - seen[:ROWS]
        recall = reads[u][:, :width] + seen[ROWS:]
        rows = spans[part]
        cols = slice(head * width, (head + 1) * width)
        recall_ref[rows, cols] = recall
        scale = lax.rsqrt(jnp.mean(recall * recall, axis=-1, keepdims=True) + EPS)
        gate = raw_ref[rows, unit_slices(heads, head)[5]]
        mixed = recall * scale * gain_ref[...] * (gate * jax.nn.sigmoid(gate))
        mixed_ref[rows, cols] = mixed.astype(jnp.bfloat16)


def bwd_kernel(
    heads, per_step, grad_ref, raw_ref, aux_ref, segrow_ref, pre_ref, recall_ref, inv_ref,
    prox_ref, state_ref, move_ref, probe_ref, taps_ref, bias_ref, gain_ref,
    adj_in, head_in, taps_grad_in, bias_grad_in, gain_grad_in, low_in,
    low_ref, taps_grad_ref, bias_grad_ref, gain_grad_ref, adj_ref, head_ref,
    act_ref, norm_ref, dact_ref, keep_ref,
):
    width = HEAD_DIM
    block = per_step * CHUNK

    @pl.when(pl.program_id(0) == 0)
    def _():
        adj_ref[...] = adj_in[...]
        head_ref[...] = head_in[...]
        taps_grad_ref[...] = taps_grad_in[...]
        bias_grad_ref[...] = bias_grad_in[...]
        gain_grad_ref[...] = gain_grad_in[...]

    row, col, lower_eq, strict, pair, levels = chunk_masks()
    tri = (row[:CHUNK, :CHUNK] >= col[:CHUNK, :CHUNK]).astype(jnp.float32)
    tri_t = (row[:CHUNK, :CHUNK] <= col[:CHUNK, :CHUNK]).astype(jnp.float32)
    lanes = col[:CHUNK, :]
    rates = raw_ref[:, 6 * heads * width :]
    beta_tile = jax.nn.sigmoid(rates)
    keep_in = rates + bias_ref[...]
    log_tile = -softplus(keep_in)
    units = [(part, head) for part in reversed(range(per_step)) for head in range(heads)]
    spans = [slice(part * CHUNK, (part + 1) * CHUNK) for part in range(per_step)]
    cumuls = [mm(tri, log_tile[rows], NN, EXACT) for rows in spans]
    cumul_ts = [twice(cumul).T for cumul in cumuls]
    sames = [
        (twice(aux_ref[rows, 8:9]) == segrow_ref[part]) & lower_eq
        for part, rows in enumerate(spans)
    ]
    gain_total = jnp.zeros((1, width), jnp.float32)
    out_grads = []
    for part, head in units:
        rows = spans[part]
        q0, g0 = unit_slices(heads, head)[4:]
        recall = recall_ref[rows, q0]
        grad = grad_ref[rows, q0].astype(jnp.float32)
        gate = raw_ref[rows, g0]
        gate_sig = jax.nn.sigmoid(gate)
        silu_gate = gate * gate_sig
        scale = lax.rsqrt(jnp.mean(recall * recall, axis=-1, keepdims=True) + EPS)
        normed = recall * scale
        gain_total = gain_total + jnp.sum(grad * normed * silu_gate, axis=0, keepdims=True)
        weighted = grad * gain_ref[...]
        low_ref[rows, g0] = (
            weighted * normed * gate_sig * (1.0 + gate * (1.0 - gate_sig))
        ).astype(jnp.bfloat16)
        normed_grad = weighted * silu_gate
        out_grads.append(
            scale * (normed_grad - normed * jnp.mean(normed_grad * normed, axis=-1, keepdims=True))
        )
    gain_grad_ref[...] += gain_total
    reads = [
        mm(probe_ref[part * heads + head], out_grads[u], TN) for u, (part, head) in enumerate(units)
    ]
    for u, (part, head) in enumerate(units):
        spot = part * heads + head
        c_end = cumuls[part][CHUNK - 1 :, 3 * head + 2 : 3 * head + 3]
        total = aux_ref[(part + 1) * CHUNK - 1 : (part + 1) * CHUNK, 0:1] * jnp.exp(c_end)
        adjoint = adj_ref[head]
        keep_ref[spot] = adjoint
        adj_ref[head] = total * adjoint + reads[u] - mm(move_ref[spot], adjoint, TN)
    for tile in range(5 * heads):
        cols = slice(tile * width, (tile + 1) * width)
        pre = pre_ref[:, cols]
        act = pre * jax.nn.sigmoid(pre)
        if tile < 3 * heads:
            scale = lax.rsqrt(col_sum(act * act) + EPS)
            norm_ref[:, cols] = jnp.broadcast_to(scale, act.shape)
            act = act * scale
        act_ref[:, cols] = act
    keys, decays, dots = [], [], []
    for u, (part, head) in enumerate(units):
        k1, k2, v1, v2, q0, g0 = unit_slices(heads, head)
        rows = spans[part]
        key = jnp.concatenate([act_ref[rows, k1], act_ref[rows, k2]], axis=0)
        keys.append(key)
        decays.append(
            decays_of(
                cumuls[part], cumul_ts[part], beta_tile[rows], aux_ref[rows], sames[part], 3 * head
            )
        )
        dots.append(mm(jnp.concatenate([key, act_ref[rows, q0]], axis=0), key, NT))
    scores = [decays[u][0][CHUNK:] * dots[u][ROWS:] for u in range(len(units))]
    proxy_grads = [
        mm(scores[u], out_grads[u], TN)
        + mm(decays[u][3] * keys[u], keep_ref[part * heads + head])
        for u, (part, head) in enumerate(units)
    ]
    both_grads = [
        jnp.concatenate(
            [mm(inv_ref[part * heads + head], proxy_grads[u], TN), out_grads[u]], axis=0
        )
        for u, (part, head) in enumerate(units)
    ]
    outers = [
        mm(both_grads[u], prox_ref[part * heads + head], NT)
        for u, (part, head) in enumerate(units)
    ]
    throughs = [
        mm(both_grads[u], state_ref[part * heads + head], NT)
        for u, (part, head) in enumerate(units)
    ]
    finals = [
        decays[u][3] * mm(prox_ref[part * heads + head], keep_ref[part * heads + head], NT)
        for u, (part, head) in enumerate(units)
    ]
    score_grads, inners, beta_parts, log_cols = [], [], [], []
    for u, (part, head) in enumerate(units):
        decay, beta, start, final, total = decays[u]
        key_decay = jnp.where(strict, decay * dots[u][:ROWS], 0.0)
        lower_grad = -outers[u][:ROWS]
        beta_part = lower_grad * key_decay
        dots_grad = jnp.where(strict, lower_grad * beta * decay, 0.0)
        score_grad = outers[u][ROWS:] * decay[CHUNK:]
        log_part = beta_part * beta
        log_part = jnp.concatenate(
            [log_part[:CHUNK], log_part[CHUNK:] + outers[u][ROWS:] * scores[u]], axis=0
        )
        log_cols.append(col_sum(log_part - log_part.T))
        beta_parts.append(col_sum(beta_part))
        score_grads.append(score_grad)
        inners.append(
            mm(jnp.concatenate([dots_grad + dots_grad.T, score_grad], axis=0), keys[u])
        )
    zero = jnp.zeros((CHUNK, width), jnp.float32)
    beta_grads, cumul_grads, end_grads = [zero] * per_step, [zero] * per_step, [zero] * per_step
    for u, (part, head) in enumerate(units):
        k1, k2, v1, v2, q0, g0 = unit_slices(heads, head)
        rows = spans[part]
        spot = part * heads + head
        lane = 3 * head
        decay, beta, start, final, total = decays[u]
        through, final_part, right_grad = throughs[u], finals[u], both_grads[u][:ROWS]
        query = act_ref[rows, q0]
        value = jnp.concatenate([act_ref[rows, v1], act_ref[rows, v2]], axis=0)
        beta_start = beta * twice(start)
        key_through = col_sum(keys[u] * through[:ROWS])
        query_through = start * col_sum(query * through[ROWS:])
        final_sum = col_sum(keys[u] * final_part)
        key_grad = (
            inners[u][:ROWS]
            + mm(score_grads[u], query, TN)
            - beta_start * through[:ROWS]
            + final_part
        )
        dact_ref[rows, k1] = key_grad[:CHUNK]
        dact_ref[rows, k2] = key_grad[CHUNK:]
        value_grad = beta * right_grad
        dact_ref[rows, v1] = value_grad[:CHUNK]
        dact_ref[rows, v2] = value_grad[CHUNK:]
        dact_ref[rows, q0] = inners[u][ROWS:] + start * through[ROWS:]
        beta_col = col_sum(right_grad * value) - twice(start) * key_through + beta_parts[u]
        c_grad = log_cols[u] - beta_start * key_through - final_sum
        c_grad = c_grad[:CHUNK] + c_grad[CHUNK:] + query_through
        end_part = jnp.sum(final_sum, axis=0, keepdims=True) + total * jnp.sum(
            col_sum(state_ref[spot] * keep_ref[spot]), axis=0, keepdims=True
        )
        beta_grads[part] = jnp.where(
            lanes == lane,
            beta_col[:CHUNK],
            jnp.where(lanes == lane + 1, beta_col[CHUNK:], beta_grads[part]),
        )
        cumul_grads[part] = jnp.where(lanes == lane + 2, c_grad, cumul_grads[part])
        end_grads[part] = jnp.where(lanes == lane + 2, end_part, end_grads[part])
    bias_total = jnp.zeros((1, width), jnp.float32)
    for part, rows in enumerate(spans):
        log_grad = mm(tri_t, cumul_grads[part], NN, EXACT) + end_grads[part]
        beta_rows = beta_tile[rows]
        keep_grad = -log_grad * jax.nn.sigmoid(keep_in[rows]) * aux_ref[rows, 2:3]
        rate_grad = beta_grads[part] * beta_rows * (1.0 - beta_rows) + keep_grad
        bias_total = bias_total + jnp.sum(keep_grad, axis=0, keepdims=True)
        low_ref[rows, 6 * heads * width :] = rate_grad.astype(jnp.bfloat16)
    bias_grad_ref[...] += bias_total

    masks = [aux_ref[:, 5 + s : 6 + s] for s in range(3)]
    for tile in range(5 * heads):
        cols = slice(tile * width, (tile + 1) * width)
        pre = pre_ref[:, cols]
        sig = jax.nn.sigmoid(pre)
        grad = dact_ref[:, cols]
        if tile < 3 * heads:
            act = act_ref[:, cols]
            grad = norm_ref[:, cols] * (grad - act * col_sum(grad * act))
        grad = grad * sig * (1.0 + pre * (1.0 - sig))
        raw = raw_ref[:, cols]
        joined = jnp.concatenate([grad, head_ref[:, cols]], axis=0)
        head_ref[:, cols] = grad[:8]
        raw_grad = grad * taps_ref[0:1, cols]
        taps_grad_ref[0:1, cols] += jnp.sum(raw * grad, axis=0, keepdims=True)
        for s in range(1, 4):
            shifted = pltpu.roll(joined, block + 8 - s, 0)[:block] * masks[s - 1]
            raw_grad = raw_grad + shifted * taps_ref[s : s + 1, cols]
            taps_grad_ref[s : s + 1, cols] += jnp.sum(raw * shifted, axis=0, keepdims=True)
        low_ref[:, cols] = raw_grad.astype(jnp.bfloat16)


def token_aux(segments):
    length = segments.shape[0]
    seg = segments.astype(jnp.int32)
    chunks = seg.reshape(length // CHUNK, CHUNK)
    last = chunks[:, -1]
    before = jnp.concatenate([jnp.full((1,), -1, jnp.int32), last[:-1]])
    columns = [
        (chunks == before[:, None]).reshape(length),
        (chunks == last[:, None]).reshape(length),
    ]
    for s in range(1, 4):
        columns.append(jnp.pad(seg, (s, 0), constant_values=-1)[:length] == seg)
    for s in range(1, 4):
        columns.append(jnp.pad(seg, (0, s), constant_values=-1)[s:] == seg)
    columns.append(seg)
    columns += [jnp.zeros_like(seg)] * 7
    aux = jnp.stack([c.astype(jnp.float32) for c in columns], axis=1)
    row = chunks.astype(jnp.float32)
    return aux, jnp.concatenate([row, row], axis=1)[:, None, :]


def kernel_params():
    return pltpu.CompilerParams(
        dimension_semantics=("arbitrary",), vmem_limit_bytes=48 * 1024 * 1024
    )


def pin(array):
    return pltpu.with_memory_space_constraint(array, pltpu.HBM)


def whole(shape):
    zeros = (0,) * len(shape)
    return pl.BlockSpec(shape, lambda i: zeros)


def mixer_forward(raw, aux, segrow, taps, bias, gain, carry, heads, per_step, part, parts):
    width = HEAD_DIM
    block = per_step * CHUNK
    length = raw.shape[0] // parts
    steps = length // block
    first = part * steps
    units = per_step * heads
    total_units = steps * units
    cols = raw.shape[1]
    f32 = jnp.float32
    if carry is None:
        carry = (jnp.zeros((heads, width, width), f32), jnp.zeros((8, 5 * heads * width), f32))
    memory, tail = carry
    read = lambda i: (first + i, 0)
    read_cube = lambda i: (first + i, 0, 0)
    tiles = lambda i: (i, 0)
    cubes = lambda i: (i, 0, 0)
    unit_spec = pl.BlockSpec((units, ROWS, width), cubes)
    unit_shape = pltpu.HBM((total_units, ROWS, width), f32)
    out = pl.pallas_call(
        partial(fwd_kernel, heads, per_step),
        grid=(steps,),
        in_specs=[
            pl.BlockSpec((block, cols), read),
            pl.BlockSpec((block, 16), read),
            pl.BlockSpec((per_step, 1, ROWS), read_cube),
            whole(taps.shape),
            whole((1, width)),
            whole((1, width)),
            whole(memory.shape),
            whole(tail.shape),
        ],
        out_specs=[
            pl.BlockSpec((block, heads * width), tiles),
            pl.BlockSpec((block, 5 * heads * width), tiles),
            pl.BlockSpec((block, heads * width), tiles),
            unit_spec,
            unit_spec,
            unit_spec,
            unit_spec,
            pl.BlockSpec((units, CHUNK, width), cubes),
            whole(memory.shape),
            whole(tail.shape),
        ],
        out_shape=[
            jax.ShapeDtypeStruct((length, heads * width), jnp.bfloat16),
            pltpu.HBM((length, 5 * heads * width), f32),
            pltpu.HBM((length, heads * width), f32),
            unit_shape,
            unit_shape,
            unit_shape,
            unit_shape,
            pltpu.HBM((total_units, CHUNK, width), f32),
            jax.ShapeDtypeStruct(memory.shape, f32),
            jax.ShapeDtypeStruct(tail.shape, f32),
        ],
        scratch_shapes=[pltpu.VMEM((block, 5 * heads * width), f32)],
        compiler_params=kernel_params(),
        name="mixer_forward",
    )(raw, aux, segrow, taps, bias, gain, memory, tail)
    return out[0], out[1:8], (out[8], out[9])


def mixer_backward(grad, raw, aux, segrow, saved, taps, bias, gain, carry, heads, per_step, part, parts):
    width = HEAD_DIM
    block = per_step * CHUNK
    length = raw.shape[0] // parts
    steps = length // block
    last = (part + 1) * steps - 1
    units = per_step * heads
    cols = raw.shape[1]
    f32 = jnp.float32
    shapes = [
        (heads, width, width),
        (8, 5 * heads * width),
        taps.shape,
        (1, width),
        (1, width),
    ]
    low_shape = pltpu.HBM(raw.shape, jnp.bfloat16)
    if carry is None:
        carry = [jnp.zeros(shape, f32) for shape in shapes] + [jnp.zeros((16, width), jnp.bfloat16)]
        aliases = {}
    else:
        aliases = {19: 0}
    read = lambda i: (last - i, 0)
    read_cube = lambda i: (last - i, 0, 0)
    tiles, cubes = read, read_cube
    unit_spec = pl.BlockSpec((units, ROWS, width), cubes)
    out = pl.pallas_call(
        partial(bwd_kernel, heads, per_step),
        grid=(steps,),
        in_specs=[
            pl.BlockSpec((block, heads * width), read),
            pl.BlockSpec((block, cols), read),
            pl.BlockSpec((block, 16), read),
            pl.BlockSpec((per_step, 1, ROWS), read_cube),
            pl.BlockSpec((block, 5 * heads * width), tiles),
            pl.BlockSpec((block, heads * width), tiles),
            unit_spec,
            unit_spec,
            unit_spec,
            unit_spec,
            pl.BlockSpec((units, CHUNK, width), cubes),
            whole(taps.shape),
            whole((1, width)),
            whole((1, width)),
        ]
        + [whole(shape) for shape in shapes]
        + [pl.BlockSpec(memory_space=pl.ANY)],
        out_specs=[
            pl.BlockSpec((block, cols), read),
            whole(taps.shape),
            whole((1, width)),
            whole((1, width)),
            whole(shapes[0]),
            whole(shapes[1]),
        ],
        out_shape=[
            low_shape,
            jax.ShapeDtypeStruct(taps.shape, f32),
            jax.ShapeDtypeStruct((1, width), f32),
            jax.ShapeDtypeStruct((1, width), f32),
            jax.ShapeDtypeStruct(shapes[0], f32),
            jax.ShapeDtypeStruct(shapes[1], f32),
        ],
        scratch_shapes=[
            pltpu.VMEM((block, 5 * heads * width), f32),
            pltpu.VMEM((block, 3 * heads * width), f32),
            pltpu.VMEM((block, 5 * heads * width), f32),
            pltpu.VMEM((units, width, width), f32),
        ],
        input_output_aliases=aliases,
        compiler_params=kernel_params(),
        name="mixer_backward",
    )(grad, raw, aux, segrow, *[pin(array) for array in saved], taps, bias, gain, *carry)
    low, taps_grad, bias_grad, gain_grad, adjoint, head = out
    return [adjoint, head, taps_grad, bias_grad, gain_grad, low]


def up_to(x, multiple):
    return -(-x // multiple) * multiple


def row_scale(values):
    return lax.rsqrt(jnp.mean(values * values, axis=-1, keepdims=True) + EPS)


def norm_back(grad, values, scale, gain):
    normed = values * scale
    gain_grad = jnp.sum(grad * normed, axis=0)
    weighted = grad * gain
    value_grad = scale * (weighted - normed * jnp.mean(weighted * normed, axis=-1, keepdims=True))
    return (value_grad, gain_grad)


def dot(left, right, dims=NN):
    return lax.dot_general(left, right, (dims, ((), ())), preferred_element_type=jnp.float32)


def swap(x, axis, bit):
    size = lax.axis_size(axis)
    return lax.ppermute(x, axis, [(i, i ^ bit) for i in range(size)])


def exchange(blocks, axis):
    return lax.all_to_all(blocks, axis, split_axis=0, concat_axis=0, tiled=True)


def trade(blocks, axis):
    return [blocks[0]] + [swap(block, axis, r) for r, block in enumerate(blocks) if r > 0]


def rows_of(array, index, rows):
    return lax.dynamic_slice_in_dim(array, index * rows, rows, axis=0)


def in_order(blocks, index):
    rows = blocks[0].shape[0]
    out = jnp.zeros((rows * len(blocks),) + blocks[0].shape[1:], blocks[0].dtype)
    for r, block in enumerate(blocks):
        out = lax.dynamic_update_slice_in_dim(out, block, (index ^ r) * rows, axis=0)
    return out


def bits_of(size):
    return [1 << b for b in range(size.bit_length() - 1)]


def chip_sum(left, right, axis):
    size = lax.axis_size(axis)
    core = lax.axis_index(axis) % 2
    width = left.shape[1] // size
    even = jnp.concatenate(
        [left[:, j * width : (j + 1) * width] for j in range(0, size, 2)], axis=1
    )
    odd = jnp.concatenate([left[:, j * width : (j + 1) * width] for j in range(1, size, 2)], axis=1)
    got = swap(dot(jnp.where(core == 0, odd, even), right, TN).astype(jnp.bfloat16), axis, 1)
    held = dot(jnp.where(core == 0, even, odd), right, TN) + got.astype(jnp.float32)
    return held.astype(jnp.bfloat16)


def plane_scatter(held, axis):
    chips = lax.axis_size(axis) // 2
    chip = lax.axis_index(axis) // 2
    width = held.shape[0] // chips
    total = rows_of(held, chip, width).astype(jnp.float32)
    for step in range(1, chips):
        total = total + swap(rows_of(held, chip ^ step, width), axis, 2 * step).astype(jnp.float32)
    return total


def body(
    layer_input,
    cotangent,
    segments,
    mix_gain,
    query_weight,
    key_weight,
    value_weight,
    outgate_weight,
    rate_weight,
    conv_query,
    conv_key,
    conv_value,
    decay_bias,
    out_gain,
    out_weight,
    mlp_gain,
    gate_weight,
    up_weight,
    down_weight,
):
    f32, bf16 = jnp.float32, jnp.bfloat16
    head_index = lax.axis_index("head")
    n_head, n_batch = lax.axis_size("head"), lax.axis_size("batch")
    rows, width = layer_input.shape
    length = rows * n_head
    local_heads = query_weight.shape[1] // HEAD_DIM
    unit = local_heads * HEAD_DIM
    mix_cols = 6 * unit + HEAD_DIM
    ff = gate_weight.shape[1]
    ff_pad = up_to(ff, LANE)

    copies = jnp.broadcast_to(layer_input[None], (n_head,) + layer_input.shape)
    copies, query_weight, key_weight, value_weight, outgate_weight = lax.optimization_barrier(
        (copies, query_weight, key_weight, value_weight, outgate_weight)
    )
    tokens = exchange(copies, "head")
    own_mix = jnp.concatenate(
        [
            query_weight,
            key_weight,
            value_weight,
            outgate_weight,
            jnp.pad(rate_weight, ((0, 0), (0, HEAD_DIM - rate_weight.shape[1]))),
        ],
        axis=1,
    )
    proj_w = lax.all_gather(own_mix, "batch", axis=0, tiled=True)

    pad = ((0, 0), (0, ff_pad - ff))
    own_ff = jnp.concatenate(
        [jnp.pad(gate_weight, pad), jnp.pad(up_weight, pad), jnp.pad(down_weight.T, pad)], axis=1
    )
    ff_sets = [lax.all_gather(own_ff, "batch", axis=0, tiled=True)]
    def head_cols(table, per_head):
        return lax.dynamic_slice_in_dim(
            table, head_index * local_heads * per_head, local_heads * per_head, axis=table.ndim - 1
        )

    taps = jnp.concatenate(
        [
            head_cols(conv_query, HEAD_DIM),
            head_cols(conv_key, 2 * HEAD_DIM),
            head_cols(conv_value, 2 * HEAD_DIM),
        ],
        axis=1,
    )
    own_bias = head_cols(decay_bias, 1)
    bias = jnp.stack([jnp.zeros_like(own_bias), jnp.zeros_like(own_bias), own_bias], axis=1)
    bias = jnp.pad(bias.reshape(-1), (0, HEAD_DIM - 3 * local_heads))[None]
    aux, segrow = token_aux(segments)
    tokens, later_ff, later_out, later_cot, aux, segrow, taps, bias = lax.optimization_barrier(
        (tokens, own_ff, out_weight.T, cotangent, aux, segrow, taps, bias)
    )
    out_shards = trade([later_out] * n_head, "head")
    shards = [later_ff]
    for bit in bits_of(n_head)[1:]:
        shards = shards + [swap(shard, "head", bit) for shard in shards]
    pair_grad = swap(later_cot, "head", 1)

    all_in = tokens.reshape(length, width).astype(f32)
    scale_all = row_scale(all_in)
    rows_in = (all_in * scale_all * mix_gain).astype(bf16)
    rows_in, out_shards = lax.optimization_barrier((rows_in, out_shards))
    out_all = lax.all_gather(
        jnp.concatenate(out_shards, axis=1), "batch", axis=0, tiled=True
    )
    raw = dot(rows_in, proj_w)

    gain = out_gain[None]
    consts = (raw, aux, segrow, taps, bias, gain)
    mixed_low, saved, _ = mixer_forward(*consts, None, local_heads, FWD_CHUNKS, 0, 1)
    mixed_low, pair_grad, shards, ff_sets[0] = lax.optimization_barrier(
        (mixed_low, pair_grad, shards, ff_sets[0])
    )
    ff_sets += [lax.all_gather(shard, "batch", axis=0, tiled=True) for shard in shards[1:]]

    mixed_all = jnp.concatenate(
        trade([rows_of(mixed_low, head_index ^ r, rows) for r in range(n_head)], "head"), axis=1
    )
    resid_in = layer_input.astype(f32)
    resid_mid = resid_in + dot(mixed_all, out_all, NT)
    scale_mid = row_scale(resid_mid)
    normed_mid = (resid_mid * scale_mid * mlp_gain).astype(bf16)
    pair_mid = swap(normed_mid, "head", 1)

    def feed_forward(mid, cot):
        mid_part = None
        grads = []
        for ff_set in ff_sets:
            gate_up = dot(mid, ff_set[:, : 2 * ff_pad])
            gate_pre, up_pre = gate_up[:, :ff_pad], gate_up[:, ff_pad:]
            gate_sig = jax.nn.sigmoid(gate_pre)
            silu_gate = gate_pre * gate_sig
            hidden = (silu_gate * up_pre).astype(bf16)
            hidden_grad = dot(cot, ff_set[:, 2 * ff_pad : 3 * ff_pad])
            gate_grad = (
                hidden_grad * up_pre * gate_sig * (1.0 + gate_pre * (1.0 - gate_sig))
            ).astype(bf16)
            up_grad = (hidden_grad * silu_gate).astype(bf16)
            both_grad = jnp.concatenate([gate_grad, up_grad], axis=1)
            mid_here = dot(both_grad, ff_set[:, : 2 * ff_pad], NT)
            mid_part = mid_here if mid_part is None else mid_part + mid_here
            grads.append((both_grad, hidden))
        return mid_part, grads

    mid_own, grads_own = feed_forward(normed_mid, cotangent)
    pair_mid, grads_own[0] = lax.optimization_barrier((pair_mid, grads_own[0]))
    mid_pair, grads_pair = feed_forward(pair_mid, pair_grad)
    both_mid = jnp.concatenate([normed_mid, pair_mid], axis=0)
    both_cot = jnp.concatenate([cotangent, pair_grad], axis=0)

    def weight_sums(mid, cot, own, pair):
        both, hidden = [jnp.concatenate(pieces, axis=0) for pieces in zip(own, pair)]
        return jnp.concatenate([dot(mid, both, TN), dot(cot, hidden, TN)], axis=1).astype(bf16)

    half = len(ff_sets) // 2
    ff_grads = list(zip(grads_own, grads_pair))
    ff_first = [weight_sums(both_mid, both_cot, *grads) for grads in reversed(ff_grads[half:])]
    mid_swap, ff_first, mid_own = lax.optimization_barrier(
        (swap(mid_pair.astype(bf16), "head", 1), ff_first, mid_own)
    )
    mid_grad = mid_own + mid_swap.astype(f32)
    mid_back, mlp_gain_part = norm_back(mid_grad, resid_mid, scale_mid, mlp_gain)
    resid_grad = cotangent.astype(f32) + mid_back
    branch_grad = resid_grad.astype(bf16)
    mixed_grad = dot(branch_grad, out_all).astype(bf16)
    mixed_grad = trade([mixed_grad[:, r * unit : (r + 1) * unit] for r in range(n_head)], "head")
    mixed_grad[1], out_hidden = lax.optimization_barrier(
        (mixed_grad[1], [hidden for _, hidden in grads_pair])
    )
    mixed_grad = in_order(mixed_grad, head_index)
    ff_first = [
        lax.psum_scatter(part, "batch", scatter_dimension=0, tiled=True) for part in ff_first
    ]
    downs = [ff_set[:, 2 * ff_pad : 3 * ff_pad] for ff_set in ff_sets]
    out_pair = sum(dot(hidden, down, NT) for hidden, down in zip(out_hidden, downs))
    out_pair, mixed_grad = lax.optimization_barrier((out_pair.astype(bf16), mixed_grad))
    out_swap = swap(out_pair, "head", 1)

    carry = None
    for part in reversed(range(SPANS)):
        if part == 0:
            carry, branch_rows, both_mid, both_cot, ff_grads = lax.optimization_barrier(
                (carry, branch_grad, both_mid, both_cot, ff_grads[:half])
            )
            ff_last = [weight_sums(both_mid, both_cot, *grads) for grads in reversed(ff_grads)]
            ff_last[-1] = jnp.concatenate(
                [ff_last[-1], dot(branch_rows.T, mixed_all).astype(bf16)], axis=1
            )
            carry, _, ff_first = lax.optimization_barrier((carry, ff_last, ff_first))
            ff_last = [
                lax.psum_scatter(rest, "batch", scatter_dimension=0, tiled=True)
                for rest in ff_last
            ]
        carry = mixer_backward(
            mixed_grad, raw, aux, segrow, saved, taps, bias, gain, carry,
            local_heads, BWD_CHUNKS, part, SPANS,
        )
    _, _, taps_grad, bias_grad, gain_grad, raw_low = carry
    raw_low, taps_grad, bias_grad, gain_grad, out_swap, sent = lax.optimization_barrier(
        (
            raw_low,
            taps_grad,
            bias_grad,
            gain_grad,
            out_swap,
            [swap(part, "head", bits_of(n_head)[-1]) for part in ff_first],
        )
    )
    total = dot(raw_low, proj_w, NT).astype(bf16)
    total, later_low = lax.optimization_barrier((total, raw_low))
    received = exchange(total.reshape(n_head, rows, width), "head")
    held = chip_sum(rows_in, later_low, "batch")
    mix_rows, late_tokens, late_scale, held = lax.optimization_barrier(
        (total, tokens, scale_all, held)
    )
    normed_all = late_tokens.reshape(length, width).astype(f32) * late_scale
    mix_gain_part = jnp.sum(mix_rows.astype(f32) * normed_all, axis=0)
    mix_total = plane_scatter(held, "batch")
    hiddens, _ = lax.optimization_barrier(([hidden for _, hidden in grads_own], held))
    out_own = sum(dot(own, down, NT) for own, down in zip(hiddens, downs))
    layer_output = (resid_mid + out_own + out_swap.astype(f32)).astype(bf16)
    ff_kept, _ = lax.optimization_barrier((ff_last, held))
    ff_total = [got.astype(f32) + kept.astype(f32) for got, kept in zip(sent, [kept[:, : 3 * ff_pad] for kept in ff_kept])]
    for bit in reversed(bits_of(n_head)[1:-1]):
        half = len(ff_total) // 2
        ff_total = [
            kept + swap(part.astype(bf16), "head", bit).astype(f32)
            for part, kept in zip(ff_total[:half], ff_total[half:])
        ]
    ff_total = ff_total[0].T
    done = (
        layer_output,
        mix_total[:, :unit],
        mix_total[:, unit : 3 * unit],
        mix_total[:, 3 * unit : 5 * unit],
        mix_total[:, 5 * unit : 6 * unit],
        mix_total[:, 6 * unit : 6 * unit + rate_weight.shape[1]],
        ff_total[:ff].T,
        ff_total[ff_pad : ff_pad + ff].T,
        ff_total[2 * ff_pad : 2 * ff_pad + ff],
    )

    own_bias_grad = bias_grad[0, : 3 * local_heads].reshape(local_heads, 3)[:, 2]
    small = [
        taps_grad[:, :unit].reshape(-1),
        taps_grad[:, unit : 3 * unit].reshape(-1),
        taps_grad[:, 3 * unit :].reshape(-1),
        own_bias_grad,
        gain_grad[0],
        mlp_gain_part,
        mix_gain_part,
    ]
    lengths = [part.shape[0] for part in small]
    packed, mix_total, out_sum = lax.optimization_barrier(
        (pack(small), mix_total, ff_kept[-1][:, 3 * ff_pad :])
    )
    out_blocks = trade([out_sum[:, r * unit : (r + 1) * unit] for r in range(n_head)], "head")
    for bit in bits_of(n_batch):
        packed = packed + swap(packed, "batch", bit)
    small = unpack(packed, lengths)

    def place_cols(table_shape, local_part, per_head):
        local_part = local_part.reshape(table_shape[:-1] + (-1,))
        return lax.dynamic_update_slice_in_dim(
            jnp.zeros(table_shape, f32),
            local_part,
            head_index * local_heads * per_head,
            axis=len(table_shape) - 1,
        ).reshape(-1)

    tables = [
        place_cols(conv_query.shape, small[0], HEAD_DIM),
        place_cols(conv_key.shape, small[1], 2 * HEAD_DIM),
        place_cols(conv_value.shape, small[2], 2 * HEAD_DIM),
        place_cols(decay_bias.shape, small[3], 1),
    ] + small[4:]
    lengths = [part.shape[0] for part in tables]
    packed, received, done = lax.optimization_barrier((pack(tables), received, done))
    for bit in bits_of(n_head):
        packed = packed + swap(packed, "head", bit)
    tables = unpack(packed, lengths)
    in_grad = jnp.sum(received.astype(f32), axis=0)
    in_back, _ = norm_back(in_grad, resid_in, row_scale(resid_in), mix_gain)
    input_grad = resid_grad + in_back

    out_total = sum(block.astype(f32) for block in out_blocks)
    return (
        done[0],
        input_grad,
        tables[6],
        *done[1:6],
        tables[0].reshape(conv_query.shape),
        tables[1].reshape(conv_key.shape),
        tables[2].reshape(conv_value.shape),
        tables[3],
        tables[4],
        out_total.T,
        tables[5],
        *done[6:],
    )


def pack(parts):
    flat = jnp.concatenate(parts)
    return jnp.pad(flat, (0, -flat.shape[0] % (8 * LANE))).reshape(-1, LANE)


def unpack(packed, lengths):
    flat = packed.reshape(-1)
    out, at = [], 0
    for size in lengths:
        out.append(flat[at : at + size])
        at += size
    return out


def solution(mesh):
    placed = (
        P(("batch", "head"), None),
        P(("batch", "head"), None),
        P("batch"),
        P(),
        P("batch", "head"),
        P("batch", "head"),
        P("batch", "head"),
        P("batch", "head"),
        P("batch", "head"),
        P(),
        P(),
        P(),
        P(),
        P(),
        P("head", "batch"),
        P(),
        P("batch", "head"),
        P("batch", "head"),
        P("head", "batch"),
    )
    return jax.shard_map(
        body,
        mesh=mesh,
        in_specs=placed,
        out_specs=(
            P(("batch", "head"), None),
            P(("batch", "head"), None),
            P(),
            P("batch", "head"),
            P("batch", "head"),
            P("batch", "head"),
            P("batch", "head"),
            P("batch", "head"),
            P(),
            P(),
            P(),
            P(),
            P(),
            P("head", "batch"),
            P(),
            P("batch", "head"),
            P("batch", "head"),
            P("head", "batch"),
        ),
        check_vma=False,
    )
```
